128 devices in a mesh: ep: 32 (over z, y, core), tp: 4 (over x).
Axes of the slice: x: 4, y: 4, z: 4, core: 2. Of those that a mesh axis runs over, the one named last changes fastest.
Arguments:
- hidden_in: bfloat16 [4096, 5120], P('ep', 'tp'), may hold values from -12 to 12
- out_grad: bfloat16 [4096, 5120], P('ep', 'tp'), may hold values from -6 to 6
- norm_gain: float32 [5120], P('tp'), may hold values from 0.5 to 1.5
- router_weight: float32 [5120, 32], P('tp'), may hold values from -0.078125 to 0.078125
- route_ids: int32 [4096, 8], P('ep'), may hold values from 0 to 31, all different within a row; in each aligned block of 128 rows (0 to 127, 128 to 255, ...) at most 36 rows name the same one
- expert_gate: bfloat16 [32, 5120, 768], P('ep', 'tp'), may hold values from -0.078125 to 0.078125
- expert_up: bfloat16 [32, 5120, 768], P('ep', 'tp'), may hold values from -0.078125 to 0.078125
- expert_down: bfloat16 [32, 768, 5120], P('ep', None, 'tp'), may hold values from -0.21875 to 0.21875
- shared_gate: bfloat16 [5120, 768], P('tp', 'ep'), may hold values from -0.078125 to 0.078125
- shared_up: bfloat16 [5120, 768], P('tp', 'ep'), may hold values from -0.078125 to 0.078125
- shared_down: bfloat16 [768, 5120], P('ep', 'tp'), may hold values from -0.21875 to 0.21875
- dense_gate: bfloat16 [4096, 6144], P(None, 'ep'), may hold values from -6 to 6
- dense_up: bfloat16 [4096, 6144], P(None, 'ep'), may hold values from -6 to 6
- dense_down: bfloat16 [6144, 5120], P('ep', 'tp'), may hold values from -0.078125 to 0.078125
Outputs:
- grad_gate2: bfloat16 [4096, 6144], P('tp', 'ep')
- grad_up2: bfloat16 [4096, 6144], P('tp', 'ep')
- grad_dense_down: bfloat16 [6144, 5120], P('ep', 'tp')
- grad_expert_gate: bfloat16 [32, 5120, 768], P('ep', 'tp')
- grad_expert_up: bfloat16 [32, 5120, 768], P('ep', 'tp')
- grad_expert_down: bfloat16 [32, 768, 5120], P('ep', None, 'tp')
- grad_shared_gate: bfloat16 [5120, 768], P('tp', 'ep')
- grad_shared_up: bfloat16 [5120, 768], P('tp', 'ep')
- grad_shared_down: bfloat16 [768, 5120], P('ep', 'tp')
- grad_router: float32 [5120, 32], P('tp')
The draws below stay inside these ranges and needn't reach their ends.
Inputs may be any that keep to these rules, and one draw needn't show every extreme that they name: `route_ids`: each row names 8 different experts. Among the rows of one index of ep (128 consecutive tokens) no expert is named more than 36 times, a bound that some block reaches. A pair (t, k) takes slot number p of its expert's slots from that index, where p counts the earlier pairs of the same index and expert in the order of t, then k.
All inputs are finite; a program needn't handle non-finite values.
Results may differ from the reference program's by a relative error of at most 0.035.
Values may be sent and summed in bfloat16 or wider, within the bound.
No kernel may reach another device: no remote copies, remote signals or barrier semaphores. Data moves between devices by JAX's collectives and lax.ppermute only.
A program may use at most 128 MiB of HBM per device.

```python
import math
import jax
import jax.numpy as jnp
import numpy as np
from jax import lax

D = 5120
EFF = 768
SFF = 768
DFF = 6144
EXPERTS = 32
TOP = 8
TOK_DEV = 128
CAP = 36
TOKENS = 4096
N_EP = 32
N_TP = 4


def draw_hidden_in(key, part):
    key = jax.random.fold_in(key, 11)
    base_key, rough_key, row_key = jax.random.split(key, 3)
    column = jnp.arange(D, dtype=jnp.float32) / (D - 1)
    rough = jax.random.uniform(rough_key, (1, D), jnp.float32, 0.7, 1.4)
    row_scale = jnp.exp(jax.random.uniform(row_key, (TOKENS, 1), jnp.float32, jnp.log(0.6), jnp.log(1.6)))
    base = jnp.clip(jax.random.normal(base_key, (TOKENS, D), jnp.float32), -3.0, 3.0)
    column_scale = 0.3 * jnp.exp(jnp.log(6.0) * column)
    values = base * column_scale[None, :] * rough * row_scale
    return values.astype(jnp.bfloat16)


def block_scale(own_key, extent, cuts, least, largest):
    def one(axis_at, blocks):
        draws = jax.random.uniform(jax.random.fold_in(jax.random.fold_in(own_key, 6), axis_at), (blocks,), jnp.float32, least / len(cuts), largest / len(cuts))
        return jnp.repeat(jnp.exp(draws), extent[axis_at] // blocks).reshape((-1,) + (1,) * (len(extent) - axis_at - 1))

    level = one(*cuts[0])
    for cut in cuts[1:]:
        level = level * one(*cut)
    return level


def routed_block(rng, own, number, rows, number_of, top, bound, lean):
    order = jax.random.permutation(rng, number_of)
    packed, usual = load_shares(number_of, rows * top, bound, lean, True), load_shares(number_of, rows * top, bound, lean, False)
    places = jnp.arange(number_of)

    def named(sizes, rotation):
        used = int((sizes > 0).sum())
        fixed = max(1, used // 4)
        moved = fixed + (places - fixed + rotation * (used - fixed)) % max(1, number_of - fixed)
        return jnp.zeros((number_of,), jnp.int32).at[order[jnp.where(places < fixed, places, moved)]].set(jnp.asarray(sizes, jnp.int32))

    sizes = jnp.where(number % 4 == 0, named(packed, number // 4), named(usual, number - number // 4 - 1))
    mixed = jax.random.permutation(jax.random.fold_in(own, 3), number_of)
    donor, taker = mixed[0:number_of // 2 * 2:2], mixed[1:number_of // 2 * 2:2]
    margin = jnp.minimum(sizes[donor] - 1, bound - sizes[taker]) // 2
    margin = jnp.where((donor == order[0]) | (taker == order[0]) | (sizes[taker] == 0), 0, jnp.maximum(margin, 0))
    moved = jax.random.randint(jax.random.fold_in(own, 4), (number_of // 2,), 0, 1 << 20) % (margin + 1)
    sizes = sizes.at[donor].add(-moved).at[taker].add(moved)
    items = jnp.searchsorted(jnp.cumsum(sizes), jnp.arange(rows * top), side="right").astype(jnp.int32)
    listing = items.reshape(top, rows).T
    listing = listing[jax.random.permutation(jax.random.fold_in(own, 1), rows)]
    rotation = jax.random.randint(jax.random.fold_in(own, 2), (rows, 1), 0, top)
    return jnp.take_along_axis(listing, (jnp.arange(top)[None, :] + rotation) % top, axis=1)


def load_shares(number_of, total, most, skew, full):
    weights = [(1 << 20) // math.isqrt(rank ** skew) + 1 for rank in range(1, number_of + 1)]
    largest = most if full else min(most, max(-(-total // number_of), total * weights[0] // sum(weights)))
    least = 1 if total - largest >= number_of - 1 else 0
    holding, surplus = [largest] + [least] * (number_of - 1), total - largest - least * (number_of - 1)
    while surplus > 0:
        free = [i for i in range(1, number_of) if holding[i] < largest] or [i for i in range(1, number_of) if holding[i] < most]
        whole, budget = sum([weights[i] for i in free]), surplus
        for i in free:
            more = min(most - holding[i], max(1, budget * weights[i] // whole), surplus)
            holding[i] = holding[i] + more
            surplus = surplus - more
    return np.array(holding)


def normal_values(stream_key, extent, spread, most, pieces=(), held_as=jnp.bfloat16):
    array = spread * jax.random.normal(stream_key, extent, jnp.float32)
    if pieces:
        array = array * block_scale(stream_key, extent, pieces, -0.22, 0.18)
    return jnp.clip(array, -most, most).astype(held_as)


def setup_inputs(seed: int = 0) -> dict:
    key_list = jax.random.split(jax.random.key(seed), 15)
    hidden_in = draw_hidden_in(jax.random.fold_in(key_list[14], 71), 0)
    out_grad = normal_values(key_list[1], (TOKENS, D), 1.0, 6.0, ((0, 32), (1, 4)))
    norm_gain = jnp.clip(1.0 + 0.1 * jax.random.normal(key_list[2], (D,), jnp.float32), 0.5, 1.5)
    router_weight = normal_values(key_list[3], (D, EXPERTS), D ** -0.5, 0.078125, ((0, 4),), jnp.float32)
    route_ids_keys = jax.random.split(jax.random.fold_in(key_list[4], 1), TOKENS // TOK_DEV)
    route_ids_turns = jax.random.permutation(jax.random.fold_in(key_list[4], 3), TOKENS // TOK_DEV)
    route_ids = jax.vmap(lambda own, number: routed_block(jax.random.fold_in(key_list[4], 2), own, number, TOK_DEV, EXPERTS, TOP, CAP, 2))(route_ids_keys, route_ids_turns).reshape((TOKENS, TOP))
    expert_gate = normal_values(key_list[5], (EXPERTS, D, EFF), D ** -0.5, 0.078125, ((0, 32), (1, 4)))
    expert_up = normal_values(key_list[6], (EXPERTS, D, EFF), D ** -0.5, 0.078125, ((0, 32), (1, 4)))
    expert_down = normal_values(key_list[7], (EXPERTS, EFF, D), EFF ** -0.5, 0.21875, ((0, 32), (2, 4)))
    shared_gate = normal_values(key_list[8], (D, SFF), D ** -0.5, 0.078125, ((0, 4), (1, 32)))
    shared_up = normal_values(key_list[9], (D, SFF), D ** -0.5, 0.078125, ((0, 4), (1, 32)))
    shared_down = normal_values(key_list[10], (SFF, D), SFF ** -0.5, 0.21875, ((0, 32), (1, 4)))
    dense_gate = normal_values(key_list[11], (TOKENS, DFF), 1.0, 6.0, ((1, 32),))
    dense_up = normal_values(key_list[12], (TOKENS, DFF), 1.0, 6.0, ((1, 32),))
    dense_down = normal_values(key_list[13], (DFF, D), DFF ** -0.5, 0.078125, ((0, 32), (1, 4)))
    return dict(hidden_in=hidden_in, out_grad=out_grad, norm_gain=norm_gain, router_weight=router_weight, route_ids=route_ids, expert_gate=expert_gate, expert_up=expert_up, expert_down=expert_down, shared_gate=shared_gate, shared_up=shared_up, shared_down=shared_down, dense_gate=dense_gate, dense_up=dense_up, dense_down=dense_down)


EPSILON = 1e-05
ROUTE_SCALE = 2.5

def rounded(values):
    return lax.optimization_barrier(values.astype(jnp.bfloat16)).astype(jnp.float32)

def split_dot(operand, weights):
    inner_size = operand.shape[1] // N_TP
    running = jnp.zeros((operand.shape[0], weights.shape[1]), jnp.float32)
    for block_id in range(N_TP):
        lower = block_id * inner_size
        partial_value = jnp.dot(operand[:, lower:lower + inner_size], weights[lower:lower + inner_size], preferred_element_type=jnp.float32)
        running = running + rounded(partial_value)
    return running

def split_inner(first_rows, second_rows):
    inner_size = first_rows.shape[1] // N_TP
    running = jnp.zeros((first_rows.shape[0],), jnp.float32)
    for block_id in range(N_TP):
        lower = block_id * inner_size
        partial_value = lax.optimization_barrier(jnp.sum(first_rows[:, lower:lower + inner_size].astype(jnp.float32) * second_rows[:, lower:lower + inner_size].astype(jnp.float32), axis=1))
        running = running + rounded(partial_value)
    return running

def gate_grads(hidden_cot, gate_value, up_value):
    sigma = jax.nn.sigmoid(gate_value)
    gate_cot = (hidden_cot * up_value * sigma * (1.0 + gate_value * (1.0 - sigma))).astype(jnp.bfloat16)
    up_cot = (hidden_cot * gate_value * sigma).astype(jnp.bfloat16)
    return (gate_cot, up_cot)

def block_grad(first_rows, second_rows):
    first_blocks = first_rows.reshape(N_EP, TOK_DEV, first_rows.shape[1])
    second_blocks = second_rows.reshape(N_EP, TOK_DEV, second_rows.shape[1])

    def add_block(running, operands):
        partial_value = jnp.dot(operands[0].T, operands[1], preferred_element_type=jnp.float32)
        return (running + rounded(partial_value), None)
    start = jnp.zeros((first_rows.shape[1], second_rows.shape[1]), jnp.float32)
    running, unused = lax.scan(add_block, start, (first_blocks, second_blocks))
    return running.astype(jnp.bfloat16)

def reference(hidden_in, out_grad, norm_gain, router_weight, route_ids, expert_gate, expert_up, expert_down, shared_gate, shared_up, shared_down, dense_gate, dense_up, dense_down):
    highest = lax.Precision.HIGHEST
    tokens = hidden_in.shape[0]
    wide_in = hidden_in.astype(jnp.float32)
    inv_rms = lax.rsqrt(lax.optimization_barrier(jnp.mean(wide_in * wide_in, axis=1, keepdims=True)) + EPSILON)
    normed = (wide_in * inv_rms * norm_gain).astype(jnp.bfloat16)
    logits = jnp.dot(normed.astype(jnp.float32), router_weight, precision=highest)
    scores = jax.nn.sigmoid(logits)
    picks = (route_ids[:, :, None] == jnp.arange(EXPERTS, dtype=jnp.int32)[None, None, :]).astype(jnp.float32)
    chosen = lax.optimization_barrier(jnp.sum(picks * scores[:, None, :], axis=2))
    chosen_total = lax.optimization_barrier(jnp.sum(chosen, axis=1, keepdims=True))
    route_weight = ROUTE_SCALE * chosen / chosen_total
    weight_low = route_weight.astype(jnp.bfloat16)
    pair_count = tokens * TOP
    flat_ids = route_ids.reshape(N_EP, TOK_DEV * TOP)
    member = (flat_ids[:, :, None] == jnp.arange(EXPERTS, dtype=jnp.int32)[None, None, :]).astype(jnp.int32)
    before = jnp.cumsum(member, axis=1) - member
    position = lax.optimization_barrier(jnp.sum(before * member, axis=2))
    group_id = jnp.arange(N_EP, dtype=jnp.int32)[:, None]
    span = N_EP * CAP
    slot_index = (flat_ids * span + group_id * CAP + position).reshape(-1)
    source = jnp.full((EXPERTS * span,), pair_count, jnp.int32).at[slot_index].set(jnp.arange(pair_count, dtype=jnp.int32))
    normed_pad = jnp.concatenate([normed, jnp.zeros((1, D), jnp.bfloat16)], axis=0)
    grad_pad = jnp.concatenate([out_grad, jnp.zeros((1, D), jnp.bfloat16)], axis=0)
    weight_pad = jnp.concatenate([weight_low.reshape(-1), jnp.zeros((1,), jnp.bfloat16)], axis=0)

    def one_expert(carried, expert):
        back_sum, inner_all = carried
        pair_index = lax.dynamic_slice_in_dim(source, (expert * span).astype(jnp.int32), span)
        pair_row = pair_index // TOP
        rows_in = normed_pad[pair_row]
        rows_grad = grad_pad[pair_row]
        rows_weight = weight_pad[pair_index].astype(jnp.float32)
        w_gate = expert_gate[expert]
        w_up = expert_up[expert]
        w_down = expert_down[expert]
        gate_value = split_dot(rows_in, w_gate)
        up_value = split_dot(rows_in, w_up)
        hidden = (jax.nn.silu(gate_value) * up_value).astype(jnp.bfloat16)
        out_rows = jnp.dot(hidden, w_down, preferred_element_type=jnp.float32).astype(jnp.bfloat16)
        inner_part = split_inner(rows_grad, out_rows)
        out_cot = (rows_weight[:, None] * rows_grad.astype(jnp.float32)).astype(jnp.bfloat16)
        hidden_cot = split_dot(out_cot, w_down.T)
        gate_cot, up_cot = gate_grads(hidden_cot, gate_value, up_value)
        grad_down = jnp.dot(hidden.T, out_cot, preferred_element_type=jnp.float32).astype(jnp.bfloat16)
        grad_gate = jnp.dot(rows_in.T, gate_cot, preferred_element_type=jnp.float32).astype(jnp.bfloat16)
        grad_up = jnp.dot(rows_in.T, up_cot, preferred_element_type=jnp.float32).astype(jnp.bfloat16)
        back_rows = (jnp.dot(gate_cot, w_gate.T, preferred_element_type=jnp.float32) + jnp.dot(up_cot, w_up.T, preferred_element_type=jnp.float32)).astype(jnp.bfloat16)
        back_sum = back_sum.at[pair_row].add(back_rows.astype(jnp.float32))
        inner_all = inner_all.at[pair_index].add(inner_part)
        return ((back_sum, inner_all), (grad_gate, grad_up, grad_down))
    start = (jnp.zeros((tokens + 1, D), jnp.float32), jnp.zeros((pair_count + 1,), jnp.float32))
    finals, grads = lax.scan(one_expert, start, jnp.arange(EXPERTS, dtype=jnp.int32))
    back_sum, inner_all = finals
    grad_expert_gate, grad_expert_up, grad_expert_down = grads
    routed_cot = back_sum[:tokens]
    weight_cot = inner_all[:pair_count].reshape(tokens, TOP)
    chosen_cot = ROUTE_SCALE * (weight_cot / chosen_total - lax.optimization_barrier(jnp.sum(weight_cot * chosen, axis=1, keepdims=True)) / (chosen_total * chosen_total))
    score_cot = lax.optimization_barrier(jnp.sum(picks * chosen_cot[:, :, None], axis=1))
    logit_cot = score_cot * scores * (1.0 - scores)
    grad_router = jnp.dot(normed.astype(jnp.float32).T, logit_cot, precision=highest)
    router_cot = jnp.dot(logit_cot, router_weight.T, precision=highest)
    gate_s = split_dot(normed, shared_gate)
    up_s = split_dot(normed, shared_up)
    hid_s = (jax.nn.silu(gate_s) * up_s).astype(jnp.bfloat16)
    hid_cot_s = split_dot(out_grad, shared_down.T)
    gate_cot_s, up_cot_s = gate_grads(hid_cot_s, gate_s, up_s)
    grad_shared_gate = block_grad(normed, gate_cot_s)
    grad_shared_up = block_grad(normed, up_cot_s)
    grad_shared_down = block_grad(hid_s, out_grad)
    shared_cot = jnp.dot(gate_cot_s, shared_gate.T, preferred_element_type=jnp.float32) + jnp.dot(up_cot_s, shared_up.T, preferred_element_type=jnp.float32)
    normed_cot = routed_cot + shared_cot + router_cot
    scaled = normed_cot * norm_gain
    inner_mean = lax.optimization_barrier(jnp.mean(scaled * wide_in, axis=1, keepdims=True))
    input_cot = inv_rms * scaled - wide_in * (inv_rms * inv_rms * inv_rms) * inner_mean
    dense_cot = (out_grad.astype(jnp.float32) + input_cot).astype(jnp.bfloat16)
    gate_two = dense_gate.astype(jnp.float32)
    up_two = dense_up.astype(jnp.float32)
    hidden2 = (jax.nn.silu(gate_two) * up_two).astype(jnp.bfloat16)
    grad_dense_down = jnp.dot(hidden2.T, dense_cot, preferred_element_type=jnp.float32).astype(jnp.bfloat16)
    hidden2_cot = split_dot(dense_cot, dense_down.T)
    grad_gate2, grad_up2 = gate_grads(hidden2_cot, gate_two, up_two)
    return (grad_gate2, grad_up2, grad_dense_down, grad_expert_gate, grad_expert_up, grad_expert_down, grad_shared_gate, grad_shared_up, grad_shared_down, grad_router)
```

```python
import functools

import jax
import jax.numpy as jnp
from jax import lax
from jax.experimental import pallas as pl
from jax.experimental.pallas import tpu as pltpu
from jax.sharding import PartitionSpec as P

EXPERTS = 32
TOP = 8
CAP = 36
SIDE = 4
GROUPS = 8
ROWS = SIDE * CAP

EPSILON = 1e-05
ROUTE_SCALE = 2.5
F32 = jnp.float32
BF16 = jnp.bfloat16
HIGHEST = lax.Precision.HIGHEST
VMEM_BYTES = 50 * 1024 * 1024


def ep_at(z, y, core):
    return ((z % SIDE) * SIDE + y % SIDE) * 2 + core


def ep_pairs(target):
    return [
        (ep_at(z, y, core), target(z, y, core))
        for z in range(SIDE)
        for y in range(SIDE)
        for core in range(2)
    ]


def first_hop(k):
    return ep_pairs(lambda z, y, core: ep_at(z, y + k, 1) if core else ep_at(z + k, y, 0))


def second_hop(k):
    return ep_pairs(lambda z, y, core: ep_at(z + k, y, 1) if core else ep_at(z, y + k, 0))


def swap_second_hop(k):
    return ep_pairs(lambda z, y, core: ep_at(z, y + k, 0) if core else ep_at(z + k, y, 1))


def core_swap():
    return ep_pairs(lambda z, y, core: ep_at(z, y, 1 - core))


def tp_hop(k):
    return [(i, (i + k) % SIDE) for i in range(SIDE)]


def join_kernel(*refs):
    blocks, out = refs[:SIDE], refs[SIDE]
    rows = blocks[0].shape[0]
    for i in range(SIDE):
        out[i * rows : (i + 1) * rows] = blocks[i][...]


def join(blocks):
    rows, width = blocks[0].shape
    return local_call(
        join_kernel,
        jax.ShapeDtypeStruct((SIDE * rows, width), blocks[0].dtype),
        vmem(SIDE),
        0,
        4 * SIDE * rows * width,
    )(*blocks)


def path_gather(block, after=None):
    if after is not None:
        block, unused = lax.optimization_barrier((block, after[0]))
    first = [block] + [lax.ppermute(block, "ep", first_hop(k)) for k in range(1, SIDE)]
    joined = join(first)
    if after is not None:
        joined, *unused = lax.optimization_barrier((joined, *after[1:SIDE]))
    own = [joined] + [lax.ppermute(joined, "ep", second_hop(k)) for k in range(1, SIDE)]
    other = [lax.ppermute(chunk, "ep", core_swap()) for chunk in own]
    return own + other


def ep_sum(value):
    for dz, dy, dcore in ((0, 0, 1), (0, 1, 0), (1, 0, 0), (0, 2, 0), (2, 0, 0)):
        pairs = ep_pairs(lambda z, y, core: ep_at(z ^ dz, y ^ dy, core ^ dcore))
        value = value + lax.ppermute(value, "ep", pairs)
    return value


def tp_sum(value):
    return value + sum(lax.ppermute(value, "tp", tp_hop(k)) for k in range(1, SIDE))


def tp_exchange(parts):
    return lax.all_to_all(parts, "tp", split_axis=0, concat_axis=0, tiled=True)


def tp_scatter(parts):
    return jnp.sum(tp_exchange(parts).astype(F32), axis=0)


def vmem(count):
    return [pl.BlockSpec(memory_space=pltpu.VMEM)] * count


def smem():
    return pl.BlockSpec(memory_space=pltpu.SMEM)


def local_call(body, out_shape, in_specs, flops, moved, scratch=()):
    many = isinstance(out_shape, (list, tuple))
    return pl.pallas_call(
        body,
        out_shape=out_shape,
        in_specs=in_specs,
        out_specs=vmem(len(out_shape)) if many else vmem(1)[0],
        scratch_shapes=list(scratch),
        cost_estimate=pl.CostEstimate(flops=flops, bytes_accessed=moved, transcendentals=0),
        compiler_params=pltpu.CompilerParams(vmem_limit_bytes=VMEM_BYTES),
    )


def nt_dot(left, right):
    return lax.dot_general(left, right, (((1,), (1,)), ((), ())), preferred_element_type=F32)


def dispatch_kernel(scale, slot, *refs):
    if scale:
        inv, gain, *refs = refs
    chunks, out = refs[:GROUPS], refs[GROUPS]
    for g in range(GROUPS):
        tokens = chunks[g].shape[0]
        hit = lax.broadcasted_iota(jnp.int32, (ROWS, tokens), 0) == slot[g]
        pick = jnp.where(hit, 1.0, 0.0).astype(BF16)
        rows = jnp.dot(pick, chunks[g][...], preferred_element_type=F32)
        if scale:
            row_inv = jnp.sum(jnp.where(hit, inv[g], 0.0), axis=1, keepdims=True)
            rows = rows * row_inv * gain[...]
        out[g] = rows.astype(BF16)


def dispatch(slot, chunks, inv=None, gain=None):
    scale = inv is not None
    tokens, width = chunks[0].shape
    extra = (inv, gain) if scale else ()
    return local_call(
        functools.partial(dispatch_kernel, scale),
        jax.ShapeDtypeStruct((GROUPS, ROWS, width), BF16),
        vmem(1 + len(extra) + GROUPS),
        2 * GROUPS * ROWS * tokens * width,
        2 * GROUPS * (tokens + ROWS) * width,
    )(slot, *extra, *chunks)


def back_kernel(cots, weights, *out):
    tile = 256

    def step(n, unused):
        columns = pl.ds(pl.multiple_of(n * tile, tile), tile)
        for k in range(SIDE):
            rows = jnp.dot(cots[k], weights[:, columns], preferred_element_type=F32).astype(BF16)
            out[2 * k][:, columns] = rows[:ROWS]
            out[2 * k + 1][:, columns] = rows[ROWS:]
        return unused

    lax.fori_loop(0, weights.shape[1] // tile, step, 0)


def back_rows_of(cots, weights):
    hidden, width = weights.shape
    return local_call(
        back_kernel,
        [jax.ShapeDtypeStruct((ROWS, width), BF16)] * GROUPS,
        vmem(2),
        2 * GROUPS * ROWS * hidden * width,
        2 * (GROUPS * ROWS * hidden + hidden * width + GROUPS * ROWS * width),
    )(cots, weights)


def act_kernel(weight, gate_ups, cots, cot_out, hidden_out, row_cot, row_inner):
    tile = 32
    width = cots.shape[2]

    def step(n, unused):
        rows = pl.ds(pl.multiple_of(n * tile, tile), tile)

        def total(parts, columns):
            return sum(parts[k, rows, columns].astype(F32) for k in range(SIDE))

        gate = total(gate_ups, slice(0, width))
        up = total(gate_ups, slice(width, 2 * width))
        cot = total(cots, slice(0, width))
        weight_here = weight[rows, :]
        sigma = 1.0 / (1.0 + jnp.exp(-gate))
        silu = gate * sigma
        hidden = silu * up
        row_cot[rows, :] = jnp.sum(cot * hidden, axis=1, keepdims=True)
        cot = cot * weight_here
        gate_cot = cot * up * (sigma + silu * (1.0 - sigma))
        up_cot = cot * silu
        row_inner[rows, :] = jnp.sum(gate_cot * gate + up_cot * up, axis=1, keepdims=True)
        for k in range(SIDE):
            cot_out[k, rows, :width] = gate_cot.astype(BF16)
            cot_out[k, rows, width:] = up_cot.astype(BF16)
            hidden_out[k, rows, :] = (hidden * weight_here).astype(BF16)
        return unused

    lax.fori_loop(0, weight.shape[0] // tile, step, 0)


def act(weight, gate_ups, cots):
    parts, rows, hidden = cots.shape
    return local_call(
        act_kernel,
        [
            jax.ShapeDtypeStruct((parts, rows, 2 * hidden), BF16),
            jax.ShapeDtypeStruct((parts, rows, hidden), BF16),
        ]
        + [jax.ShapeDtypeStruct((rows, 1), F32)] * 2,
        vmem(3),
        40 * rows * hidden,
        48 * rows * hidden,
    )(weight, gate_ups, cots)


def combine_kernel(slots, *refs):
    rows, out, pick = refs[:GROUPS], refs[GROUPS], refs[GROUPS + 1]
    tokens = slots.shape[0]
    tile = 256
    for m in range(GROUPS):
        hit = lax.broadcasted_iota(jnp.int32, (tokens, ROWS), 1) == slots[:, m : m + 1]
        pick[m] = jnp.where(hit, 1.0, 0.0).astype(BF16)

    def step(n, unused):
        columns = pl.ds(pl.multiple_of(n * tile, tile), tile)
        total = jnp.dot(pick[0], rows[0][:, columns], preferred_element_type=F32)
        for m in range(1, GROUPS):
            total = total + jnp.dot(pick[m], rows[m][:, columns], preferred_element_type=F32)
        out[:, columns] = total.astype(BF16)
        return unused

    lax.fori_loop(0, out.shape[1] // tile, step, 0)


def combine(slots, rows):
    tokens, width = slots.shape[0], rows[0].shape[1]
    return local_call(
        combine_kernel,
        jax.ShapeDtypeStruct((tokens, width), BF16),
        vmem(1 + GROUPS),
        2 * GROUPS * ROWS * tokens * width,
        2 * (GROUPS * ROWS + tokens) * width,
        [pltpu.VMEM((GROUPS, tokens, ROWS), BF16)],
    )(slots, *rows)


def shared_kernel(place, w_in, w_out, *refs):
    ins, grads, out = refs[:GROUPS], refs[GROUPS : 2 * GROUPS], refs[2 * GROUPS]
    top, block = w_in.shape[0], out.shape[2]
    for g in range(GROUPS):
        first = nt_dot(w_in[...], ins[g][...]).astype(BF16)
        second = nt_dot(w_out[...], grads[g][...]).astype(BF16)
        for i in range(SIDE):
            at = place[g * SIDE + i]
            out[at, :top] = first[:, i * block : (i + 1) * block]
            out[at, top:] = second[:, i * block : (i + 1) * block]


def shared_partials(place, w_in, w_out, ins, grads):
    tokens, width = ins[0].shape
    hidden = w_in.shape[0] + w_out.shape[0]
    return local_call(
        shared_kernel,
        jax.ShapeDtypeStruct((GROUPS * SIDE, hidden, tokens // SIDE), BF16),
        [smem()] + vmem(2 + 2 * GROUPS),
        2 * GROUPS * tokens * width * hidden,
        4 * GROUPS * tokens * width,
    )(place, w_in, w_out, *ins, *grads)


def shared_grad_kernel(place, cots, gain, *refs):
    ins, grads = refs[:GROUPS], refs[GROUPS : 2 * GROUPS]
    out_in, out_down, sum_in, sum_down = refs[2 * GROUPS :]
    top = out_in.shape[0]
    for g in range(GROUPS):
        cot = jnp.concatenate([cots[place[g * SIDE + i]] for i in range(SIDE)], axis=1)
        first = jnp.dot(cot[:top], ins[g][...], preferred_element_type=F32)
        second = jnp.dot(cot[top:], grads[g][...], preferred_element_type=F32)
        sum_in[...] = first if g == 0 else sum_in[...] + first
        sum_down[...] = second if g == 0 else sum_down[...] + second
    out_in[...] = (sum_in[...] * gain[...]).astype(BF16)
    out_down[...] = sum_down[...].astype(BF16)


def shared_grads(place, cots, gain, ins, grads, top):
    tokens, width = ins[0].shape
    rest = cots.shape[1] - top
    return local_call(
        shared_grad_kernel,
        [jax.ShapeDtypeStruct((top, width), BF16), jax.ShapeDtypeStruct((rest, width), BF16)],
        [smem()] + vmem(2 + 2 * GROUPS),
        2 * GROUPS * tokens * width * (top + rest),
        4 * GROUPS * tokens * width,
        [pltpu.VMEM((top, width), F32), pltpu.VMEM((rest, width), F32)],
    )(place, cots, gain, *ins, *grads)


def dense_hidden_kernel(place, w_down, *refs):
    chunks, out = refs[:GROUPS], refs[GROUPS]
    block = chunks[0].shape[0] // SIDE
    for g in range(GROUPS):
        columns = nt_dot(w_down[...], chunks[g][...]).astype(BF16)
        for i in range(SIDE):
            at = place[g * SIDE + i]
            lane = pl.multiple_of(lax.rem(at, 8) * block, block)
            out[lax.div(at, 8), :, pl.ds(lane, block)] = columns[:, i * block : (i + 1) * block]


def dense_hidden(place, w_down, chunks):
    tokens, width = chunks[0].shape
    hidden = w_down.shape[0]
    return local_call(
        dense_hidden_kernel,
        jax.ShapeDtypeStruct((SIDE, hidden, 2 * tokens), BF16),
        [smem()] + vmem(1 + GROUPS),
        2 * GROUPS * tokens * width * hidden,
        2 * GROUPS * tokens * width,
    )(place, w_down, *chunks)


def dense_grad_kernel(place, hidden, *refs):
    chunks, out, total = refs[:GROUPS], refs[GROUPS], refs[GROUPS + 1]
    block = chunks[0].shape[0] // SIDE
    for g in range(GROUPS):
        left = jnp.concatenate(
            [
                hidden[:, pl.ds(pl.multiple_of(place[g * SIDE + i] * block, block), block)]
                for i in range(SIDE)
            ],
            axis=1,
        )
        term = jnp.dot(left, chunks[g][...], preferred_element_type=F32)
        total[...] = term if g == 0 else total[...] + term
    out[...] = total[...].astype(BF16)


def dense_grad(place, hidden, chunks):
    tokens, width = chunks[0].shape
    units = hidden.shape[0]
    return local_call(
        dense_grad_kernel,
        jax.ShapeDtypeStruct((units, width), BF16),
        [smem()] + vmem(1 + GROUPS),
        2 * GROUPS * tokens * width * units,
        2 * GROUPS * tokens * width,
        [pltpu.VMEM((units, width), F32)],
    )(place, hidden, *chunks)


def gate_grads(hidden_cot, gate_value, up_value):
    sigma = jax.nn.sigmoid(gate_value)
    gate_cot = hidden_cot * up_value * sigma * (1.0 + gate_value * (1.0 - sigma))
    up_cot = hidden_cot * gate_value * sigma
    return (gate_cot, up_cot)


def local(
    hidden_in,
    out_grad,
    norm_gain,
    router_weight,
    route_ids,
    expert_gate,
    expert_up,
    expert_down,
    shared_gate,
    shared_up,
    shared_down,
    dense_gate,
    dense_up,
    dense_down,
):
    tok_rows, quarter = hidden_in.shape
    feature_count = quarter * lax.axis_size("tp")
    ep, tp = lax.axis_index("ep"), lax.axis_index("tp")
    z, y, core = ep // 8, (ep // 2) % SIDE, ep % 2
    w_gate, w_up, w_down = expert_gate[0], expert_up[0], expert_down[0]
    gain = norm_gain[None, :]

    in_chunks = path_gather(hidden_in)
    grad_chunks = path_gather(out_grad, in_chunks)

    g_at = jnp.arange(GROUPS, dtype=jnp.int32)[:, None]
    i_at = jnp.arange(SIDE, dtype=jnp.int32)[None, :]
    j_at = g_at % SIDE
    block_core = (core + g_at // SIDE) % 2
    block_z = jnp.where(block_core == 0, z - i_at, z - j_at) % SIDE
    block_y = jnp.where(block_core == 0, y - j_at, y - i_at) % SIDE
    block_of = ((block_z * SIDE + block_y) * 2 + block_core).reshape(-1)
    to_path = (block_of[:, None] == jnp.arange(EXPERTS, dtype=jnp.int32)[None, :]).astype(F32)

    wide_in = hidden_in.astype(F32)
    square_part = jnp.sum(wide_in * wide_in, axis=1, keepdims=True)
    logit_part = jnp.dot(wide_in * gain, router_weight, precision=HIGHEST)
    stats = tp_sum(jnp.concatenate([logit_part, square_part], axis=1))
    plain_logits = stats[:, :EXPERTS]
    mean_square = stats[:, EXPERTS:] / feature_count + EPSILON
    inv_rms = lax.rsqrt(mean_square)
    rms = mean_square * inv_rms
    normed = (wide_in * inv_rms * gain).astype(BF16)
    scores = jax.nn.sigmoid(plain_logits * inv_rms)
    picks = jnp.any(
        route_ids[:, :, None] == jnp.arange(EXPERTS, dtype=jnp.int32)[None, None, :], axis=1
    ).astype(F32)
    chosen = picks * scores
    chosen_total = jnp.sum(chosen, axis=1, keepdims=True)
    route_weight = ROUTE_SCALE * chosen / chosen_total

    token_line = jnp.arange(tok_rows, dtype=jnp.int32)
    earlier = (token_line[:, None] < token_line[None, :]).astype(F32)
    own_position = jnp.dot(picks.T, earlier, precision=HIGHEST)
    own_position = jnp.where(picks.T > 0.0, own_position, -1.0)
    told = jnp.concatenate(
        [
            own_position[:, None, :],
            route_weight.T[:, None, :],
            jnp.broadcast_to(inv_rms.reshape(1, 1, tok_rows), (EXPERTS, 1, tok_rows)),
        ],
        axis=1,
    )
    told = lax.all_to_all(told, "ep", split_axis=0, concat_axis=0, tiled=True)
    told_path = jnp.dot(to_path, told.reshape(EXPERTS, 3 * tok_rows), precision=HIGHEST)
    told_path = told_path.reshape(GROUPS, SIDE, 3, tok_rows)
    position = told_path[:, :, 0].astype(jnp.int32)
    offset = (CAP * jnp.arange(SIDE, dtype=jnp.int32))[None, :, None]
    slot = jnp.where(position >= 0, position + offset, -1).reshape(GROUPS, 1, SIDE * tok_rows)
    weight_path = told_path[:, :, 1].reshape(GROUPS, 1, SIDE * tok_rows)
    inv_path = told_path[:, :, 2].reshape(GROUPS, 1, SIDE * tok_rows)

    s_line = jnp.arange(2, dtype=jnp.int32)[None, :]
    j_line = jnp.arange(SIDE, dtype=jnp.int32)
    j_col = j_line[:, None]
    return_expert = jnp.where(
        core == 0,
        (z * SIDE + (y + j_col) % SIDE) * 2 + s_line,
        (((z + j_col) % SIDE) * SIDE + y) * 2 + 1 - s_line,
    ).reshape(-1)
    pick_expert = (
        return_expert[:, None] == jnp.arange(EXPERTS, dtype=jnp.int32)[None, :]
    ).astype(F32)
    line_position = jnp.stack(
        [own_position]
        + [lax.ppermute(own_position, "ep", first_hop(k)) for k in range(1, SIDE)]
    )
    position_here = jnp.einsum(
        "ket,me->ktm", line_position, pick_expert, precision=HIGHEST
    ).astype(jnp.int32)
    return_slot = jnp.where(
        position_here >= 0, position_here + (CAP * j_line)[:, None, None], -1
    ).reshape(SIDE * tok_rows, GROUPS)

    w_both = jnp.concatenate([w_gate, w_up], axis=1)
    w_both_t = jnp.concatenate([w_gate.T, w_up.T], axis=0)
    rows_in = dispatch(slot, in_chunks, inv_path, gain).reshape(-1, quarter)
    both_part = jnp.dot(rows_in, w_both, preferred_element_type=F32).astype(BF16)
    rows_grad = dispatch(slot, grad_chunks).reshape(-1, quarter)
    hidden_part = jnp.dot(rows_grad, w_down.T, preferred_element_type=F32).astype(BF16)
    quarter_rows = 2 * ROWS
    both_terms = tp_exchange(both_part.reshape(SIDE, quarter_rows, -1))
    cot_terms = tp_exchange(hidden_part.reshape(SIDE, quarter_rows, -1))
    own_slot = lax.dynamic_slice_in_dim(slot, 2 * tp, 2, 0)
    own_weight = lax.dynamic_slice_in_dim(weight_path, 2 * tp, 2, 0)
    own_hit = jnp.arange(ROWS, dtype=jnp.int32)[None, :, None] == own_slot
    row_weight = jnp.sum(jnp.where(own_hit, own_weight, 0.0), axis=2).reshape(quarter_rows, 1)
    both_cot, hidden, row_cot, row_inner = act(row_weight, both_terms, cot_terms)
    both_cots = tp_exchange(both_cot)
    hidden, unused = lax.optimization_barrier((hidden, both_cots))
    hidden_all = tp_exchange(hidden).reshape(GROUPS * ROWS, -1)
    back = back_rows_of(both_cots, w_both_t)

    returned = []
    for j in range(SIDE):
        own, other = back[j], back[SIDE + j]
        returned.append(own if j == 0 else lax.ppermute(own, "ep", second_hop(-j)))
        returned.append(lax.ppermute(other, "ep", swap_second_hop(-j)))
    summed = combine(return_slot, returned).reshape(SIDE, tok_rows, quarter)
    routed_cot = summed[0].astype(F32)
    for k in range(1, SIDE):
        routed_cot = routed_cot + lax.ppermute(summed[k], "ep", first_hop(-k)).astype(F32)

    units = shared_down.shape[0]
    shared_in = (jnp.concatenate([shared_gate.T, shared_up.T], axis=0).astype(F32) * gain).astype(
        BF16
    )
    shared_out = jnp.concatenate([shared_down, jnp.zeros((8, quarter), BF16)], axis=0)
    late_in, late_grad, unused = lax.optimization_barrier((in_chunks, grad_chunks, hidden_part))
    parts = shared_partials(block_of, shared_in, shared_out, late_in, late_grad)
    inner = parts.shape[1]
    shared_sum = tp_scatter(parts.reshape(SIDE, 8, inner, tok_rows))
    own_inv = lax.dynamic_slice_in_dim(told[:, 2:], 8 * tp, 8, 0)
    gate_s = shared_sum[:, :units] * own_inv
    up_s = shared_sum[:, units : 2 * units] * own_inv
    hid_cot_s = shared_sum[:, 2 * units : 3 * units]
    gate_cot_s, up_cot_s = gate_grads(hid_cot_s, gate_s, up_s)
    cots = jnp.concatenate(
        [
            gate_cot_s * own_inv,
            up_cot_s * own_inv,
            gate_s * jax.nn.sigmoid(gate_s) * up_s,
            jnp.zeros((8, 8, tok_rows), F32),
        ],
        axis=1,
    ).astype(BF16)
    cots_all = tp_exchange(jnp.broadcast_to(cots[None], (SIDE,) + cots.shape))
    grads_in, grads_down = shared_grads(
        block_of, cots_all.reshape(EXPERTS, inner, tok_rows), gain, in_chunks, grad_chunks, 2 * units
    )
    to_owner = cots_all[:, :, : 2 * units].reshape(EXPERTS, 2 * units, tok_rows)
    to_owner = lax.all_to_all(to_owner, "ep", split_axis=0, concat_axis=0, tiled=True)
    shared_whole = lax.all_gather(shared_in, "ep", axis=0, tiled=True)
    shared_scaled = lax.dot_general(
        to_owner.reshape(-1, tok_rows),
        shared_whole,
        (((0,), (0,)), ((), ())),
        preferred_element_type=F32,
    ) * rms

    def to_tokens(row_value):
        token_value = jnp.sum(
            jnp.where(own_hit, row_value.reshape(2, ROWS, 1), 0.0), axis=1
        ).reshape(GROUPS, tok_rows)
        own_blocks = lax.dynamic_slice_in_dim(to_path, GROUPS * tp, GROUPS, 0)
        return jnp.dot(own_blocks.T, token_value, precision=HIGHEST)

    shared_inner = lax.dynamic_update_slice_in_dim(
        jnp.zeros((EXPERTS, tok_rows), F32),
        jnp.sum(gate_cot_s * gate_s + up_cot_s * up_s, axis=1),
        8 * tp,
        0,
    )
    sums = jnp.stack([to_tokens(row_cot), to_tokens(row_inner) + shared_inner], axis=1)
    sums = tp_sum(lax.all_to_all(sums, "ep", split_axis=0, concat_axis=0, tiled=True))
    weight_cot = sums[:, 0].T
    chosen_cot = picks * (
        ROUTE_SCALE
        * (
            weight_cot / chosen_total
            - jnp.sum(weight_cot * chosen, axis=1, keepdims=True) / (chosen_total * chosen_total)
        )
    )
    logit_cot = chosen_cot * scores * (1.0 - scores)
    grad_router = ep_sum(jnp.dot(logit_cot.T, normed.astype(F32), precision=HIGHEST)).T
    router_cot = jnp.dot(logit_cot, router_weight.T, precision=HIGHEST)
    inner_sum = jnp.sum(sums[:, 1], axis=0).reshape(tok_rows, 1) * rms + jnp.sum(
        logit_cot * plain_logits, axis=1, keepdims=True
    )

    scaled = (routed_cot + router_cot) * gain + shared_scaled
    input_cot = inv_rms * scaled - wide_in * (inv_rms * inv_rms * inv_rms) * (
        inner_sum / feature_count
    )
    dense_cot = (out_grad.astype(F32) + input_cot).astype(BF16)

    cot_chunks = path_gather(dense_cot)
    gate_t, up_t = dense_gate.T, dense_up.T
    hidden2 = (jax.nn.silu(gate_t.astype(F32)) * up_t.astype(F32)).astype(BF16)
    hidden2_part = dense_hidden(block_of, dense_down, cot_chunks)
    hidden2_cot = tp_scatter(hidden2_part)
    share = 8 * tok_rows
    gate_mine = lax.dynamic_slice_in_dim(gate_t, tp * share, share, 1).astype(F32)
    up_mine = lax.dynamic_slice_in_dim(up_t, tp * share, share, 1).astype(F32)
    grad_gate2, grad_up2 = gate_grads(hidden2_cot, gate_mine, up_mine)
    grad_dense_down = dense_grad(block_of, hidden2, cot_chunks)

    rows_late, cots_late, unused = lax.optimization_barrier((rows_in, both_cots, back[0]))
    cots_late = cots_late.reshape(GROUPS * ROWS, -1)
    units_r = w_gate.shape[1]

    def rows_dot(left, right):
        return lax.dot_general(
            left, right, (((0,), (0,)), ((), ())), preferred_element_type=F32
        ).astype(BF16)[None]

    return (
        grad_gate2.astype(BF16).T,
        grad_up2.astype(BF16).T,
        grad_dense_down,
        rows_dot(rows_late, cots_late[:, :units_r]),
        rows_dot(rows_late, cots_late[:, units_r:]),
        rows_dot(hidden_all, rows_grad),
        grads_in[:units].T,
        grads_in[units:].T,
        grads_down[:units],
        grad_router,
    )


def solution(mesh):
    in_specs = (
        P("ep", "tp"),
        P("ep", "tp"),
        P("tp"),
        P("tp", None),
        P("ep", None),
        P("ep", "tp", None),
        P("ep", "tp", None),
        P("ep", None, "tp"),
        P("tp", "ep"),
        P("tp", "ep"),
        P("ep", "tp"),
        P(None, "ep"),
        P(None, "ep"),
        P("ep", "tp"),
    )
    out_specs = (
        P("tp", "ep"),
        P("tp", "ep"),
        P("ep", "tp"),
        P("ep", "tp", None),
        P("ep", "tp", None),
        P("ep", None, "tp"),
        P("tp", "ep"),
        P("tp", "ep"),
        P("ep", "tp"),
        P("tp", None),
    )
    return jax.shard_map(local, mesh=mesh, in_specs=in_specs, out_specs=out_specs, check_vma=False)
```

```python
import functools

import jax
import jax.numpy as jnp
from jax import lax
from jax.experimental import pallas as pl
from jax.experimental.pallas import tpu as pltpu
from jax.sharding import PartitionSpec as P

EXPERTS = 32
TOP = 8
CAP = 36
SIDE = 4
GROUPS = 8
ROWS = SIDE * CAP

EPSILON = 1e-05
ROUTE_SCALE = 2.5
F32 = jnp.float32
BF16 = jnp.bfloat16
HIGHEST = lax.Precision.HIGHEST
VMEM_BYTES = 50 * 1024 * 1024


def ep_at(z, y, core):
    return ((z % SIDE) * SIDE + y % SIDE) * 2 + core


def ep_pairs(target):
    return [
        (ep_at(z, y, core), target(z, y, core))
        for z in range(SIDE)
        for y in range(SIDE)
        for core in range(2)
    ]


def first_hop(k):
    return ep_pairs(lambda z, y, core: ep_at(z, y + k, 1) if core else ep_at(z + k, y, 0))


def first_lines():
    core_0 = [[ep_at(z, y, 0) for z in range(SIDE)] for y in range(SIDE)]
    return core_0 + [[ep_at(z, y, 1) for y in range(SIDE)] for z in range(SIDE)]


def second_hop(k):
    return ep_pairs(lambda z, y, core: ep_at(z + k, y, 1) if core else ep_at(z, y + k, 0))


def swap_second_hop(k):
    return ep_pairs(lambda z, y, core: ep_at(z, y + k, 0) if core else ep_at(z + k, y, 1))


def core_swap():
    return ep_pairs(lambda z, y, core: ep_at(z, y, 1 - core))


def tp_hop(k):
    return [(i, (i + k) % SIDE) for i in range(SIDE)]


def join_kernel(*refs):
    blocks, outs = refs[:SIDE], refs[SIDE:]
    rows = blocks[0].shape[0] // len(outs)
    for i in range(SIDE):
        for n, out in enumerate(outs):
            out[i * rows : (i + 1) * rows] = blocks[i][n * rows : (n + 1) * rows]


def join(blocks, count):
    rows, width = blocks[0].shape
    return local_call(
        join_kernel,
        [jax.ShapeDtypeStruct((SIDE * rows // count, width), blocks[0].dtype)] * count,
        vmem(SIDE),
        0,
        4 * SIDE * rows * width,
    )(*blocks)


def path_gather(blocks):
    stack = jnp.concatenate(blocks, axis=0) if len(blocks) > 1 else blocks[0]
    first = [stack] + [lax.ppermute(stack, "ep", first_hop(k)) for k in range(1, SIDE)]
    gathered = []
    for joined in join(first, len(blocks)):
        if gathered:
            joined, *unused = lax.optimization_barrier((joined, *gathered[-1][1:SIDE]))
        own = [joined] + [lax.ppermute(joined, "ep", second_hop(k)) for k in range(1, SIDE)]
        other = [lax.ppermute(chunk, "ep", core_swap()) for chunk in own]
        gathered.append(own + other)
    return gathered


def ep_sum(value, stages):
    pairings = ((0, 0, 1), (0, 1, 0), (1, 0, 0), (0, 2, 0), (2, 0, 0))
    for (dz, dy, dcore), stage in zip(pairings, stages, strict=True):
        pairs = ep_pairs(lambda z, y, core: ep_at(z ^ dz, y ^ dy, core ^ dcore))
        met = lax.ppermute(value, "ep", pairs)
        met, unused = lax.optimization_barrier((met, stage))
        value = value + met
    return value


def tp_gather(piece):
    return [piece] + [lax.ppermute(piece, "tp", tp_hop(-k)) for k in (1, 2, 3)]


def tp_terms(parts):
    return [parts[0]] + [lax.ppermute(parts[k], "tp", tp_hop(k)) for k in (1, 3, 2)]


def tp_exchange(parts):
    return lax.all_to_all(parts, "tp", split_axis=0, concat_axis=0, tiled=True)


def tp_scatter(parts):
    return jnp.sum(tp_exchange(parts).astype(F32), axis=0)


def vmem(count):
    return [pl.BlockSpec(memory_space=pltpu.VMEM)] * count


def smem():
    return pl.BlockSpec(memory_space=pltpu.SMEM)


def local_call(body, out_shape, in_specs, flops, moved, scratch=()):
    many = isinstance(out_shape, (list, tuple))
    return pl.pallas_call(
        body,
        out_shape=out_shape,
        in_specs=in_specs,
        out_specs=vmem(len(out_shape)) if many else vmem(1)[0],
        scratch_shapes=list(scratch),
        cost_estimate=pl.CostEstimate(flops=flops, bytes_accessed=moved, transcendentals=0),
        compiler_params=pltpu.CompilerParams(vmem_limit_bytes=VMEM_BYTES),
    )


def nt_dot(left, right):
    return lax.dot_general(left, right, (((1,), (1,)), ((), ())), preferred_element_type=F32)


def pick_rows(slot, chunk, gain=None):
    hit = lax.broadcasted_iota(jnp.int32, (ROWS, chunk.shape[0]), 0) == slot
    pick = jnp.where(hit, 1.0, 0.0).astype(BF16)
    rows = jnp.dot(pick, chunk[...], preferred_element_type=F32)
    return (rows if gain is None else rows * gain).astype(BF16)


def store_groups(out, columns, value):
    for k in range(SIDE):
        out[k, :, columns] = value[k * ROWS : (k + 1) * ROWS].astype(BF16)


TILE = 256


def in_kernel(slot, gain, w_gate, w_up, *refs):
    chunks, (rows, both) = refs[:SIDE], refs[SIDE:]
    for k in range(SIDE):
        rows[k] = pick_rows(slot[k], chunks[k], gain[...])
    units = w_gate.shape[1]

    def step(n, unused):
        left = rows[...].reshape(SIDE * ROWS, -1)
        for at, weights in ((0, w_gate), (units, w_up)):
            columns = pl.ds(pl.multiple_of(n * TILE, TILE), TILE)
            target = pl.ds(pl.multiple_of(at + n * TILE, TILE), TILE)
            value = jnp.dot(left, weights[:, columns], preferred_element_type=F32)
            store_groups(both, target, value)
        return unused

    lax.fori_loop(0, units // TILE, step, 0)


def rows_through_in(slot, gain, w_gate, w_up, chunks):
    tokens, width = chunks[0].shape
    units = w_gate.shape[1]
    return local_call(
        in_kernel,
        [
            jax.ShapeDtypeStruct((SIDE, ROWS, width), BF16),
            jax.ShapeDtypeStruct((SIDE, ROWS, 2 * units), BF16),
        ],
        vmem(4 + SIDE),
        2 * SIDE * ROWS * width * (tokens + 2 * units),
        2 * width * (SIDE * (tokens + ROWS) + 2 * units),
    )(slot, gain, w_gate, w_up, *chunks)


def grad_kernel(place, slot, w_down, *refs):
    chunks, rows, parts = refs[:SIDE], refs[SIDE], refs[SIDE + 1 :]
    for k in range(SIDE):
        rows[k] = pick_rows(slot[k], chunks[k])

    def step(n, unused):
        left = jnp.concatenate([rows[place[k]] for k in range(SIDE)], axis=0)
        columns = pl.ds(pl.multiple_of(n * TILE, TILE), TILE)
        value = nt_dot(left, w_down[columns, :]).astype(BF16)
        for k in range(SIDE):
            parts[k][:, columns] = value[k * ROWS : (k + 1) * ROWS]
        return unused

    lax.fori_loop(0, w_down.shape[0] // TILE, step, 0)


def rows_through_down(place, slot, w_down, chunks):
    tokens, width = chunks[0].shape
    units = w_down.shape[0]
    rows, *parts = local_call(
        grad_kernel,
        [jax.ShapeDtypeStruct((SIDE, ROWS, width), BF16)]
        + [jax.ShapeDtypeStruct((ROWS, units), BF16)] * SIDE,
        [smem()] + vmem(2 + SIDE),
        2 * SIDE * ROWS * width * (tokens + units),
        2 * width * (SIDE * (tokens + ROWS) + units),
    )(place, slot, w_down, *chunks)
    return rows, parts


def back_kernel(place, w_gate, w_up, *refs):
    pieces, cots, out = refs[:SIDE], refs[SIDE], refs[SIDE + 1 :]
    units = w_gate.shape[1]
    for k in range(SIDE):
        cots[place[k]] = pieces[k][...]

    def step(n, unused):
        columns = pl.ds(pl.multiple_of(n * TILE, TILE), TILE)
        left = cots[...].reshape(SIDE * ROWS, 2 * units)
        rows = nt_dot(left[:, :units], w_gate[columns, :])
        rows = (rows + nt_dot(left[:, units:], w_up[columns, :])).astype(BF16)
        for k in range(SIDE):
            out[k][:, columns] = rows[k * ROWS : (k + 1) * ROWS]
        return unused

    lax.fori_loop(0, w_gate.shape[0] // TILE, step, 0)


def back_rows_of(place, w_gate, w_up, pieces):
    width, units = w_gate.shape
    cots, *back = local_call(
        back_kernel,
        [jax.ShapeDtypeStruct((SIDE, ROWS, 2 * units), BF16)]
        + [jax.ShapeDtypeStruct((ROWS, width), BF16)] * SIDE,
        [smem()] + vmem(2 + SIDE),
        4 * SIDE * ROWS * units * width,
        2 * (2 * SIDE * ROWS * units + 2 * units * width + SIDE * ROWS * width),
    )(place, w_gate, w_up, *pieces)
    return cots, back


def act_kernel(scales, gate_ups, *refs):
    cots, hidden_before = refs[:SIDE], refs[SIDE:-4]
    cot_out, hidden_out, row_cot, row_inner = refs[-4:]
    tile = 48
    count, width = cots[0].shape

    def step(n, unused):
        rows = pl.ds(pl.multiple_of(n * tile, tile), tile)

        def total(columns):
            return sum(gate_ups[k, rows, columns].astype(F32) for k in range(SIDE))

        weight, inv = scales[rows, 0:1], scales[rows, 1:2]
        gate = total(slice(0, width)) * inv
        up = total(slice(width, 2 * width)) * inv
        cot = sum(term[rows, :].astype(F32) for term in cots)
        sigma = 1.0 / (1.0 + jnp.exp(-gate))
        silu = gate * sigma
        hidden = silu * up
        row_cot[rows, :] = jnp.sum(cot * hidden, axis=1, keepdims=True)
        cot = cot * weight
        gate_cot = cot * up * (sigma + silu * (1.0 - sigma))
        up_cot = cot * silu
        row_inner[rows, :] = jnp.sum(gate_cot * gate + up_cot * up, axis=1, keepdims=True)
        cot_out[rows, :width] = (gate_cot * inv).astype(BF16)
        cot_out[rows, width:] = (up_cot * inv).astype(BF16)
        hidden = (hidden * weight).astype(BF16)
        if hidden_before:
            later = pl.ds(pl.multiple_of(count + n * tile, 16), tile)
            for k in range(SIDE):
                hidden_out[k, rows, :] = hidden_before[0][rows, :]
                hidden_out[k, later, :] = hidden
        else:
            hidden_out[rows, :] = hidden
        return unused

    lax.fori_loop(0, scales.shape[0] // tile, step, 0)


def act(scales, gate_ups, cots, *hidden_before):
    rows, hidden = cots[0].shape
    hidden_shape = (SIDE, 2 * rows, hidden) if hidden_before else (rows, hidden)
    return local_call(
        act_kernel,
        [
            jax.ShapeDtypeStruct((rows, 2 * hidden), BF16),
            jax.ShapeDtypeStruct(hidden_shape, BF16),
        ]
        + [jax.ShapeDtypeStruct((rows, 1), F32)] * 2,
        vmem(2 + SIDE + len(hidden_before)),
        40 * rows * hidden,
        48 * rows * hidden,
    )(scales, gate_ups, *cots, *hidden_before)


def combine_kernel(slots, *refs):
    rows, out, pick = refs[:GROUPS], refs[GROUPS], refs[GROUPS + 1]
    tokens = slots.shape[0]
    tile = 256
    for m in range(GROUPS):
        hit = lax.broadcasted_iota(jnp.int32, (tokens, ROWS), 1) == slots[:, m : m + 1]
        pick[m] = jnp.where(hit, 1.0, 0.0).astype(BF16)

    def step(n, unused):
        columns = pl.ds(pl.multiple_of(n * tile, tile), tile)
        total = jnp.dot(pick[0], rows[0][:, columns], preferred_element_type=F32)
        for m in range(1, GROUPS):
            total = total + jnp.dot(pick[m], rows[m][:, columns], preferred_element_type=F32)
        out[:, columns] = total.astype(BF16)
        return unused

    lax.fori_loop(0, out.shape[1] // tile, step, 0)


def combine(slots, rows):
    tokens, width = slots.shape[0], rows[0].shape[1]
    return local_call(
        combine_kernel,
        jax.ShapeDtypeStruct((tokens, width), BF16),
        vmem(1 + GROUPS),
        2 * GROUPS * ROWS * tokens * width,
        2 * (GROUPS * ROWS + tokens) * width,
        [pltpu.VMEM((GROUPS, tokens, ROWS), BF16)],
    )(slots, *rows)


def shared_kernel(w_in, w_out, *refs):
    ins, grads, out = refs[:GROUPS], refs[GROUPS : 2 * GROUPS], refs[2 * GROUPS]
    top = w_in.shape[0]
    for g in range(GROUPS):
        out[g % SIDE, g // SIDE, :top] = nt_dot(w_in[...], ins[g][...]).astype(BF16)
        out[g % SIDE, g // SIDE, top:] = nt_dot(w_out[...], grads[g][...]).astype(BF16)


def shared_partials(w_in, w_out, ins, grads):
    tokens, width = ins[0].shape
    hidden = w_in.shape[0] + w_out.shape[0]
    return local_call(
        shared_kernel,
        jax.ShapeDtypeStruct((SIDE, 2, hidden, tokens), BF16),
        vmem(2 + 2 * GROUPS),
        2 * GROUPS * tokens * width * hidden,
        4 * GROUPS * tokens * width,
    )(w_in, w_out, *ins, *grads)


def shared_grad_kernel(cots, gain, *refs):
    ins, grads = refs[:GROUPS], refs[GROUPS : 2 * GROUPS]
    out_in, out_down, sum_in, sum_down = refs[2 * GROUPS :]
    top = out_in.shape[0]
    for g in range(GROUPS):
        cot = cots[g % SIDE, g // SIDE]
        first = jnp.dot(cot[:top], ins[g][...], preferred_element_type=F32)
        second = jnp.dot(cot[top:], grads[g][...], preferred_element_type=F32)
        sum_in[...] = first if g == 0 else sum_in[...] + first
        sum_down[...] = second if g == 0 else sum_down[...] + second
    out_in[...] = (sum_in[...] * gain[...]).astype(BF16)
    out_down[...] = sum_down[...].astype(BF16)


def shared_grads(cots, gain, ins, grads, top):
    tokens, width = ins[0].shape
    rest = cots.shape[2] - top
    return local_call(
        shared_grad_kernel,
        [jax.ShapeDtypeStruct((top, width), BF16), jax.ShapeDtypeStruct((rest, width), BF16)],
        vmem(2 + 2 * GROUPS),
        2 * GROUPS * tokens * width * (top + rest),
        4 * GROUPS * tokens * width,
        [pltpu.VMEM((top, width), F32), pltpu.VMEM((rest, width), F32)],
    )(cots, gain, *ins, *grads)


def owner_kernel(place, cots, out):
    block = out.shape[2]
    for g in range(GROUPS):
        for i in range(SIDE):
            out[place[g * SIDE + i]] = cots[g % SIDE, g // SIDE, :, i * block : (i + 1) * block]


def by_owner(place, cots):
    rows, tokens = cots.shape[2:]
    return local_call(
        owner_kernel,
        jax.ShapeDtypeStruct((GROUPS * SIDE, rows, tokens // SIDE), BF16),
        [smem()] + vmem(1),
        0,
        4 * GROUPS * rows * tokens,
    )(place, cots)


def dense_hidden_kernel(place, w_down, *refs):
    chunks, out = refs[:GROUPS], refs[GROUPS]
    block = chunks[0].shape[0] // SIDE
    for g in range(GROUPS):
        columns = nt_dot(w_down[...], chunks[g][...]).astype(BF16)
        for i in range(SIDE):
            at = place[g * SIDE + i]
            lane = pl.multiple_of(lax.rem(at, 8) * block, block)
            out[lax.div(at, 8), :, pl.ds(lane, block)] = columns[:, i * block : (i + 1) * block]


def dense_hidden(place, w_down, chunks):
    tokens, width = chunks[0].shape
    hidden = w_down.shape[0]
    return local_call(
        dense_hidden_kernel,
        jax.ShapeDtypeStruct((SIDE, hidden, 2 * tokens), BF16),
        [smem()] + vmem(1 + GROUPS),
        2 * GROUPS * tokens * width * hidden,
        2 * GROUPS * tokens * width,
    )(place, w_down, *chunks)


def dense_grad_kernel(place, hidden, *refs):
    chunks, out, total = refs[:GROUPS], refs[GROUPS], refs[GROUPS + 1]
    block = chunks[0].shape[0] // SIDE
    for g in range(GROUPS):
        left = jnp.concatenate(
            [
                hidden[:, pl.ds(pl.multiple_of(place[g * SIDE + i] * block, block), block)]
                for i in range(SIDE)
            ],
            axis=1,
        )
        term = jnp.dot(left, chunks[g][...], preferred_element_type=F32)
        total[...] = term if g == 0 else total[...] + term
    out[...] = total[...].astype(BF16)


def dense_grad(place, hidden, chunks):
    tokens, width = chunks[0].shape
    units = hidden.shape[0]
    return local_call(
        dense_grad_kernel,
        jax.ShapeDtypeStruct((units, width), BF16),
        [smem()] + vmem(1 + GROUPS),
        2 * GROUPS * tokens * width * units,
        2 * GROUPS * tokens * width,
        [pltpu.VMEM((units, width), F32)],
    )(place, hidden, *chunks)


def gate_grads(hidden_cot, gate_value, up_value):
    sigma = jax.nn.sigmoid(gate_value)
    gate_cot = hidden_cot * up_value * sigma * (1.0 + gate_value * (1.0 - sigma))
    up_cot = hidden_cot * gate_value * sigma
    return (gate_cot, up_cot)


def local(
    hidden_in,
    out_grad,
    norm_gain,
    router_weight,
    route_ids,
    expert_gate,
    expert_up,
    expert_down,
    shared_gate,
    shared_up,
    shared_down,
    dense_gate,
    dense_up,
    dense_down,
):
    tok_rows, quarter = hidden_in.shape
    feature_count = quarter * lax.axis_size("tp")
    ep, tp = lax.axis_index("ep"), lax.axis_index("tp")
    z, y, core = ep // 8, (ep // 2) % SIDE, ep % 2
    w_gate, w_up, w_down = expert_gate[0], expert_up[0], expert_down[0]
    gain = norm_gain[None, :]

    in_chunks, grad_chunks = path_gather([hidden_in, out_grad])

    g_at = jnp.arange(GROUPS, dtype=jnp.int32)[:, None]
    i_at = jnp.arange(SIDE, dtype=jnp.int32)[None, :]
    j_at = g_at % SIDE
    block_core = (core + g_at // SIDE) % 2
    block_z = jnp.where(block_core == 0, z - i_at, z - j_at) % SIDE
    block_y = jnp.where(block_core == 0, y - j_at, y - i_at) % SIDE
    block_of = ((block_z * SIDE + block_y) * 2 + block_core).reshape(-1)
    to_path = (block_of[:, None] == jnp.arange(EXPERTS, dtype=jnp.int32)[None, :]).astype(F32)

    picks = jnp.any(
        route_ids[:, :, None] == jnp.arange(EXPERTS, dtype=jnp.int32)[None, None, :], axis=1
    ).astype(F32)
    token_line = jnp.arange(tok_rows, dtype=jnp.int32)
    earlier = (token_line[:, None] < token_line[None, :]).astype(F32)
    own_position = jnp.dot(picks.T, earlier, precision=HIGHEST)
    own_position = jnp.where(picks.T > 0.0, own_position, -1.0)
    positions = lax.all_to_all(own_position, "ep", split_axis=0, concat_axis=0, tiled=True)
    position = jnp.dot(to_path, positions, precision=HIGHEST).astype(jnp.int32)
    position = position.reshape(GROUPS, SIDE, tok_rows)
    offset = (CAP * jnp.arange(SIDE, dtype=jnp.int32))[None, :, None]
    slot = jnp.where(position >= 0, position + offset, -1).reshape(GROUPS, 1, SIDE * tok_rows)

    wide_in = hidden_in.astype(F32)
    square_part = jnp.sum(wide_in * wide_in, axis=1, keepdims=True)
    logit_part = jnp.dot(wide_in * gain, router_weight, precision=HIGHEST)
    stats = jnp.concatenate([logit_part, square_part], axis=1)
    stats, unused = lax.optimization_barrier((stats, positions))
    stats = tp_scatter(jnp.broadcast_to(stats[None], (SIDE,) + stats.shape))
    plain_logits = stats[:, :EXPERTS]
    mean_square = stats[:, EXPERTS:] / feature_count + EPSILON
    inv_rms = lax.rsqrt(mean_square)
    rms = mean_square * inv_rms
    normed = (wide_in * inv_rms * gain).astype(BF16)
    scores = jax.nn.sigmoid(plain_logits * inv_rms)
    chosen = picks * scores
    chosen_total = jnp.sum(chosen, axis=1, keepdims=True)
    route_weight = ROUTE_SCALE * chosen / chosen_total

    told = jnp.concatenate(
        [
            route_weight.T[:, None, :],
            jnp.broadcast_to(inv_rms.reshape(1, 1, tok_rows), (EXPERTS, 1, tok_rows)),
        ],
        axis=1,
    )
    told = lax.all_to_all(told, "ep", split_axis=0, concat_axis=0, tiled=True)
    slot, told = lax.optimization_barrier((slot, told))
    told_path = jnp.dot(to_path, told.reshape(EXPERTS, 2 * tok_rows), precision=HIGHEST)
    told_path = told_path.reshape(2, SIDE, SIDE, 2, tok_rows)
    own_told = lax.dynamic_index_in_dim(told_path, tp, 1, keepdims=False)
    own_weight = own_told[:, :, 0].reshape(2, 1, SIDE * tok_rows)
    own_inv = own_told[:, :, 1].reshape(2, 1, SIDE * tok_rows)

    s_line = jnp.arange(2, dtype=jnp.int32)[None, :]
    j_line = jnp.arange(SIDE, dtype=jnp.int32)
    j_col = j_line[:, None]
    return_expert = jnp.where(
        core == 0,
        (z * SIDE + (y + j_col) % SIDE) * 2 + s_line,
        (((z + j_col) % SIDE) * SIDE + y) * 2 + 1 - s_line,
    ).reshape(-1)
    pick_expert = (
        return_expert[:, None] == jnp.arange(EXPERTS, dtype=jnp.int32)[None, :]
    ).astype(F32)
    line_position, *unused = lax.optimization_barrier((own_position, *grad_chunks[1:SIDE]))
    line_position = jnp.stack(
        [line_position]
        + [lax.ppermute(line_position, "ep", first_hop(k)) for k in range(1, SIDE)]
    )
    position_here = jnp.einsum(
        "ket,me->ktm", line_position, pick_expert, precision=HIGHEST
    ).astype(jnp.int32)
    return_slot = jnp.where(
        position_here >= 0, position_here + (CAP * j_line)[:, None, None], -1
    ).reshape(SIDE * tok_rows, GROUPS)

    own, other = slice(0, SIDE), slice(SIDE, GROUPS)
    halves = (own, other)
    rows_in, both_terms, rows_grad, cot_terms = [], [], [], []
    for half in halves:
        rows, part = rows_through_in(slot[half], gain, w_gate, w_up, in_chunks[half])
        rows_in.append(rows)
        both_terms.append(tp_exchange(part))
    turn = (jnp.arange(SIDE, dtype=jnp.int32) + tp) % SIDE
    for half in halves:
        rows, parts = rows_through_down(turn, slot[half], w_down, grad_chunks[half])
        rows_grad.append(rows)
        cot_terms.append(tp_terms(parts))
    hidden_part = parts[0]
    own_slot = jnp.stack(
        [lax.dynamic_index_in_dim(slot[half], tp, 0, keepdims=False) for half in halves]
    )
    own_hit = jnp.arange(ROWS, dtype=jnp.int32)[None, :, None] == own_slot
    row_scales = jnp.concatenate(
        [
            jnp.sum(jnp.where(own_hit, value, 0.0), axis=2, keepdims=True)
            for value in (own_weight, own_inv)
        ],
        axis=2,
    )
    both_cots, hiddens, row_cots, row_inners = [], (), [], []
    for n in range(2):
        both_cot, hidden, row_cot, row_inner = act(
            row_scales[n], both_terms[n], cot_terms[n], *hiddens
        )
        both_cots.append(tp_gather(both_cot))
        hiddens = (hidden,)
        row_cots.append(row_cot)
        row_inners.append(row_inner)
    back, ordered_cots = [], []
    turn, return_slot = lax.optimization_barrier((turn, return_slot))
    for n in range(2):
        ordered, rows = back_rows_of(turn, w_gate, w_up, both_cots[n])
        ordered_cots.append(ordered)
        back.extend(rows)

    returned = []
    for j in range(SIDE):
        returned.append(back[j] if j == 0 else lax.ppermute(back[j], "ep", second_hop(-j)))
        returned.append(lax.ppermute(back[SIDE + j], "ep", swap_second_hop(-j)))
    summed = combine(return_slot, returned).reshape(SIDE, tok_rows, quarter)
    routed_cot = summed[0].astype(F32)
    for k in range(1, SIDE):
        routed_cot = routed_cot + lax.ppermute(summed[k], "ep", first_hop(-k)).astype(F32)

    units = shared_down.shape[0]
    shared_in = (jnp.concatenate([shared_gate.T, shared_up.T], axis=0).astype(F32) * gain).astype(
        BF16
    )
    shared_out = jnp.concatenate([shared_down, jnp.zeros((8, quarter), BF16)], axis=0)
    late_in, late_grad, unused = lax.optimization_barrier((in_chunks, grad_chunks, hidden_part))
    parts = shared_partials(shared_in, shared_out, late_in, late_grad)
    inner = parts.shape[2]
    shared_sum = tp_scatter(parts)
    gate_s = shared_sum[:, :units] * own_inv
    up_s = shared_sum[:, units : 2 * units] * own_inv
    hid_cot_s = shared_sum[:, 2 * units : 3 * units]
    gate_cot_s, up_cot_s = gate_grads(hid_cot_s, gate_s, up_s)

    def to_tokens(row_values):
        return jnp.sum(jnp.where(own_hit, jnp.stack(row_values), 0.0), axis=1, keepdims=True)

    shared_inner = jnp.sum(gate_cot_s * gate_s + up_cot_s * up_s, axis=1, keepdims=True)
    cots = jnp.concatenate(
        [
            gate_cot_s * own_inv,
            up_cot_s * own_inv,
            gate_s * jax.nn.sigmoid(gate_s) * up_s,
            to_tokens(row_cots),
            to_tokens(row_inners) + shared_inner,
            jnp.zeros((2, inner - 3 * units - 2, SIDE * tok_rows), F32),
        ],
        axis=1,
    ).astype(BF16)
    cots_all = tp_exchange(jnp.broadcast_to(cots[None], (SIDE,) + cots.shape))
    to_owner = by_owner(block_of, cots_all)
    to_owner = lax.all_to_all(to_owner, "ep", split_axis=0, concat_axis=0, tiled=True)
    shared_whole = lax.all_gather(shared_in, "ep", axis=0, tiled=True)
    shared_scaled = lax.dot_general(
        to_owner[:, : 2 * units].reshape(-1, tok_rows),
        shared_whole,
        (((0,), (0,)), ((), ())),
        preferred_element_type=F32,
    ) * rms

    sums = to_owner[:, 3 * units : 3 * units + 2].astype(F32)
    weight_cot = sums[:, 0].T
    chosen_cot = picks * (
        ROUTE_SCALE
        * (
            weight_cot / chosen_total
            - jnp.sum(weight_cot * chosen, axis=1, keepdims=True) / (chosen_total * chosen_total)
        )
    )
    logit_cot = chosen_cot * scores * (1.0 - scores)
    router_part = jnp.dot(logit_cot.T, normed.astype(F32), precision=HIGHEST)
    router_cot = jnp.dot(logit_cot, router_weight.T, precision=HIGHEST)
    inner_sum = jnp.sum(sums[:, 1], axis=0).reshape(tok_rows, 1) * rms + jnp.sum(
        logit_cot * plain_logits, axis=1, keepdims=True
    )

    scaled = (routed_cot * rms + router_cot) * gain + shared_scaled
    input_cot = inv_rms * scaled - wide_in * (inv_rms * inv_rms * inv_rms) * (
        inner_sum / feature_count
    )
    dense_cot = (out_grad.astype(F32) + input_cot).astype(BF16)

    (cot_chunks,) = path_gather([dense_cot])
    gate_t, up_t = dense_gate.T, dense_up.T
    hidden2 = (jax.nn.silu(gate_t.astype(F32)) * up_t.astype(F32)).astype(BF16)

    def flat(parts, columns=slice(None)):
        whole = jnp.concatenate([part[:, :, columns] for part in parts], axis=1)
        return whole.reshape(GROUPS * ROWS, -1)

    def rows_dot(left, right):
        return lax.dot_general(
            left, right, (((0,), (0,)), ((), ())), preferred_element_type=F32
        ).astype(BF16)[None]

    cots_k8, unused = lax.optimization_barrier((cots_all, back[-1]))
    grads_in, grads_down = shared_grads(cots_k8, gain, in_chunks, grad_chunks, 2 * units)
    rows_late, cots_late, unused = lax.optimization_barrier((rows_in, ordered_cots, summed))
    units_r = w_gate.shape[1]
    rows_late = flat(rows_late)
    grad_expert_gate = rows_dot(rows_late, flat(cots_late, slice(0, units_r)))
    hidden_all, unused = lax.optimization_barrier((hiddens[0], back[-1]))
    hidden_all = tp_exchange(hidden_all).reshape(GROUPS * ROWS, -1)

    cot_ready, hidden2, unused = lax.optimization_barrier(
        (cot_chunks, hidden2, (grads_in, grad_expert_gate))
    )
    hidden2_part = dense_hidden(block_of, dense_down, cot_ready)
    hidden2_cot = tp_scatter(hidden2_part)
    share = 8 * tok_rows
    gate_mine = lax.dynamic_slice_in_dim(gate_t, tp * share, share, 1).astype(F32)
    up_mine = lax.dynamic_slice_in_dim(up_t, tp * share, share, 1).astype(F32)
    grad_gate2, grad_up2 = gate_grads(hidden2_cot, gate_mine, up_mine)
    grad_dense_down = dense_grad(block_of, hidden2, cot_ready)
    grad_router = ep_sum(
        router_part, (summed, cot_chunks[0], cot_chunks[1], hidden2_part, grad_dense_down)
    ).T
    rows_last, cots_last, rows_grad, unused = lax.optimization_barrier(
        (rows_late, cots_late, rows_grad, hidden2_part)
    )

    return (
        grad_gate2.astype(BF16).T,
        grad_up2.astype(BF16).T,
        grad_dense_down,
        grad_expert_gate,
        rows_dot(rows_last, flat(cots_last, slice(units_r, None))),
        rows_dot(hidden_all, flat(rows_grad)),
        grads_in[:units].T,
        grads_in[units:].T,
        grads_down[:units],
        grad_router,
    )


def solution(mesh):
    in_specs = (
        P("ep", "tp"),
        P("ep", "tp"),
        P("tp"),
        P("tp", None),
        P("ep", None),
        P("ep", "tp", None),
        P("ep", "tp", None),
        P("ep", None, "tp"),
        P("tp", "ep"),
        P("tp", "ep"),
        P("ep", "tp"),
        P(None, "ep"),
        P(None, "ep"),
        P("ep", "tp"),
    )
    out_specs = (
        P("tp", "ep"),
        P("tp", "ep"),
        P("ep", "tp"),
        P("ep", "tp", None),
        P("ep", "tp", None),
        P("ep", None, "tp"),
        P("tp", "ep"),
        P("tp", "ep"),
        P("ep", "tp"),
        P("tp", None),
    )
    return jax.shard_map(local, mesh=mesh, in_specs=in_specs, out_specs=out_specs, check_vma=False)
```

```python
import functools

import jax
import jax.numpy as jnp
from jax import lax
from jax.experimental import pallas as pl
from jax.experimental.pallas import tpu as pltpu
from jax.sharding import PartitionSpec as P

EXPERTS = 32
TOP = 8
CAP = 36
SIDE = 4
GROUPS = 8
ROWS = SIDE * CAP

EPSILON = 1e-05
ROUTE_SCALE = 2.5
F32 = jnp.float32
BF16 = jnp.bfloat16
HIGHEST = lax.Precision.HIGHEST
VMEM_BYTES = 50 * 1024 * 1024


def ep_at(z, y, core):
    return ((z % SIDE) * SIDE + y % SIDE) * 2 + core


def ep_pairs(target):
    return [
        (ep_at(z, y, core), target(z, y, core))
        for z in range(SIDE)
        for y in range(SIDE)
        for core in range(2)
    ]


def first_hop(k):
    return ep_pairs(lambda z, y, core: ep_at(z, y + k, 1) if core else ep_at(z + k, y, 0))


def first_lines():
    core_0 = [[ep_at(z, y, 0) for z in range(SIDE)] for y in range(SIDE)]
    return core_0 + [[ep_at(z, y, 1) for y in range(SIDE)] for z in range(SIDE)]


def second_hop(k):
    return ep_pairs(lambda z, y, core: ep_at(z + k, y, 1) if core else ep_at(z, y + k, 0))


def swap_second_hop(k):
    return ep_pairs(lambda z, y, core: ep_at(z, y + k, 0) if core else ep_at(z + k, y, 1))


def core_swap():
    return ep_pairs(lambda z, y, core: ep_at(z, y, 1 - core))


def tp_hop(k):
    return [(i, (i + k) % SIDE) for i in range(SIDE)]


def join_kernel(*refs):
    blocks, outs = refs[:SIDE], refs[SIDE:]
    rows = blocks[0].shape[0] // len(outs)
    for i in range(SIDE):
        for n, out in enumerate(outs):
            out[i * rows : (i + 1) * rows] = blocks[i][n * rows : (n + 1) * rows]


def join(blocks, count):
    rows, width = blocks[0].shape
    return local_call(
        join_kernel,
        [jax.ShapeDtypeStruct((SIDE * rows // count, width), blocks[0].dtype)] * count,
        vmem(SIDE),
        0,
        4 * SIDE * rows * width,
    )(*blocks)


def path_gather(blocks, after=()):
    stack = jnp.concatenate(blocks, axis=0) if len(blocks) > 1 else blocks[0]
    first = [stack] + [lax.ppermute(stack, "ep", first_hop(k)) for k in range(1, SIDE)]
    first, unused = lax.optimization_barrier((first, after))
    gathered = []
    for joined in join(first, len(blocks)):
        if gathered:
            joined, *unused = lax.optimization_barrier((joined, *gathered[-1][1:]))
        own = [joined] + [lax.ppermute(joined, "ep", second_hop(k)) for k in range(1, SIDE)]
        other = [lax.ppermute(chunk, "ep", core_swap()) for chunk in own]
        gathered.append(own + other)
    return gathered


def ep_sum(value, stages):
    pairings = ((0, 0, 1), (0, 1, 0), (1, 0, 0), (0, 2, 0), (2, 0, 0))
    for (dz, dy, dcore), stage in zip(pairings, stages, strict=True):
        pairs = ep_pairs(lambda z, y, core: ep_at(z ^ dz, y ^ dy, core ^ dcore))
        met = lax.ppermute(value, "ep", pairs)
        met, unused = lax.optimization_barrier((met, stage))
        value = value + met
    return value


def tp_gather(piece):
    return [piece] + [lax.ppermute(piece, "tp", tp_hop(-k)) for k in (1, 2, 3)]


def tp_terms(parts):
    return [parts[0]] + [lax.ppermute(parts[k], "tp", tp_hop(k)) for k in (1, 3, 2)]


def tp_exchange(parts):
    return lax.all_to_all(parts, "tp", split_axis=0, concat_axis=0, tiled=True)


def tp_scatter(parts):
    return jnp.sum(tp_exchange(parts).astype(F32), axis=0)


def vmem(count):
    return [pl.BlockSpec(memory_space=pltpu.VMEM)] * count


def smem():
    return pl.BlockSpec(memory_space=pltpu.SMEM)


def local_call(body, out_shape, in_specs, flops, moved, scratch=()):
    many = isinstance(out_shape, (list, tuple))
    return pl.pallas_call(
        body,
        out_shape=out_shape,
        in_specs=in_specs,
        out_specs=vmem(len(out_shape)) if many else vmem(1)[0],
        scratch_shapes=list(scratch),
        cost_estimate=pl.CostEstimate(flops=flops, bytes_accessed=moved, transcendentals=0),
        compiler_params=pltpu.CompilerParams(vmem_limit_bytes=VMEM_BYTES),
    )


def nt_dot(left, right):
    return lax.dot_general(left, right, (((1,), (1,)), ((), ())), preferred_element_type=F32)


def pick_rows(slot, chunk, gain=None):
    hit = lax.broadcasted_iota(jnp.int32, (ROWS, chunk.shape[0]), 0) == slot
    pick = jnp.where(hit, 1.0, 0.0).astype(BF16)
    rows = jnp.dot(pick, chunk[...], preferred_element_type=F32)
    return (rows if gain is None else rows * gain).astype(BF16)


def store_groups(out, columns, value):
    for k in range(SIDE):
        out[k, :, columns] = value[k * ROWS : (k + 1) * ROWS].astype(BF16)


TILE = 256


def in_kernel(slot, gain, w_gate, w_up, *refs):
    chunks, (rows, both) = refs[:SIDE], refs[SIDE:]
    for k in range(SIDE):
        rows[k] = pick_rows(slot[k], chunks[k], gain[...])
    units = w_gate.shape[1]

    def step(n, unused):
        left = rows[...].reshape(SIDE * ROWS, -1)
        for at, weights in ((0, w_gate), (units, w_up)):
            columns = pl.ds(pl.multiple_of(n * TILE, TILE), TILE)
            target = pl.ds(pl.multiple_of(at + n * TILE, TILE), TILE)
            value = jnp.dot(left, weights[:, columns], preferred_element_type=F32)
            store_groups(both, target, value)
        return unused

    lax.fori_loop(0, units // TILE, step, 0)


def rows_through_in(slot, gain, w_gate, w_up, chunks):
    tokens, width = chunks[0].shape
    units = w_gate.shape[1]
    return local_call(
        in_kernel,
        [
            jax.ShapeDtypeStruct((SIDE, ROWS, width), BF16),
            jax.ShapeDtypeStruct((SIDE, ROWS, 2 * units), BF16),
        ],
        vmem(4 + SIDE),
        2 * SIDE * ROWS * width * (tokens + 2 * units),
        2 * width * (SIDE * (tokens + ROWS) + 2 * units),
    )(slot, gain, w_gate, w_up, *chunks)


def grad_kernel(place, slot, w_down, *refs):
    chunks, rows, parts = refs[:SIDE], refs[SIDE], refs[SIDE + 1 :]
    for k in range(SIDE):
        rows[k] = pick_rows(slot[k], chunks[k])

    def step(n, unused):
        left = jnp.concatenate([rows[place[k]] for k in range(SIDE)], axis=0)
        columns = pl.ds(pl.multiple_of(n * TILE, TILE), TILE)
        value = nt_dot(left, w_down[columns, :]).astype(BF16)
        for k in range(SIDE):
            parts[k][:, columns] = value[k * ROWS : (k + 1) * ROWS]
        return unused

    lax.fori_loop(0, w_down.shape[0] // TILE, step, 0)


def rows_through_down(place, slot, w_down, chunks):
    tokens, width = chunks[0].shape
    units = w_down.shape[0]
    rows, *parts = local_call(
        grad_kernel,
        [jax.ShapeDtypeStruct((SIDE, ROWS, width), BF16)]
        + [jax.ShapeDtypeStruct((ROWS, units), BF16)] * SIDE,
        [smem()] + vmem(2 + SIDE),
        2 * SIDE * ROWS * width * (tokens + units),
        2 * width * (SIDE * (tokens + ROWS) + units),
    )(place, slot, w_down, *chunks)
    return rows, parts


def back_kernel(place, w_gate, w_up, *refs):
    pieces, cots, out = refs[:SIDE], refs[SIDE], refs[SIDE + 1 :]
    units = w_gate.shape[1]
    for k in range(SIDE):
        cots[place[k]] = pieces[k][...]

    def step(n, unused):
        columns = pl.ds(pl.multiple_of(n * TILE, TILE), TILE)
        left = cots[...].reshape(SIDE * ROWS, 2 * units)
        rows = nt_dot(left[:, :units], w_gate[columns, :])
        rows = (rows + nt_dot(left[:, units:], w_up[columns, :])).astype(BF16)
        for k in range(SIDE):
            out[k][:, columns] = rows[k * ROWS : (k + 1) * ROWS]
        return unused

    lax.fori_loop(0, w_gate.shape[0] // TILE, step, 0)


def back_rows_of(place, w_gate, w_up, pieces):
    width, units = w_gate.shape
    cots, *back = local_call(
        back_kernel,
        [jax.ShapeDtypeStruct((SIDE, ROWS, 2 * units), BF16)]
        + [jax.ShapeDtypeStruct((ROWS, width), BF16)] * SIDE,
        [smem()] + vmem(2 + SIDE),
        4 * SIDE * ROWS * units * width,
        2 * (2 * SIDE * ROWS * units + 2 * units * width + SIDE * ROWS * width),
    )(place, w_gate, w_up, *pieces)
    return cots, back


def act_kernel(scales, gate_ups, *refs):
    cots, hidden_before = refs[:SIDE], refs[SIDE:-4]
    cot_out, hidden_out, row_cot, row_inner = refs[-4:]
    tile = 48
    count, width = cots[0].shape

    def step(n, unused):
        rows = pl.ds(pl.multiple_of(n * tile, tile), tile)

        def total(columns):
            return sum(gate_ups[k, rows, columns].astype(F32) for k in range(SIDE))

        weight, inv = scales[rows, 0:1], scales[rows, 1:2]
        gate = total(slice(0, width)) * inv
        up = total(slice(width, 2 * width)) * inv
        cot = sum(term[rows, :].astype(F32) for term in cots)
        sigma = 1.0 / (1.0 + jnp.exp(-gate))
        silu = gate * sigma
        hidden = silu * up
        row_cot[rows, :] = jnp.sum(cot * hidden, axis=1, keepdims=True)
        cot = cot * weight
        gate_cot = cot * up * (sigma + silu * (1.0 - sigma))
        up_cot = cot * silu
        row_inner[rows, :] = jnp.sum(gate_cot * gate + up_cot * up, axis=1, keepdims=True)
        cot_out[rows, :width] = (gate_cot * inv).astype(BF16)
        cot_out[rows, width:] = (up_cot * inv).astype(BF16)
        hidden = (hidden * weight).astype(BF16)
        if hidden_before:
            later = pl.ds(pl.multiple_of(count + n * tile, 16), tile)
            for k in range(SIDE):
                hidden_out[k, rows, :] = hidden_before[0][rows, :]
                hidden_out[k, later, :] = hidden
        else:
            hidden_out[rows, :] = hidden
        return unused

    lax.fori_loop(0, scales.shape[0] // tile, step, 0)


def act(scales, gate_ups, cots, *hidden_before):
    rows, hidden = cots[0].shape
    hidden_shape = (SIDE, 2 * rows, hidden) if hidden_before else (rows, hidden)
    return local_call(
        act_kernel,
        [
            jax.ShapeDtypeStruct((rows, 2 * hidden), BF16),
            jax.ShapeDtypeStruct(hidden_shape, BF16),
        ]
        + [jax.ShapeDtypeStruct((rows, 1), F32)] * 2,
        vmem(2 + SIDE + len(hidden_before)),
        40 * rows * hidden,
        48 * rows * hidden,
    )(scales, gate_ups, *cots, *hidden_before)


def combine_kernel(slots, *refs):
    rows, out, pick = refs[:GROUPS], refs[GROUPS:-1], refs[-1]
    tokens = slots.shape[0]
    block = tokens // SIDE
    for m in range(GROUPS):
        hit = lax.broadcasted_iota(jnp.int32, (tokens, ROWS), 1) == slots[:, m : m + 1]
        pick[m] = jnp.where(hit, 1.0, 0.0).astype(BF16)

    def step(n, unused):
        columns = pl.ds(pl.multiple_of(n * TILE, TILE), TILE)
        total = jnp.dot(pick[0], rows[0][:, columns], preferred_element_type=F32)
        for m in range(1, GROUPS):
            total = total + jnp.dot(pick[m], rows[m][:, columns], preferred_element_type=F32)
        total = total.astype(BF16)
        for k in range(SIDE):
            out[k][:, columns] = total[k * block : (k + 1) * block]
        return unused

    lax.fori_loop(0, rows[0].shape[1] // TILE, step, 0)


def combine(slots, rows):
    tokens, width = slots.shape[0], rows[0].shape[1]
    return local_call(
        combine_kernel,
        [jax.ShapeDtypeStruct((tokens // SIDE, width), BF16)] * SIDE,
        vmem(1 + GROUPS),
        2 * GROUPS * ROWS * tokens * width,
        2 * (GROUPS * ROWS + tokens) * width,
        [pltpu.VMEM((GROUPS, tokens, ROWS), BF16)],
    )(slots, *rows)


def shared_kernel(w_in, w_out, *refs):
    ins, grads, out = refs[:GROUPS], refs[GROUPS : 2 * GROUPS], refs[2 * GROUPS]
    top = w_in.shape[0]
    for g in range(GROUPS):
        out[g % SIDE, g // SIDE, :top] = nt_dot(w_in[...], ins[g][...]).astype(BF16)
        out[g % SIDE, g // SIDE, top:] = nt_dot(w_out[...], grads[g][...]).astype(BF16)


def shared_partials(w_in, w_out, ins, grads):
    tokens, width = ins[0].shape
    hidden = w_in.shape[0] + w_out.shape[0]
    return local_call(
        shared_kernel,
        jax.ShapeDtypeStruct((SIDE, 2, hidden, tokens), BF16),
        vmem(2 + 2 * GROUPS),
        2 * GROUPS * tokens * width * hidden,
        4 * GROUPS * tokens * width,
    )(w_in, w_out, *ins, *grads)


def shared_grad_kernel(cots, gain, *refs):
    ins, grads = refs[:GROUPS], refs[GROUPS : 2 * GROUPS]
    out_in, out_down, sum_in, sum_down = refs[2 * GROUPS :]
    top = out_in.shape[0]
    for g in range(GROUPS):
        cot = cots[g % SIDE, g // SIDE]
        first = jnp.dot(cot[:top], ins[g][...], preferred_element_type=F32)
        second = jnp.dot(cot[top:], grads[g][...], preferred_element_type=F32)
        sum_in[...] = first if g == 0 else sum_in[...] + first
        sum_down[...] = second if g == 0 else sum_down[...] + second
    out_in[...] = (sum_in[...] * gain[...]).astype(BF16)
    out_down[...] = sum_down[...].astype(BF16)


def shared_grads(cots, gain, ins, grads, top):
    tokens, width = ins[0].shape
    rest = cots.shape[2] - top
    return local_call(
        shared_grad_kernel,
        [jax.ShapeDtypeStruct((top, width), BF16), jax.ShapeDtypeStruct((rest, width), BF16)],
        vmem(2 + 2 * GROUPS),
        2 * GROUPS * tokens * width * (top + rest),
        4 * GROUPS * tokens * width,
        [pltpu.VMEM((top, width), F32), pltpu.VMEM((rest, width), F32)],
    )(cots, gain, *ins, *grads)


def owner_kernel(place, cots, out):
    block = out.shape[2]
    for g in range(GROUPS):
        for i in range(SIDE):
            out[place[g * SIDE + i]] = cots[g % SIDE, g // SIDE, :, i * block : (i + 1) * block]


def by_owner(place, cots):
    rows, tokens = cots.shape[2:]
    return local_call(
        owner_kernel,
        jax.ShapeDtypeStruct((GROUPS * SIDE, rows, tokens // SIDE), BF16),
        [smem()] + vmem(1),
        0,
        4 * GROUPS * rows * tokens,
    )(place, cots)


def dense_hidden_kernel(place, w_down, *refs):
    chunks, out = refs[:SIDE], refs[SIDE]
    block = chunks[0].shape[0] // SIDE
    for g in range(SIDE):
        columns = nt_dot(w_down[...], chunks[g][...]).astype(BF16)
        for i in range(SIDE):
            at = place[g * SIDE + i]
            lane = pl.multiple_of(lax.rem(at, SIDE) * block, block)
            out[lax.div(at, SIDE), :, pl.ds(lane, block)] = columns[
                :, i * block : (i + 1) * block
            ]


def dense_hidden(place, w_down, chunks):
    tokens, width = chunks[0].shape
    hidden = w_down.shape[0]
    return local_call(
        dense_hidden_kernel,
        jax.ShapeDtypeStruct((SIDE, hidden, tokens), BF16),
        [smem()] + vmem(1 + SIDE),
        2 * SIDE * tokens * width * hidden,
        2 * SIDE * tokens * width,
    )(place, w_down, *chunks)


def dense_grad_kernel(place, hidden, *refs):
    chunks, out, total = refs[:GROUPS], refs[GROUPS], refs[GROUPS + 1]
    block = chunks[0].shape[0] // SIDE
    for g in range(GROUPS):
        left = jnp.concatenate(
            [
                hidden[:, pl.ds(pl.multiple_of(place[g * SIDE + i] * block, block), block)]
                for i in range(SIDE)
            ],
            axis=1,
        )
        term = jnp.dot(left, chunks[g][...], preferred_element_type=F32)
        total[...] = term if g == 0 else total[...] + term
    out[...] = total[...].astype(BF16)


def dense_grad(place, hidden, chunks):
    tokens, width = chunks[0].shape
    units = hidden.shape[0]
    return local_call(
        dense_grad_kernel,
        jax.ShapeDtypeStruct((units, width), BF16),
        [smem()] + vmem(1 + GROUPS),
        2 * GROUPS * tokens * width * units,
        2 * GROUPS * tokens * width,
        [pltpu.VMEM((units, width), F32)],
    )(place, hidden, *chunks)


def gate_grads(hidden_cot, gate_value, up_value):
    sigma = jax.nn.sigmoid(gate_value)
    gate_cot = hidden_cot * up_value * sigma * (1.0 + gate_value * (1.0 - sigma))
    up_cot = hidden_cot * gate_value * sigma
    return (gate_cot, up_cot)


def local(
    hidden_in,
    out_grad,
    norm_gain,
    router_weight,
    route_ids,
    expert_gate,
    expert_up,
    expert_down,
    shared_gate,
    shared_up,
    shared_down,
    dense_gate,
    dense_up,
    dense_down,
):
    tok_rows, quarter = hidden_in.shape
    feature_count = quarter * lax.axis_size("tp")
    ep, tp = lax.axis_index("ep"), lax.axis_index("tp")
    z, y, core = ep // 8, (ep // 2) % SIDE, ep % 2
    w_gate, w_up, w_down = expert_gate[0], expert_up[0], expert_down[0]
    gain = norm_gain[None, :]

    g_at = jnp.arange(GROUPS, dtype=jnp.int32)[:, None]
    i_at = jnp.arange(SIDE, dtype=jnp.int32)[None, :]
    j_at = g_at % SIDE
    block_core = (core + g_at // SIDE) % 2
    block_z = jnp.where(block_core == 0, z - i_at, z - j_at) % SIDE
    block_y = jnp.where(block_core == 0, y - j_at, y - i_at) % SIDE
    block_of = ((block_z * SIDE + block_y) * 2 + block_core).reshape(-1)
    to_path = (block_of[:, None] == jnp.arange(EXPERTS, dtype=jnp.int32)[None, :]).astype(F32)

    picks = jnp.any(
        route_ids[:, :, None] == jnp.arange(EXPERTS, dtype=jnp.int32)[None, None, :], axis=1
    ).astype(F32)
    token_line = jnp.arange(tok_rows, dtype=jnp.int32)
    earlier = (token_line[:, None] < token_line[None, :]).astype(F32)
    own_position = jnp.dot(picks.T, earlier, precision=HIGHEST)
    own_position = jnp.where(picks.T > 0.0, own_position, -1.0)
    wide_in = hidden_in.astype(F32)
    square_part = jnp.sum(wide_in * wide_in, axis=1, keepdims=True)
    logit_part = jnp.dot(wide_in * gain, router_weight, precision=HIGHEST)
    stats = jnp.concatenate([logit_part, square_part], axis=1)
    stats = tp_scatter(jnp.broadcast_to(stats[None], (SIDE,) + stats.shape))
    plain_logits = stats[:, :EXPERTS]
    mean_square = stats[:, EXPERTS:] / feature_count + EPSILON
    inv_rms = lax.rsqrt(mean_square)
    rms = mean_square * inv_rms
    normed = (wide_in * inv_rms * gain).astype(BF16)
    scores = jax.nn.sigmoid(plain_logits * inv_rms)
    chosen = picks * scores
    chosen_total = jnp.sum(chosen, axis=1, keepdims=True)
    route_weight = ROUTE_SCALE * chosen / chosen_total

    told = jnp.concatenate(
        [
            own_position[:, None, :],
            route_weight.T[:, None, :],
            jnp.broadcast_to(inv_rms.reshape(1, 1, tok_rows), (EXPERTS, 1, tok_rows)),
        ],
        axis=1,
    )
    told = lax.all_to_all(told, "ep", split_axis=0, concat_axis=0, tiled=True)
    told_path = jnp.dot(to_path, told.reshape(EXPERTS, 3 * tok_rows), precision=HIGHEST)
    told_path = told_path.reshape(GROUPS, SIDE, 3, tok_rows)
    position = told_path[:, :, 0].astype(jnp.int32)
    offset = (CAP * jnp.arange(SIDE, dtype=jnp.int32))[None, :, None]
    slot = jnp.where(position >= 0, position + offset, -1).reshape(GROUPS, 1, SIDE * tok_rows)
    own_told = told_path.reshape(2, SIDE, SIDE, 3, tok_rows)
    own_told = lax.dynamic_index_in_dim(own_told, tp, 1, keepdims=False)
    own_weight = own_told[:, :, 1].reshape(2, 1, SIDE * tok_rows)
    own_inv = own_told[:, :, 2].reshape(2, 1, SIDE * tok_rows)

    in_chunks, grad_chunks = path_gather([hidden_in, out_grad], told)

    s_line = jnp.arange(2, dtype=jnp.int32)[None, :]
    j_line = jnp.arange(SIDE, dtype=jnp.int32)
    j_col = j_line[:, None]
    return_expert = jnp.where(
        core == 0,
        (z * SIDE + (y + j_col) % SIDE) * 2 + s_line,
        (((z + j_col) % SIDE) * SIDE + y) * 2 + 1 - s_line,
    ).reshape(-1)
    pick_expert = (
        return_expert[:, None] == jnp.arange(EXPERTS, dtype=jnp.int32)[None, :]
    ).astype(F32)
    line_position, *unused = lax.optimization_barrier((own_position, *grad_chunks[1:SIDE]))
    line_position = jnp.stack(
        [line_position]
        + [lax.ppermute(line_position, "ep", first_hop(k)) for k in range(1, SIDE)]
    )
    position_here = jnp.einsum(
        "ket,me->ktm", line_position, pick_expert, precision=HIGHEST
    ).astype(jnp.int32)
    return_slot = jnp.where(
        position_here >= 0, position_here + (CAP * j_line)[:, None, None], -1
    ).reshape(SIDE * tok_rows, GROUPS)

    own, other = slice(0, SIDE), slice(SIDE, GROUPS)
    halves = (own, other)
    rows_in, both_terms, rows_grad, cot_terms = [], [], [], []
    for half in halves:
        rows, part = rows_through_in(slot[half], gain, w_gate, w_up, in_chunks[half])
        rows_in.append(rows)
        both_terms.append(tp_exchange(part))
    turn = (jnp.arange(SIDE, dtype=jnp.int32) + tp) % SIDE
    for half in halves:
        rows, parts = rows_through_down(turn, slot[half], w_down, grad_chunks[half])
        rows_grad.append(rows)
        cot_terms.append(tp_terms(parts))
    hidden_part = parts[0]
    own_slot = jnp.stack(
        [lax.dynamic_index_in_dim(slot[half], tp, 0, keepdims=False) for half in halves]
    )
    own_hit = jnp.arange(ROWS, dtype=jnp.int32)[None, :, None] == own_slot
    row_scales = jnp.concatenate(
        [
            jnp.sum(jnp.where(own_hit, value, 0.0), axis=2, keepdims=True)
            for value in (own_weight, own_inv)
        ],
        axis=2,
    )
    cot_terms[0], unused = lax.optimization_barrier((cot_terms[0], hidden_part))
    both_cots, hiddens, row_cots, row_inners = [], (), [], []
    for n in range(2):
        both_cot, hidden, row_cot, row_inner = act(
            row_scales[n], both_terms[n], cot_terms[n], *hiddens
        )
        both_cots.append(tp_gather(both_cot))
        hiddens = (hidden,)
        row_cots.append(row_cot)
        row_inners.append(row_inner)
    back, ordered_cots = [], []
    turn, return_slot = lax.optimization_barrier((turn, return_slot))
    for n in range(2):
        ordered, rows = back_rows_of(turn, w_gate, w_up, both_cots[n])
        ordered_cots.append(ordered)
        back.extend(rows)

    returned = []
    for j in range(SIDE):
        returned.append(back[j] if j == 0 else lax.ppermute(back[j], "ep", second_hop(-j)))
        returned.append(lax.ppermute(back[SIDE + j], "ep", swap_second_hop(-j)))
    summed = combine(return_slot, returned)
    routed_cot = summed[0].astype(F32)
    for k in range(1, SIDE):
        routed_cot = routed_cot + lax.ppermute(summed[k], "ep", first_hop(-k)).astype(F32)

    units = shared_down.shape[0]
    shared_in = (jnp.concatenate([shared_gate.T, shared_up.T], axis=0).astype(F32) * gain).astype(
        BF16
    )
    shared_out = jnp.concatenate([shared_down, jnp.zeros((8, quarter), BF16)], axis=0)
    late_in, late_grad, unused = lax.optimization_barrier((in_chunks, grad_chunks, row_cots))
    parts = shared_partials(shared_in, shared_out, late_in, late_grad)
    inner = parts.shape[2]
    shared_sum = tp_scatter(parts)
    gate_s = shared_sum[:, :units] * own_inv
    up_s = shared_sum[:, units : 2 * units] * own_inv
    hid_cot_s = shared_sum[:, 2 * units : 3 * units]
    gate_cot_s, up_cot_s = gate_grads(hid_cot_s, gate_s, up_s)

    def to_tokens(row_values):
        return jnp.sum(jnp.where(own_hit, jnp.stack(row_values), 0.0), axis=1, keepdims=True)

    shared_inner = jnp.sum(gate_cot_s * gate_s + up_cot_s * up_s, axis=1, keepdims=True)
    cots = jnp.concatenate(
        [
            gate_cot_s * own_inv,
            up_cot_s * own_inv,
            gate_s * jax.nn.sigmoid(gate_s) * up_s,
            to_tokens(row_cots),
            to_tokens(row_inners) + shared_inner,
            jnp.zeros((2, inner - 3 * units - 2, SIDE * tok_rows), F32),
        ],
        axis=1,
    ).astype(BF16)
    cots_all = tp_exchange(jnp.broadcast_to(cots[None], (SIDE,) + cots.shape))
    to_owner = by_owner(block_of, cots_all)
    to_owner = lax.all_to_all(to_owner, "ep", split_axis=0, concat_axis=0, tiled=True)
    shared_late, unused = lax.optimization_barrier((shared_in, hidden_part))
    shared_whole = lax.all_gather(shared_late, "ep", axis=0, tiled=True)
    shared_scaled = lax.dot_general(
        to_owner[:, : 2 * units].reshape(-1, tok_rows),
        shared_whole,
        (((0,), (0,)), ((), ())),
        preferred_element_type=F32,
    ) * rms

    sums = to_owner[:, 3 * units : 3 * units + 2].astype(F32)
    weight_cot = sums[:, 0].T
    chosen_cot = picks * (
        ROUTE_SCALE
        * (
            weight_cot / chosen_total
            - jnp.sum(weight_cot * chosen, axis=1, keepdims=True) / (chosen_total * chosen_total)
        )
    )
    logit_cot = chosen_cot * scores * (1.0 - scores)
    router_part = jnp.dot(logit_cot.T, normed.astype(F32), precision=HIGHEST)
    router_cot = jnp.dot(logit_cot, router_weight.T, precision=HIGHEST)
    inner_sum = jnp.sum(sums[:, 1], axis=0).reshape(tok_rows, 1) * rms + jnp.sum(
        logit_cot * plain_logits, axis=1, keepdims=True
    )

    scaled = (routed_cot * rms + router_cot) * gain + shared_scaled
    input_cot = inv_rms * scaled - wide_in * (inv_rms * inv_rms * inv_rms) * (
        inner_sum / feature_count
    )
    dense_cot = (out_grad.astype(F32) + input_cot).astype(BF16)

    (cot_chunks,) = path_gather([dense_cot])
    gate_t, up_t = dense_gate.T, dense_up.T
    hidden2 = (jax.nn.silu(gate_t.astype(F32)) * up_t.astype(F32)).astype(BF16)

    def flat(parts, columns=slice(None)):
        whole = jnp.concatenate([part[:, :, columns] for part in parts], axis=1)
        return whole.reshape(GROUPS * ROWS, -1)

    def rows_dot(left, right):
        return lax.dot_general(
            left, right, (((0,), (0,)), ((), ())), preferred_element_type=F32
        ).astype(BF16)[None]

    cots_k8, unused = lax.optimization_barrier((cots_all, back[-1]))
    grads_in, grads_down = shared_grads(cots_k8, gain, in_chunks, grad_chunks, 2 * units)
    rows_late, cots_late, unused = lax.optimization_barrier((rows_in, ordered_cots, summed))
    units_r = w_gate.shape[1]
    rows_late = flat(rows_late)
    grad_expert_gate = rows_dot(rows_late, flat(cots_late, slice(0, units_r)))
    hidden_all, unused = lax.optimization_barrier((hiddens[0], summed))
    hidden_all = tp_exchange(hidden_all).reshape(GROUPS * ROWS, -1)

    cot_own, hidden2, unused = lax.optimization_barrier(
        (cot_chunks[own], hidden2, (grads_in, grad_expert_gate, hidden_all))
    )
    dense_place = (block_z * SIDE + block_y).reshape(2, -1)
    own_part = dense_hidden(dense_place[0], dense_down, cot_own)
    own_sum = tp_scatter(own_part)
    hidden2_part = dense_hidden(dense_place[1], dense_down, cot_chunks[other])
    other_sum = tp_scatter(hidden2_part)
    cot_ready = cot_own + cot_chunks[other]

    def by_core(mine, others):
        both = jnp.where(core == 0, jnp.stack([mine, others]), jnp.stack([others, mine]))
        both = both.reshape(2, mine.shape[0], SIDE, tok_rows).transpose(1, 2, 0, 3)
        return both.reshape(mine.shape[0], -1)

    hidden2_cot = by_core(own_sum, other_sum)
    share = 8 * tok_rows
    gate_mine = lax.dynamic_slice_in_dim(gate_t, tp * share, share, 1).astype(F32)
    up_mine = lax.dynamic_slice_in_dim(up_t, tp * share, share, 1).astype(F32)
    grad_gate2, grad_up2 = gate_grads(hidden2_cot, gate_mine, up_mine)
    grad_dense_down = dense_grad(block_of, hidden2, cot_ready)
    grad_router = ep_sum(
        router_part, (summed, dense_cot, cot_chunks[0], own_part, hidden2_part)
    ).T
    rows_last, cots_last, rows_grad, unused = lax.optimization_barrier(
        (rows_late, cots_late, rows_grad, hidden2_part)
    )

    return (
        grad_gate2.astype(BF16).T,
        grad_up2.astype(BF16).T,
        grad_dense_down,
        grad_expert_gate,
        rows_dot(rows_last, flat(cots_last, slice(units_r, None))),
        rows_dot(hidden_all, flat(rows_grad)),
        grads_in[:units].T,
        grads_in[units:].T,
        grads_down[:units],
        grad_router,
    )


def solution(mesh):
    in_specs = (
        P("ep", "tp"),
        P("ep", "tp"),
        P("tp"),
        P("tp", None),
        P("ep", None),
        P("ep", "tp", None),
        P("ep", "tp", None),
        P("ep", None, "tp"),
        P("tp", "ep"),
        P("tp", "ep"),
        P("ep", "tp"),
        P(None, "ep"),
        P(None, "ep"),
        P("ep", "tp"),
    )
    out_specs = (
        P("tp", "ep"),
        P("tp", "ep"),
        P("ep", "tp"),
        P("ep", "tp", None),
        P("ep", "tp", None),
        P("ep", None, "tp"),
        P("tp", "ep"),
        P("tp", "ep"),
        P("ep", "tp"),
        P("tp", None),
    )
    return jax.shard_map(local, mesh=mesh, in_specs=in_specs, out_specs=out_specs, check_vma=False)
```

```python
import functools

import jax
import jax.numpy as jnp
from jax import lax
from jax.experimental import pallas as pl
from jax.experimental.pallas import tpu as pltpu
from jax.sharding import PartitionSpec as P

EXPERTS = 32
TOP = 8
CAP = 36
SIDE = 4
GROUPS = 8
ROWS = SIDE * CAP

EPSILON = 1e-05
ROUTE_SCALE = 2.5
F32 = jnp.float32
BF16 = jnp.bfloat16
HIGHEST = lax.Precision.HIGHEST
VMEM_BYTES = 50 * 1024 * 1024


def ep_at(z, y, core):
    return ((z % SIDE) * SIDE + y % SIDE) * 2 + core


def ep_pairs(target):
    return [
        (ep_at(z, y, core), target(z, y, core))
        for z in range(SIDE)
        for y in range(SIDE)
        for core in range(2)
    ]


def first_hop(k):
    return ep_pairs(lambda z, y, core: ep_at(z, y + k, 1) if core else ep_at(z + k, y, 0))


def first_lines():
    core_0 = [[ep_at(z, y, 0) for z in range(SIDE)] for y in range(SIDE)]
    return core_0 + [[ep_at(z, y, 1) for y in range(SIDE)] for z in range(SIDE)]


def second_hop(k):
    return ep_pairs(lambda z, y, core: ep_at(z + k, y, 1) if core else ep_at(z, y + k, 0))


def swap_second_hop(k):
    return ep_pairs(lambda z, y, core: ep_at(z, y + k, 0) if core else ep_at(z + k, y, 1))


def core_swap():
    return ep_pairs(lambda z, y, core: ep_at(z, y, 1 - core))


def tp_hop(k):
    return [(i, (i + k) % SIDE) for i in range(SIDE)]


def join_kernel(first, count, *refs):
    blocks, out = refs[:SIDE], refs[SIDE]
    rows = out.shape[0] // SIDE
    for i in range(SIDE):
        out[i * rows : (i + 1) * rows] = blocks[i][first : first + rows]


def join(blocks, number, count, after):
    rows, width = blocks[0].shape[0] // count, blocks[0].shape[1]
    return local_call(
        functools.partial(join_kernel, number * rows, count),
        jax.ShapeDtypeStruct((SIDE * rows, width), blocks[0].dtype),
        vmem(SIDE),
        0,
        4 * SIDE * rows * width,
        after=after,
    )(*blocks)


def first_gather(blocks):
    stack = jnp.concatenate(blocks, axis=0) if len(blocks) > 1 else blocks[0]
    return [stack] + [lax.ppermute(stack, "ep", first_hop(k)) for k in range(1, SIDE)]


def second_gather(first, number, count, after):
    joined = join(first, number, count, after)
    own = [joined] + [lax.ppermute(joined, "ep", second_hop(k)) for k in range(1, SIDE)]
    return own + [lax.ppermute(chunk, "ep", core_swap()) for chunk in own]


def add_kernel(first, second, out):
    out[...] = first[...] + second[...]


def ep_sum(value, stages):
    pairings = ((0, 0, 1), (0, 1, 0), (1, 0, 0), (0, 2, 0), (2, 0, 0))
    shape = jax.ShapeDtypeStruct(value.shape, value.dtype)
    for (dz, dy, dcore), stage in zip(pairings, stages, strict=True):
        pairs = ep_pairs(lambda z, y, core: ep_at(z ^ dz, y ^ dy, core ^ dcore))
        met = lax.ppermute(value, "ep", pairs)
        value = local_call(add_kernel, shape, vmem(2), 0, 12 * value.size, after=[stage])(
            value, met
        )
    return value


def tp_gather(piece):
    return [piece] + [lax.ppermute(piece, "tp", tp_hop(-k)) for k in (1, 2, 3)]


def tp_terms(parts):
    return [parts[0]] + [lax.ppermute(parts[k], "tp", tp_hop(k)) for k in (1, 3, 2)]


def tp_exchange(parts):
    return lax.all_to_all(parts, "tp", split_axis=0, concat_axis=0, tiled=True)


def tp_scatter(parts):
    return jnp.sum(tp_exchange(parts).astype(F32), axis=0)


def vmem(count):
    return [pl.BlockSpec(memory_space=pltpu.VMEM)] * count


def smem():
    return pl.BlockSpec(memory_space=pltpu.SMEM)


def local_call(body, out_shape, in_specs, flops, moved, scratch=(), after=()):
    many = isinstance(out_shape, (list, tuple))
    count = len(in_specs)

    def ordered(*refs):
        body(*refs[:count], *refs[count + len(after) :])

    call = pl.pallas_call(
        ordered,
        out_shape=out_shape,
        in_specs=list(in_specs) + [pl.BlockSpec(memory_space=pl.ANY)] * len(after),
        out_specs=vmem(len(out_shape)) if many else vmem(1)[0],
        scratch_shapes=list(scratch),
        cost_estimate=pl.CostEstimate(flops=flops, bytes_accessed=moved, transcendentals=0),
        compiler_params=pltpu.CompilerParams(vmem_limit_bytes=VMEM_BYTES),
    )
    return lambda *operands: call(*operands, *after)


def held_kernel(value, out):
    out[...] = value[...]


def held(value, after):
    shape = jax.ShapeDtypeStruct(value.shape, value.dtype)
    moved = 2 * value.size * value.dtype.itemsize
    return local_call(held_kernel, shape, vmem(1), 0, moved, after=after)(value)


def nt_dot(left, right):
    return lax.dot_general(left, right, (((1,), (1,)), ((), ())), preferred_element_type=F32)


def pick_rows(slot, chunk, gain=None):
    hit = lax.broadcasted_iota(jnp.int32, (ROWS, chunk.shape[0]), 0) == slot
    pick = jnp.where(hit, 1.0, 0.0).astype(BF16)
    rows = jnp.dot(pick, chunk[...], preferred_element_type=F32)
    return (rows if gain is None else rows * gain).astype(BF16)


def store_groups(out, columns, value):
    for k in range(SIDE):
        out[k, :, columns] = value[k * ROWS : (k + 1) * ROWS].astype(BF16)


TILE = 256


def in_kernel(slot, gain, w_gate, w_up, *refs):
    chunks, (rows, both) = refs[:SIDE], refs[SIDE:]
    for k in range(SIDE):
        rows[k] = pick_rows(slot[k], chunks[k], gain[...])
    units = w_gate.shape[1]

    def step(n, unused):
        left = rows[...].reshape(SIDE * ROWS, -1)
        for at, weights in ((0, w_gate), (units, w_up)):
            columns = pl.ds(pl.multiple_of(n * TILE, TILE), TILE)
            target = pl.ds(pl.multiple_of(at + n * TILE, TILE), TILE)
            value = jnp.dot(left, weights[:, columns], preferred_element_type=F32)
            store_groups(both, target, value)
        return unused

    lax.fori_loop(0, units // TILE, step, 0)


def rows_through_in(slot, gain, w_gate, w_up, chunks, after=()):
    tokens, width = chunks[0].shape
    units = w_gate.shape[1]
    return local_call(
        in_kernel,
        [
            jax.ShapeDtypeStruct((SIDE, ROWS, width), BF16),
            jax.ShapeDtypeStruct((SIDE, ROWS, 2 * units), BF16),
        ],
        vmem(4 + SIDE),
        2 * SIDE * ROWS * width * (tokens + 2 * units),
        2 * width * (SIDE * (tokens + ROWS) + 2 * units),
        after=after,
    )(slot, gain, w_gate, w_up, *chunks)


def grad_kernel(place, slot, w_down, *refs):
    chunks, rows, parts = refs[:SIDE], refs[SIDE], refs[SIDE + 1 :]
    for k in range(SIDE):
        rows[k] = pick_rows(slot[k], chunks[k])

    def step(n, unused):
        left = jnp.concatenate([rows[place[k]] for k in range(SIDE)], axis=0)
        columns = pl.ds(pl.multiple_of(n * TILE, TILE), TILE)
        value = nt_dot(left, w_down[columns, :]).astype(BF16)
        for k in range(SIDE):
            parts[k][:, columns] = value[k * ROWS : (k + 1) * ROWS]
        return unused

    lax.fori_loop(0, w_down.shape[0] // TILE, step, 0)


def rows_through_down(place, slot, w_down, chunks, after=()):
    tokens, width = chunks[0].shape
    units = w_down.shape[0]
    rows, *parts = local_call(
        grad_kernel,
        [jax.ShapeDtypeStruct((SIDE, ROWS, width), BF16)]
        + [jax.ShapeDtypeStruct((ROWS, units), BF16)] * SIDE,
        [smem()] + vmem(2 + SIDE),
        2 * SIDE * ROWS * width * (tokens + units),
        2 * width * (SIDE * (tokens + ROWS) + units),
        after=after,
    )(place, slot, w_down, *chunks)
    return rows, parts


def back_kernel(place, w_gate, w_up, *refs):
    pieces, cots, out = refs[:SIDE], refs[SIDE], refs[SIDE + 1 :]
    units = w_gate.shape[1]
    for k in range(SIDE):
        cots[place[k]] = pieces[k][...]

    def step(n, unused):
        columns = pl.ds(pl.multiple_of(n * TILE, TILE), TILE)
        left = cots[...].reshape(SIDE * ROWS, 2 * units)
        rows = nt_dot(left[:, :units], w_gate[columns, :])
        rows = (rows + nt_dot(left[:, units:], w_up[columns, :])).astype(BF16)
        for k in range(SIDE):
            out[k][:, columns] = rows[k * ROWS : (k + 1) * ROWS]
        return unused

    lax.fori_loop(0, w_gate.shape[0] // TILE, step, 0)


def back_rows_of(place, w_gate, w_up, pieces, after):
    width, units = w_gate.shape
    cots, *back = local_call(
        back_kernel,
        [jax.ShapeDtypeStruct((SIDE, ROWS, 2 * units), BF16)]
        + [jax.ShapeDtypeStruct((ROWS, width), BF16)] * SIDE,
        [smem()] + vmem(2 + SIDE),
        4 * SIDE * ROWS * units * width,
        2 * (2 * SIDE * ROWS * units + 2 * units * width + SIDE * ROWS * width),
        after=after,
    )(place, w_gate, w_up, *pieces)
    return cots, back


def act_kernel(scales, gate_ups, *refs):
    cots, hidden_before = refs[:SIDE], refs[SIDE:-4]
    cot_out, hidden_out, row_cot, row_inner = refs[-4:]
    tile = 48
    count, width = cots[0].shape

    def step(n, unused):
        rows = pl.ds(pl.multiple_of(n * tile, tile), tile)

        def total(columns):
            return sum(gate_ups[k, rows, columns].astype(F32) for k in range(SIDE))

        weight, inv = scales[rows, 0:1], scales[rows, 1:2]
        gate = total(slice(0, width)) * inv
        up = total(slice(width, 2 * width)) * inv
        cot = sum(term[rows, :].astype(F32) for term in cots)
        sigma = 1.0 / (1.0 + jnp.exp(-gate))
        silu = gate * sigma
        hidden = silu * up
        row_cot[rows, :] = jnp.sum(cot * hidden, axis=1, keepdims=True)
        cot = cot * weight
        gate_cot = cot * up * (sigma + silu * (1.0 - sigma))
        up_cot = cot * silu
        row_inner[rows, :] = jnp.sum(gate_cot * gate + up_cot * up, axis=1, keepdims=True)
        cot_out[rows, :width] = (gate_cot * inv).astype(BF16)
        cot_out[rows, width:] = (up_cot * inv).astype(BF16)
        hidden = (hidden * weight).astype(BF16)
        if hidden_before:
            later = pl.ds(pl.multiple_of(count + n * tile, 16), tile)
            for k in range(SIDE):
                hidden_out[k, rows, :] = hidden_before[0][rows, :]
                hidden_out[k, later, :] = hidden
        else:
            hidden_out[rows, :] = hidden
        return unused

    lax.fori_loop(0, scales.shape[0] // tile, step, 0)


def act(scales, gate_ups, cots, *hidden_before, after):
    rows, hidden = cots[0].shape
    hidden_shape = (SIDE, 2 * rows, hidden) if hidden_before else (rows, hidden)
    return local_call(
        act_kernel,
        [
            jax.ShapeDtypeStruct((rows, 2 * hidden), BF16),
            jax.ShapeDtypeStruct(hidden_shape, BF16),
        ]
        + [jax.ShapeDtypeStruct((rows, 1), F32)] * 2,
        vmem(2 + SIDE + len(hidden_before)),
        40 * rows * hidden,
        48 * rows * hidden,
        after=after,
    )(scales, gate_ups, *cots, *hidden_before)


def combine_kernel(slots, *refs):
    rows, out, pick = refs[:GROUPS], refs[GROUPS:-1], refs[-1]
    tokens = slots.shape[0]
    block = tokens // SIDE
    for m in range(GROUPS):
        hit = lax.broadcasted_iota(jnp.int32, (tokens, ROWS), 1) == slots[:, m : m + 1]
        pick[m] = jnp.where(hit, 1.0, 0.0).astype(BF16)

    def step(n, unused):
        columns = pl.ds(pl.multiple_of(n * TILE, TILE), TILE)
        total = jnp.dot(pick[0], rows[0][:, columns], preferred_element_type=F32)
        for m in range(1, GROUPS):
            total = total + jnp.dot(pick[m], rows[m][:, columns], preferred_element_type=F32)
        total = total.astype(BF16)
        for k in range(SIDE):
            out[k][:, columns] = total[k * block : (k + 1) * block]
        return unused

    lax.fori_loop(0, rows[0].shape[1] // TILE, step, 0)


def combine(slots, rows):
    tokens, width = slots.shape[0], rows[0].shape[1]
    return local_call(
        combine_kernel,
        [jax.ShapeDtypeStruct((tokens // SIDE, width), BF16)] * SIDE,
        vmem(1 + GROUPS),
        2 * GROUPS * ROWS * tokens * width,
        2 * (GROUPS * ROWS + tokens) * width,
        [pltpu.VMEM((GROUPS, tokens, ROWS), BF16)],
    )(slots, *rows)


def shared_kernel(w_in, w_out, *refs):
    ins, grads, out = refs[:GROUPS], refs[GROUPS : 2 * GROUPS], refs[2 * GROUPS]
    top = w_in.shape[0]
    for g in range(GROUPS):
        out[g % SIDE, g // SIDE, :top] = nt_dot(w_in[...], ins[g][...]).astype(BF16)
        out[g % SIDE, g // SIDE, top:] = nt_dot(w_out[...], grads[g][...]).astype(BF16)


def shared_partials(w_in, w_out, ins, grads, after):
    tokens, width = ins[0].shape
    hidden = w_in.shape[0] + w_out.shape[0]
    return local_call(
        shared_kernel,
        jax.ShapeDtypeStruct((SIDE, 2, hidden, tokens), BF16),
        vmem(2 + 2 * GROUPS),
        2 * GROUPS * tokens * width * hidden,
        4 * GROUPS * tokens * width,
        after=after,
    )(w_in, w_out, *ins, *grads)


def shared_grad_kernel(cots, gain, *refs):
    ins, grads = refs[:GROUPS], refs[GROUPS : 2 * GROUPS]
    out_in, out_down, sum_in, sum_down = refs[2 * GROUPS :]
    top = out_in.shape[0]
    for g in range(GROUPS):
        cot = cots[g % SIDE, g // SIDE]
        first = jnp.dot(cot[:top], ins[g][...], preferred_element_type=F32)
        second = jnp.dot(cot[top:], grads[g][...], preferred_element_type=F32)
        sum_in[...] = first if g == 0 else sum_in[...] + first
        sum_down[...] = second if g == 0 else sum_down[...] + second
    out_in[...] = (sum_in[...] * gain[...]).astype(BF16)
    out_down[...] = sum_down[...].astype(BF16)


def shared_grads(cots, gain, ins, grads, top, after):
    tokens, width = ins[0].shape
    rest = cots.shape[2] - top
    return local_call(
        shared_grad_kernel,
        [jax.ShapeDtypeStruct((top, width), BF16), jax.ShapeDtypeStruct((rest, width), BF16)],
        vmem(2 + 2 * GROUPS),
        2 * GROUPS * tokens * width * (top + rest),
        4 * GROUPS * tokens * width,
        [pltpu.VMEM((top, width), F32), pltpu.VMEM((rest, width), F32)],
        after,
    )(cots, gain, *ins, *grads)


def owner_kernel(place, cots, out):
    block = out.shape[2]
    for g in range(GROUPS):
        for i in range(SIDE):
            out[place[g * SIDE + i]] = cots[g % SIDE, g // SIDE, :, i * block : (i + 1) * block]


def by_owner(place, cots):
    rows, tokens = cots.shape[2:]
    return local_call(
        owner_kernel,
        jax.ShapeDtypeStruct((GROUPS * SIDE, rows, tokens // SIDE), BF16),
        [smem()] + vmem(1),
        0,
        4 * GROUPS * rows * tokens,
    )(place, cots)


def dense_hidden_kernel(place, w_down, *refs):
    chunks, out = refs[:SIDE], refs[SIDE]
    block = chunks[0].shape[0] // SIDE
    for g in range(SIDE):
        columns = nt_dot(w_down[...], chunks[g][...]).astype(BF16)
        for i in range(SIDE):
            at = place[g * SIDE + i]
            lane = pl.multiple_of(lax.rem(at, SIDE) * block, block)
            out[lax.div(at, SIDE), :, pl.ds(lane, block)] = columns[
                :, i * block : (i + 1) * block
            ]


def dense_hidden(place, w_down, chunks, after=()):
    tokens, width = chunks[0].shape
    hidden = w_down.shape[0]
    return local_call(
        dense_hidden_kernel,
        jax.ShapeDtypeStruct((SIDE, hidden, tokens), BF16),
        [smem()] + vmem(1 + SIDE),
        2 * SIDE * tokens * width * hidden,
        2 * SIDE * tokens * width,
        after=after,
    )(place, w_down, *chunks)


def dense_grad_kernel(place, hidden, *refs):
    chunks, out, total = refs[:GROUPS], refs[GROUPS], refs[GROUPS + 1]
    block = chunks[0].shape[0] // SIDE
    for g in range(GROUPS):
        left = jnp.concatenate(
            [
                hidden[:, pl.ds(pl.multiple_of(place[g * SIDE + i] * block, block), block)]
                for i in range(SIDE)
            ],
            axis=1,
        )
        term = jnp.dot(left, chunks[g][...], preferred_element_type=F32)
        total[...] = term if g == 0 else total[...] + term
    out[...] = total[...].astype(BF16)


def dense_grad(place, hidden, chunks, after):
    tokens, width = chunks[0].shape
    units = hidden.shape[0]
    return local_call(
        dense_grad_kernel,
        jax.ShapeDtypeStruct((units, width), BF16),
        [smem()] + vmem(1 + GROUPS),
        2 * GROUPS * tokens * width * units,
        2 * GROUPS * tokens * width,
        [pltpu.VMEM((units, width), F32)],
        after,
    )(place, hidden, *chunks)


def gate_grads(hidden_cot, gate_value, up_value):
    sigma = jax.nn.sigmoid(gate_value)
    gate_cot = hidden_cot * up_value * sigma * (1.0 + gate_value * (1.0 - sigma))
    up_cot = hidden_cot * gate_value * sigma
    return (gate_cot, up_cot)


def local(
    hidden_in,
    out_grad,
    norm_gain,
    router_weight,
    route_ids,
    expert_gate,
    expert_up,
    expert_down,
    shared_gate,
    shared_up,
    shared_down,
    dense_gate,
    dense_up,
    dense_down,
):
    tok_rows, quarter = hidden_in.shape
    feature_count = quarter * lax.axis_size("tp")
    ep, tp = lax.axis_index("ep"), lax.axis_index("tp")
    z, y, core = ep // 8, (ep // 2) % SIDE, ep % 2
    w_gate, w_up, w_down = expert_gate[0], expert_up[0], expert_down[0]
    gain = norm_gain[None, :]

    g_at = jnp.arange(GROUPS, dtype=jnp.int32)[:, None]
    i_at = jnp.arange(SIDE, dtype=jnp.int32)[None, :]
    j_at = g_at % SIDE
    block_core = (core + g_at // SIDE) % 2
    block_z = jnp.where(block_core == 0, z - i_at, z - j_at) % SIDE
    block_y = jnp.where(block_core == 0, y - j_at, y - i_at) % SIDE
    block_of = ((block_z * SIDE + block_y) * 2 + block_core).reshape(-1)
    to_path = (block_of[:, None] == jnp.arange(EXPERTS, dtype=jnp.int32)[None, :]).astype(F32)

    picks = jnp.any(
        route_ids[:, :, None] == jnp.arange(EXPERTS, dtype=jnp.int32)[None, None, :], axis=1
    ).astype(F32)
    token_line = jnp.arange(tok_rows, dtype=jnp.int32)
    earlier = (token_line[:, None] < token_line[None, :]).astype(F32)
    own_position = jnp.dot(picks.T, earlier, precision=HIGHEST)
    own_position = jnp.where(picks.T > 0.0, own_position, -1.0)
    wide_in = hidden_in.astype(F32)
    square_part = jnp.sum(wide_in * wide_in, axis=1, keepdims=True)
    logit_part = jnp.dot(wide_in * gain, router_weight, precision=HIGHEST)
    stats = jnp.concatenate([logit_part, square_part], axis=1)
    stats = tp_scatter(jnp.broadcast_to(stats[None], (SIDE,) + stats.shape))
    plain_logits = stats[:, :EXPERTS]
    mean_square = stats[:, EXPERTS:] / feature_count + EPSILON
    inv_rms = lax.rsqrt(mean_square)
    rms = mean_square * inv_rms
    normed = (wide_in * inv_rms * gain).astype(BF16)
    scores = jax.nn.sigmoid(plain_logits * inv_rms)
    chosen = picks * scores
    chosen_total = jnp.sum(chosen, axis=1, keepdims=True)
    route_weight = ROUTE_SCALE * chosen / chosen_total

    told = jnp.concatenate(
        [
            own_position[:, None, :],
            route_weight.T[:, None, :],
            jnp.broadcast_to(inv_rms.reshape(1, 1, tok_rows), (EXPERTS, 1, tok_rows)),
        ],
        axis=1,
    )
    told = lax.all_to_all(told, "ep", split_axis=0, concat_axis=0, tiled=True)
    told_path = jnp.dot(to_path, told.reshape(EXPERTS, 3 * tok_rows), precision=HIGHEST)
    told_path = told_path.reshape(GROUPS, SIDE, 3, tok_rows)
    position = told_path[:, :, 0].astype(jnp.int32)
    offset = (CAP * jnp.arange(SIDE, dtype=jnp.int32))[None, :, None]
    slot = jnp.where(position >= 0, position + offset, -1).reshape(GROUPS, 1, SIDE * tok_rows)
    own_told = told_path.reshape(2, SIDE, SIDE, 3, tok_rows)
    own_told = lax.dynamic_index_in_dim(own_told, tp, 1, keepdims=False)
    own_weight = own_told[:, :, 1].reshape(2, 1, SIDE * tok_rows)
    own_inv = own_told[:, :, 2].reshape(2, 1, SIDE * tok_rows)

    first = first_gather([hidden_in, out_grad])
    in_chunks = second_gather(first, 0, 2, [told])

    own, other = slice(0, SIDE), slice(SIDE, GROUPS)
    halves = (own, other)
    turn = (jnp.arange(SIDE, dtype=jnp.int32) + tp) % SIDE
    rows_in, both_terms, rows_grad, cot_terms = [], [], [], []
    for half in halves:
        rows, part = rows_through_in(
            slot[half], gain, w_gate, w_up, in_chunks[half], both_terms[:1]
        )
        rows_in.append(rows)
        both_terms.append(tp_exchange(part))
        if half is own:
            grad_chunks = second_gather(first, 1, 2, [part, in_chunks[-1]])
    before = [part]
    for half in halves:
        rows, parts = rows_through_down(turn, slot[half], w_down, grad_chunks[half], before)
        rows_grad.append(rows)
        cot_terms.append(tp_terms(parts))
        before = [parts[0], both_terms[1]]
    hidden_part = parts[0]

    units = shared_down.shape[0]
    shared_in = (jnp.concatenate([shared_gate.T, shared_up.T], axis=0).astype(F32) * gain).astype(
        BF16
    )
    shared_out = jnp.concatenate([shared_down, jnp.zeros((8, quarter), BF16)], axis=0)
    shared_parts = shared_partials(
        shared_in, shared_out, in_chunks, grad_chunks, [hidden_part]
    )
    own_slot = jnp.stack(
        [lax.dynamic_index_in_dim(slot[half], tp, 0, keepdims=False) for half in halves]
    )
    own_hit = jnp.arange(ROWS, dtype=jnp.int32)[None, :, None] == own_slot
    row_scales = jnp.concatenate(
        [
            jnp.sum(jnp.where(own_hit, value, 0.0), axis=2, keepdims=True)
            for value in (own_weight, own_inv)
        ],
        axis=2,
    )
    both_cots, hiddens, row_cots, row_inners = [], (), [], []
    for n in range(2):
        both_cot, hidden, row_cot, row_inner = act(
            row_scales[n], both_terms[n], cot_terms[n], *hiddens, after=[shared_parts]
        )
        both_cots.append(tp_gather(both_cot))
        hiddens = (hidden,)
        row_cots.append(row_cot)
        row_inners.append(row_inner)
    s_line = jnp.arange(2, dtype=jnp.int32)[None, :]
    j_line = jnp.arange(SIDE, dtype=jnp.int32)
    j_col = j_line[:, None]
    return_expert = jnp.where(
        core == 0,
        (z * SIDE + (y + j_col) % SIDE) * 2 + s_line,
        (((z + j_col) % SIDE) * SIDE + y) * 2 + 1 - s_line,
    ).reshape(-1)
    pick_expert = (
        return_expert[:, None] == jnp.arange(EXPERTS, dtype=jnp.int32)[None, :]
    ).astype(F32)
    line_position = held(own_position, [hidden_part])
    line_position = jnp.stack(
        [line_position]
        + [lax.ppermute(line_position, "ep", first_hop(k)) for k in range(1, SIDE)]
    )
    position_here = jnp.einsum(
        "ket,me->ktm", line_position, pick_expert, precision=HIGHEST
    ).astype(jnp.int32)
    return_slot = jnp.where(
        position_here >= 0, position_here + (CAP * j_line)[:, None, None], -1
    ).reshape(SIDE * tok_rows, GROUPS)

    back, ordered_cots = [], []
    for n, before in ((0, row_cot), (1, return_slot)):
        ordered, rows = back_rows_of(turn, w_gate, w_up, both_cots[n], [before])
        ordered_cots.append(ordered)
        back.extend(rows)

    returned = []
    for j in range(SIDE):
        returned.append(back[j] if j == 0 else lax.ppermute(back[j], "ep", second_hop(-j)))
        returned.append(lax.ppermute(back[SIDE + j], "ep", swap_second_hop(-j)))
    summed = combine(return_slot, returned)
    routed_cot = summed[0].astype(F32)
    for k in range(1, SIDE):
        routed_cot = routed_cot + lax.ppermute(summed[k], "ep", first_hop(-k)).astype(F32)

    inner = shared_parts.shape[2]
    shared_sum = tp_scatter(shared_parts)
    gate_s = shared_sum[:, :units] * own_inv
    up_s = shared_sum[:, units : 2 * units] * own_inv
    hid_cot_s = shared_sum[:, 2 * units : 3 * units]
    gate_cot_s, up_cot_s = gate_grads(hid_cot_s, gate_s, up_s)

    def to_tokens(row_values):
        return jnp.sum(jnp.where(own_hit, jnp.stack(row_values), 0.0), axis=1, keepdims=True)

    shared_inner = jnp.sum(gate_cot_s * gate_s + up_cot_s * up_s, axis=1, keepdims=True)
    cots = jnp.concatenate(
        [
            gate_cot_s * own_inv,
            up_cot_s * own_inv,
            gate_s * jax.nn.sigmoid(gate_s) * up_s,
            to_tokens(row_cots),
            to_tokens(row_inners) + shared_inner,
            jnp.zeros((2, inner - 3 * units - 2, SIDE * tok_rows), F32),
        ],
        axis=1,
    ).astype(BF16)
    cots_all = tp_exchange(jnp.broadcast_to(cots[None], (SIDE,) + cots.shape))
    to_owner = by_owner(block_of, cots_all)
    to_owner = lax.all_to_all(to_owner, "ep", split_axis=0, concat_axis=0, tiled=True)
    shared_whole = lax.all_gather(
        held(shared_in, [hidden_part]), "ep", axis=0, tiled=True
    )
    shared_scaled = lax.dot_general(
        to_owner[:, : 2 * units].reshape(-1, tok_rows),
        shared_whole,
        (((0,), (0,)), ((), ())),
        preferred_element_type=F32,
    ) * rms

    sums = to_owner[:, 3 * units : 3 * units + 2].astype(F32)
    weight_cot = sums[:, 0].T
    chosen_cot = picks * (
        ROUTE_SCALE
        * (
            weight_cot / chosen_total
            - jnp.sum(weight_cot * chosen, axis=1, keepdims=True) / (chosen_total * chosen_total)
        )
    )
    logit_cot = chosen_cot * scores * (1.0 - scores)
    router_part = jnp.dot(logit_cot.T, normed.astype(F32), precision=HIGHEST)
    router_cot = jnp.dot(logit_cot, router_weight.T, precision=HIGHEST)
    inner_sum = jnp.sum(sums[:, 1], axis=0).reshape(tok_rows, 1) * rms + jnp.sum(
        logit_cot * plain_logits, axis=1, keepdims=True
    )

    scaled = (routed_cot * rms + router_cot) * gain + shared_scaled
    input_cot = inv_rms * scaled - wide_in * (inv_rms * inv_rms * inv_rms) * (
        inner_sum / feature_count
    )
    dense_cot = (out_grad.astype(F32) + input_cot).astype(BF16)

    cot_chunks = second_gather(first_gather([dense_cot]), 0, 1, [])
    gate_t, up_t = dense_gate.T, dense_up.T
    hidden2 = (jax.nn.silu(gate_t.astype(F32)) * up_t.astype(F32)).astype(BF16)

    def flat(parts, columns=slice(None)):
        whole = jnp.concatenate([part[:, :, columns] for part in parts], axis=1)
        return whole.reshape(GROUPS * ROWS, -1)

    def rows_dot(left, right):
        return lax.dot_general(
            left, right, (((0,), (0,)), ((), ())), preferred_element_type=F32
        ).astype(BF16)[None]

    grads_in, grads_down = shared_grads(
        cots_all, gain, in_chunks, grad_chunks, 2 * units, [summed[0]]
    )
    units_r = w_gate.shape[1]
    rows_in = flat(rows_in)
    grad_expert_gate = rows_dot(rows_in, flat(ordered_cots, slice(0, units_r)))
    hidden_all = tp_exchange(held(hiddens[0], [to_owner])).reshape(GROUPS * ROWS, -1)

    dense_place = (block_z * SIDE + block_y).reshape(2, -1)
    own_part = dense_hidden(
        dense_place[0], dense_down, cot_chunks[own], [hidden_all]
    )
    own_sum = tp_scatter(own_part)
    turned = (((block_z - tp) % SIDE) * SIDE + block_y).reshape(2, -1)
    hidden2_part = dense_hidden(turned[1], dense_down, cot_chunks[other])
    other_sum = sum(term.astype(F32) for term in tp_terms(list(hidden2_part)))

    def by_core(mine, others):
        both = jnp.where(core == 0, jnp.stack([mine, others]), jnp.stack([others, mine]))
        both = both.reshape(2, mine.shape[0], SIDE, tok_rows).transpose(1, 2, 0, 3)
        return both.reshape(mine.shape[0], -1)

    hidden2_cot = by_core(own_sum, other_sum)
    share = 8 * tok_rows
    gate_mine = lax.dynamic_slice_in_dim(gate_t, tp * share, share, 1).astype(F32)
    up_mine = lax.dynamic_slice_in_dim(up_t, tp * share, share, 1).astype(F32)
    grad_gate2, grad_up2 = gate_grads(hidden2_cot, gate_mine, up_mine)
    grad_dense_down = dense_grad(block_of, hidden2, cot_chunks, [hidden2_part])
    grad_router = ep_sum(
        router_part, (dense_cot, own_part, hidden2_part, grad_dense_down, grad_dense_down)
    ).T
    return (
        grad_gate2.astype(BF16).T,
        grad_up2.astype(BF16).T,
        grad_dense_down,
        grad_expert_gate,
        rows_dot(rows_in, flat(ordered_cots, slice(units_r, None))),
        rows_dot(hidden_all, flat(rows_grad)),
        grads_in[:units].T,
        grads_in[units:].T,
        grads_down[:units],
        grad_router,
    )


def solution(mesh):
    in_specs = (
        P("ep", "tp"),
        P("ep", "tp"),
        P("tp"),
        P("tp", None),
        P("ep", None),
        P("ep", "tp", None),
        P("ep", "tp", None),
        P("ep", None, "tp"),
        P("tp", "ep"),
        P("tp", "ep"),
        P("ep", "tp"),
        P(None, "ep"),
        P(None, "ep"),
        P("ep", "tp"),
    )
    out_specs = (
        P("tp", "ep"),
        P("tp", "ep"),
        P("ep", "tp"),
        P("ep", "tp", None),
        P("ep", "tp", None),
        P("ep", None, "tp"),
        P("tp", "ep"),
        P("tp", "ep"),
        P("ep", "tp"),
        P("tp", None),
    )
    return jax.shard_map(local, mesh=mesh, in_specs=in_specs, out_specs=out_specs, check_vma=False)
```

```python
import functools

import jax
import jax.numpy as jnp
from jax import lax
from jax.experimental import pallas as pl
from jax.experimental.pallas import tpu as pltpu
from jax.sharding import PartitionSpec as P

EXPERTS = 32
TOP = 8
CAP = 36
SIDE = 4
GROUPS = 8
ROWS = SIDE * CAP

EPSILON = 1e-05
ROUTE_SCALE = 2.5
F32 = jnp.float32
BF16 = jnp.bfloat16
HIGHEST = lax.Precision.HIGHEST
VMEM_BYTES = 50 * 1024 * 1024


def ep_at(z, y, core):
    return ((z % SIDE) * SIDE + y % SIDE) * 2 + core


def ep_pairs(target):
    return [
        (ep_at(z, y, core), target(z, y, core))
        for z in range(SIDE)
        for y in range(SIDE)
        for core in range(2)
    ]


def first_hop(k):
    return ep_pairs(lambda z, y, core: ep_at(z, y + k, 1) if core else ep_at(z + k, y, 0))


def first_lines():
    core_0 = [[ep_at(z, y, 0) for z in range(SIDE)] for y in range(SIDE)]
    return core_0 + [[ep_at(z, y, 1) for y in range(SIDE)] for z in range(SIDE)]


def second_hop(k):
    return ep_pairs(lambda z, y, core: ep_at(z + k, y, 1) if core else ep_at(z, y + k, 0))


def swap_second_hop(k):
    return ep_pairs(lambda z, y, core: ep_at(z, y + k, 0) if core else ep_at(z + k, y, 1))


def core_swap():
    return ep_pairs(lambda z, y, core: ep_at(z, y, 1 - core))


def tp_hop(k):
    return [(i, (i + k) % SIDE) for i in range(SIDE)]


def join_kernel(first, count, *refs):
    blocks, out = refs[:SIDE], refs[SIDE]
    rows = out.shape[0] // SIDE
    for i in range(SIDE):
        out[i * rows : (i + 1) * rows] = blocks[i][first : first + rows]


def join(blocks, number, count, after):
    rows, width = blocks[0].shape[0] // count, blocks[0].shape[1]
    return local_call(
        functools.partial(join_kernel, number * rows, count),
        jax.ShapeDtypeStruct((SIDE * rows, width), blocks[0].dtype),
        vmem(SIDE),
        0,
        4 * SIDE * rows * width,
        after=after,
    )(*blocks)


def first_gather(blocks):
    stack = jnp.concatenate(blocks, axis=0) if len(blocks) > 1 else blocks[0]
    return [stack] + [lax.ppermute(stack, "ep", first_hop(k)) for k in range(1, SIDE)]


def second_gather(first, number, count, after):
    joined = join(first, number, count, after)
    own = [joined] + [lax.ppermute(joined, "ep", second_hop(k)) for k in range(1, SIDE)]
    return own + [lax.ppermute(chunk, "ep", core_swap()) for chunk in own]


def add_kernel(first, second, out):
    out[...] = first[...] + second[...]


def ep_sum(value, stages):
    pairings = ((0, 0, 1), (0, 1, 0), (1, 0, 0), (0, 2, 0), (2, 0, 0))
    shape = jax.ShapeDtypeStruct(value.shape, value.dtype)
    for (dz, dy, dcore), stage in zip(pairings, stages, strict=True):
        pairs = ep_pairs(lambda z, y, core: ep_at(z ^ dz, y ^ dy, core ^ dcore))
        met = lax.ppermute(value, "ep", pairs)
        value = local_call(add_kernel, shape, vmem(2), 0, 12 * value.size, after=[stage])(
            value, met
        )
    return value


def tp_gather(piece):
    return [piece] + [lax.ppermute(piece, "tp", tp_hop(-k)) for k in (1, 2, 3)]


def tp_terms(parts):
    return [parts[0]] + [lax.ppermute(parts[k], "tp", tp_hop(k)) for k in (1, 3, 2)]


def tp_exchange(parts):
    return lax.all_to_all(parts, "tp", split_axis=0, concat_axis=0, tiled=True)


def tp_scatter(parts):
    return jnp.sum(tp_exchange(parts).astype(F32), axis=0)


def vmem(count):
    return [pl.BlockSpec(memory_space=pltpu.VMEM)] * count


def smem():
    return pl.BlockSpec(memory_space=pltpu.SMEM)


def local_call(body, out_shape, in_specs, flops, moved, scratch=(), after=()):
    many = isinstance(out_shape, (list, tuple))
    count = len(in_specs)

    def ordered(*refs):
        body(*refs[:count], *refs[count + len(after) :])

    call = pl.pallas_call(
        ordered,
        out_shape=out_shape,
        in_specs=list(in_specs) + [pl.BlockSpec(memory_space=pl.ANY)] * len(after),
        out_specs=vmem(len(out_shape)) if many else vmem(1)[0],
        scratch_shapes=list(scratch),
        cost_estimate=pl.CostEstimate(flops=flops, bytes_accessed=moved, transcendentals=0),
        compiler_params=pltpu.CompilerParams(vmem_limit_bytes=VMEM_BYTES),
    )
    return lambda *operands: call(*operands, *after)


def held_kernel(value, out):
    out[...] = value[...]


def held(value, after):
    shape = jax.ShapeDtypeStruct(value.shape, value.dtype)
    moved = 2 * value.size * value.dtype.itemsize
    return local_call(held_kernel, shape, vmem(1), 0, moved, after=after)(value)


def nt_dot(left, right):
    return lax.dot_general(left, right, (((1,), (1,)), ((), ())), preferred_element_type=F32)


def pick_rows(slot, chunk, gain=None):
    hit = lax.broadcasted_iota(jnp.int32, (ROWS, chunk.shape[0]), 0) == slot
    pick = jnp.where(hit, 1.0, 0.0).astype(BF16)
    rows = jnp.dot(pick, chunk[...], preferred_element_type=F32)
    return (rows if gain is None else rows * gain).astype(BF16)


def store_groups(out, columns, value):
    for k in range(SIDE):
        out[k, :, columns] = value[k * ROWS : (k + 1) * ROWS].astype(BF16)


TILE = 256


def in_kernel(slot, gain, w_gate, w_up, *refs):
    chunks, (rows, both) = refs[:SIDE], refs[SIDE:]
    for k in range(SIDE):
        rows[k] = pick_rows(slot[k], chunks[k], gain[...])
    units = w_gate.shape[1]

    def step(n, unused):
        left = rows[...].reshape(SIDE * ROWS, -1)
        for at, weights in ((0, w_gate), (units, w_up)):
            columns = pl.ds(pl.multiple_of(n * TILE, TILE), TILE)
            target = pl.ds(pl.multiple_of(at + n * TILE, TILE), TILE)
            value = jnp.dot(left, weights[:, columns], preferred_element_type=F32)
            store_groups(both, target, value)
        return unused

    lax.fori_loop(0, units // TILE, step, 0)


def rows_through_in(slot, gain, w_gate, w_up, chunks, after=()):
    tokens, width = chunks[0].shape
    units = w_gate.shape[1]
    return local_call(
        in_kernel,
        [
            jax.ShapeDtypeStruct((SIDE, ROWS, width), BF16),
            jax.ShapeDtypeStruct((SIDE, ROWS, 2 * units), BF16),
        ],
        vmem(4 + SIDE),
        2 * SIDE * ROWS * width * (tokens + 2 * units),
        2 * width * (SIDE * (tokens + ROWS) + 2 * units),
        after=after,
    )(slot, gain, w_gate, w_up, *chunks)


def grad_kernel(place, slot, w_down, *refs):
    chunks, rows, parts = refs[:SIDE], refs[SIDE], refs[SIDE + 1 :]
    for k in range(SIDE):
        rows[k] = pick_rows(slot[k], chunks[k])

    def step(n, unused):
        left = jnp.concatenate([rows[place[k]] for k in range(SIDE)], axis=0)
        columns = pl.ds(pl.multiple_of(n * TILE, TILE), TILE)
        value = nt_dot(left, w_down[columns, :]).astype(BF16)
        for k in range(SIDE):
            parts[k][:, columns] = value[k * ROWS : (k + 1) * ROWS]
        return unused

    lax.fori_loop(0, w_down.shape[0] // TILE, step, 0)


def rows_through_down(place, slot, w_down, chunks, after=()):
    tokens, width = chunks[0].shape
    units = w_down.shape[0]
    rows, *parts = local_call(
        grad_kernel,
        [jax.ShapeDtypeStruct((SIDE, ROWS, width), BF16)]
        + [jax.ShapeDtypeStruct((ROWS, units), BF16)] * SIDE,
        [smem()] + vmem(2 + SIDE),
        2 * SIDE * ROWS * width * (tokens + units),
        2 * width * (SIDE * (tokens + ROWS) + units),
        after=after,
    )(place, slot, w_down, *chunks)
    return rows, parts


def back_kernel(place, w_gate, w_up, *refs):
    pieces, cots, out = refs[:SIDE], refs[SIDE], refs[SIDE + 1 :]
    units = w_gate.shape[1]
    for k in range(SIDE):
        cots[place[k]] = pieces[k][...]

    def step(n, unused):
        columns = pl.ds(pl.multiple_of(n * TILE, TILE), TILE)
        left = cots[...].reshape(SIDE * ROWS, 2 * units)
        rows = nt_dot(left[:, :units], w_gate[columns, :])
        rows = (rows + nt_dot(left[:, units:], w_up[columns, :])).astype(BF16)
        for k in range(SIDE):
            out[k][:, columns] = rows[k * ROWS : (k + 1) * ROWS]
        return unused

    lax.fori_loop(0, w_gate.shape[0] // TILE, step, 0)


def back_rows_of(place, w_gate, w_up, pieces, after):
    width, units = w_gate.shape
    cots, *back = local_call(
        back_kernel,
        [jax.ShapeDtypeStruct((SIDE, ROWS, 2 * units), BF16)]
        + [jax.ShapeDtypeStruct((ROWS, width), BF16)] * SIDE,
        [smem()] + vmem(2 + SIDE),
        4 * SIDE * ROWS * units * width,
        2 * (2 * SIDE * ROWS * units + 2 * units * width + SIDE * ROWS * width),
        after=after,
    )(place, w_gate, w_up, *pieces)
    return cots, back


def act_kernel(scales, gate_ups, *refs):
    cots, hidden_before = refs[:SIDE], refs[SIDE:-4]
    cot_out, hidden_out, row_cot, row_inner = refs[-4:]
    tile = 48
    count, width = cots[0].shape

    def step(n, unused):
        rows = pl.ds(pl.multiple_of(n * tile, tile), tile)

        def total(columns):
            return sum(gate_ups[k, rows, columns].astype(F32) for k in range(SIDE))

        weight, inv = scales[rows, 0:1], scales[rows, 1:2]
        gate = total(slice(0, width)) * inv
        up = total(slice(width, 2 * width)) * inv
        cot = sum(term[rows, :].astype(F32) for term in cots)
        sigma = 1.0 / (1.0 + jnp.exp(-gate))
        silu = gate * sigma
        hidden = silu * up
        row_cot[rows, :] = jnp.sum(cot * hidden, axis=1, keepdims=True)
        cot = cot * weight
        gate_cot = cot * up * (sigma + silu * (1.0 - sigma))
        up_cot = cot * silu
        row_inner[rows, :] = jnp.sum(gate_cot * gate + up_cot * up, axis=1, keepdims=True)
        cot_out[rows, :width] = (gate_cot * inv).astype(BF16)
        cot_out[rows, width:] = (up_cot * inv).astype(BF16)
        hidden = (hidden * weight).astype(BF16)
        if hidden_before:
            later = pl.ds(pl.multiple_of(count + n * tile, 16), tile)
            for k in range(SIDE):
                hidden_out[k, rows, :] = hidden_before[0][rows, :]
                hidden_out[k, later, :] = hidden
        else:
            hidden_out[rows, :] = hidden
        return unused

    lax.fori_loop(0, scales.shape[0] // tile, step, 0)


def act(scales, gate_ups, cots, *hidden_before, after):
    rows, hidden = cots[0].shape
    hidden_shape = (SIDE, 2 * rows, hidden) if hidden_before else (rows, hidden)
    return local_call(
        act_kernel,
        [
            jax.ShapeDtypeStruct((rows, 2 * hidden), BF16),
            jax.ShapeDtypeStruct(hidden_shape, BF16),
        ]
        + [jax.ShapeDtypeStruct((rows, 1), F32)] * 2,
        vmem(2 + SIDE + len(hidden_before)),
        40 * rows * hidden,
        48 * rows * hidden,
        after=after,
    )(scales, gate_ups, *cots, *hidden_before)


def combine_kernel(slots, *refs):
    rows, out, pick = refs[:GROUPS], refs[GROUPS:-1], refs[-1]
    tokens = slots.shape[0]
    block = tokens // SIDE
    for m in range(GROUPS):
        hit = lax.broadcasted_iota(jnp.int32, (tokens, ROWS), 1) == slots[:, m : m + 1]
        pick[m] = jnp.where(hit, 1.0, 0.0).astype(BF16)

    def step(n, unused):
        columns = pl.ds(pl.multiple_of(n * TILE, TILE), TILE)
        total = jnp.dot(pick[0], rows[0][:, columns], preferred_element_type=F32)
        for m in range(1, GROUPS):
            total = total + jnp.dot(pick[m], rows[m][:, columns], preferred_element_type=F32)
        total = total.astype(BF16)
        for k in range(SIDE):
            out[k][:, columns] = total[k * block : (k + 1) * block]
        return unused

    lax.fori_loop(0, rows[0].shape[1] // TILE, step, 0)


def combine(slots, rows):
    tokens, width = slots.shape[0], rows[0].shape[1]
    return local_call(
        combine_kernel,
        [jax.ShapeDtypeStruct((tokens // SIDE, width), BF16)] * SIDE,
        vmem(1 + GROUPS),
        2 * GROUPS * ROWS * tokens * width,
        2 * (GROUPS * ROWS + tokens) * width,
        [pltpu.VMEM((GROUPS, tokens, ROWS), BF16)],
    )(slots, *rows)


def shared_kernel(w_in, w_out, *refs):
    ins, grads, out = refs[:GROUPS], refs[GROUPS : 2 * GROUPS], refs[2 * GROUPS]
    top = w_in.shape[0]
    for g in range(GROUPS):
        out[g % SIDE, g // SIDE, :top] = nt_dot(w_in[...], ins[g][...]).astype(BF16)
        out[g % SIDE, g // SIDE, top:] = nt_dot(w_out[...], grads[g][...]).astype(BF16)


def shared_partials(w_in, w_out, ins, grads, after):
    tokens, width = ins[0].shape
    hidden = w_in.shape[0] + w_out.shape[0]
    return local_call(
        shared_kernel,
        jax.ShapeDtypeStruct((SIDE, 2, hidden, tokens), BF16),
        vmem(2 + 2 * GROUPS),
        2 * GROUPS * tokens * width * hidden,
        4 * GROUPS * tokens * width,
        after=after,
    )(w_in, w_out, *ins, *grads)


def shared_grad_kernel(cots, gain, *refs):
    ins, grads = refs[:GROUPS], refs[GROUPS : 2 * GROUPS]
    out_in, out_down, sum_in, sum_down = refs[2 * GROUPS :]
    top = out_in.shape[0]
    for g in range(GROUPS):
        cot = cots[g % SIDE, g // SIDE]
        first = jnp.dot(cot[:top], ins[g][...], preferred_element_type=F32)
        second = jnp.dot(cot[top:], grads[g][...], preferred_element_type=F32)
        sum_in[...] = first if g == 0 else sum_in[...] + first
        sum_down[...] = second if g == 0 else sum_down[...] + second
    out_in[...] = (sum_in[...] * gain[...]).astype(BF16)
    out_down[...] = sum_down[...].astype(BF16)


def shared_grads(cots, gain, ins, grads, top, after):
    tokens, width = ins[0].shape
    rest = cots.shape[2] - top
    return local_call(
        shared_grad_kernel,
        [jax.ShapeDtypeStruct((top, width), BF16), jax.ShapeDtypeStruct((rest, width), BF16)],
        vmem(2 + 2 * GROUPS),
        2 * GROUPS * tokens * width * (top + rest),
        4 * GROUPS * tokens * width,
        [pltpu.VMEM((top, width), F32), pltpu.VMEM((rest, width), F32)],
        after,
    )(cots, gain, *ins, *grads)


def owner_kernel(place, cots, out):
    block = out.shape[2]
    for g in range(GROUPS):
        for i in range(SIDE):
            out[place[g * SIDE + i]] = cots[g % SIDE, g // SIDE, :, i * block : (i + 1) * block]


def by_owner(place, cots):
    rows, tokens = cots.shape[2:]
    return local_call(
        owner_kernel,
        jax.ShapeDtypeStruct((GROUPS * SIDE, rows, tokens // SIDE), BF16),
        [smem()] + vmem(1),
        0,
        4 * GROUPS * rows * tokens,
    )(place, cots)


def dense_hidden_kernel(place, w_down, *refs):
    chunks, out = refs[:SIDE], refs[SIDE]
    block = chunks[0].shape[0] // SIDE
    for g in range(SIDE):
        columns = nt_dot(w_down[...], chunks[g][...]).astype(BF16)
        for i in range(SIDE):
            at = place[g * SIDE + i]
            lane = pl.multiple_of(lax.rem(at, SIDE) * block, block)
            out[lax.div(at, SIDE), :, pl.ds(lane, block)] = columns[
                :, i * block : (i + 1) * block
            ]


def dense_hidden(place, w_down, chunks, after=()):
    tokens, width = chunks[0].shape
    hidden = w_down.shape[0]
    return local_call(
        dense_hidden_kernel,
        jax.ShapeDtypeStruct((SIDE, hidden, tokens), BF16),
        [smem()] + vmem(1 + SIDE),
        2 * SIDE * tokens * width * hidden,
        2 * SIDE * tokens * width,
        after=after,
    )(place, w_down, *chunks)


def dense_grad_kernel(place, hidden, *refs):
    chunks, out, total = refs[:GROUPS], refs[GROUPS], refs[GROUPS + 1]
    block = chunks[0].shape[0] // SIDE
    for g in range(GROUPS):
        left = jnp.concatenate(
            [
                hidden[:, pl.ds(pl.multiple_of(place[g * SIDE + i] * block, block), block)]
                for i in range(SIDE)
            ],
            axis=1,
        )
        term = jnp.dot(left, chunks[g][...], preferred_element_type=F32)
        total[...] = term if g == 0 else total[...] + term
    out[...] = total[...].astype(BF16)


def dense_grad(place, hidden, chunks, after):
    tokens, width = chunks[0].shape
    units = hidden.shape[0]
    return local_call(
        dense_grad_kernel,
        jax.ShapeDtypeStruct((units, width), BF16),
        [smem()] + vmem(1 + GROUPS),
        2 * GROUPS * tokens * width * units,
        2 * GROUPS * tokens * width,
        [pltpu.VMEM((units, width), F32)],
        after,
    )(place, hidden, *chunks)


def gate_grads(hidden_cot, gate_value, up_value):
    sigma = jax.nn.sigmoid(gate_value)
    gate_cot = hidden_cot * up_value * sigma * (1.0 + gate_value * (1.0 - sigma))
    up_cot = hidden_cot * gate_value * sigma
    return (gate_cot, up_cot)


def local(
    hidden_in,
    out_grad,
    norm_gain,
    router_weight,
    route_ids,
    expert_gate,
    expert_up,
    expert_down,
    shared_gate,
    shared_up,
    shared_down,
    dense_gate,
    dense_up,
    dense_down,
):
    tok_rows, quarter = hidden_in.shape
    feature_count = quarter * lax.axis_size("tp")
    ep, tp = lax.axis_index("ep"), lax.axis_index("tp")
    z, y, core = ep // 8, (ep // 2) % SIDE, ep % 2
    w_gate, w_up, w_down = expert_gate[0], expert_up[0], expert_down[0]
    gain = norm_gain[None, :]

    g_at = jnp.arange(GROUPS, dtype=jnp.int32)[:, None]
    i_at = jnp.arange(SIDE, dtype=jnp.int32)[None, :]
    j_at = g_at % SIDE
    block_core = (core + g_at // SIDE) % 2
    block_z = jnp.where(block_core == 0, z - i_at, z - j_at) % SIDE
    block_y = jnp.where(block_core == 0, y - j_at, y - i_at) % SIDE
    block_of = ((block_z * SIDE + block_y) * 2 + block_core).reshape(-1)
    to_path = (block_of[:, None] == jnp.arange(EXPERTS, dtype=jnp.int32)[None, :]).astype(F32)

    picks = jnp.any(
        route_ids[:, :, None] == jnp.arange(EXPERTS, dtype=jnp.int32)[None, None, :], axis=1
    ).astype(F32)
    token_line = jnp.arange(tok_rows, dtype=jnp.int32)
    earlier = (token_line[:, None] < token_line[None, :]).astype(F32)
    own_position = jnp.dot(picks.T, earlier, precision=HIGHEST)
    own_position = jnp.where(picks.T > 0.0, own_position, -1.0)
    wide_in = hidden_in.astype(F32)
    square_part = jnp.sum(wide_in * wide_in, axis=1, keepdims=True)
    logit_part = jnp.dot(wide_in * gain, router_weight, precision=HIGHEST)
    stats = jnp.concatenate([logit_part, square_part], axis=1)
    stats = tp_scatter(jnp.broadcast_to(stats[None], (SIDE,) + stats.shape))
    plain_logits = stats[:, :EXPERTS]
    mean_square = stats[:, EXPERTS:] / feature_count + EPSILON
    inv_rms = lax.rsqrt(mean_square)
    rms = mean_square * inv_rms
    normed = (wide_in * inv_rms * gain).astype(BF16)
    scores = jax.nn.sigmoid(plain_logits * inv_rms)
    chosen = picks * scores
    chosen_total = jnp.sum(chosen, axis=1, keepdims=True)
    route_weight = ROUTE_SCALE * chosen / chosen_total

    told = jnp.concatenate(
        [
            own_position[:, None, :],
            route_weight.T[:, None, :],
            jnp.broadcast_to(inv_rms.reshape(1, 1, tok_rows), (EXPERTS, 1, tok_rows)),
        ],
        axis=1,
    )
    told = lax.all_to_all(told, "ep", split_axis=0, concat_axis=0, tiled=True)
    told_path = jnp.dot(to_path, told.reshape(EXPERTS, 3 * tok_rows), precision=HIGHEST)
    told_path = told_path.reshape(GROUPS, SIDE, 3, tok_rows)
    position = told_path[:, :, 0].astype(jnp.int32)
    offset = (CAP * jnp.arange(SIDE, dtype=jnp.int32))[None, :, None]
    slot = jnp.where(position >= 0, position + offset, -1).reshape(GROUPS, 1, SIDE * tok_rows)
    own_told = told_path.reshape(2, SIDE, SIDE, 3, tok_rows)
    own_told = lax.dynamic_index_in_dim(own_told, tp, 1, keepdims=False)
    own_weight = own_told[:, :, 1].reshape(2, 1, SIDE * tok_rows)
    own_inv = own_told[:, :, 2].reshape(2, 1, SIDE * tok_rows)

    first = first_gather([hidden_in, out_grad])
    in_chunks = second_gather(first, 0, 2, [told])

    own, other = slice(0, SIDE), slice(SIDE, GROUPS)
    halves = (own, other)
    turn = (jnp.arange(SIDE, dtype=jnp.int32) + tp) % SIDE
    rows_in, both_terms, rows_grad, cot_terms = [], [], [], []
    for half in halves:
        rows, part = rows_through_in(
            slot[half], gain, w_gate, w_up, in_chunks[half], both_terms[:1]
        )
        rows_in.append(rows)
        both_terms.append(tp_exchange(part))
        if half is own:
            grad_chunks = second_gather(first, 1, 2, [part, in_chunks[-1]])
    before = [part]
    for half in halves:
        rows, parts = rows_through_down(turn, slot[half], w_down, grad_chunks[half], before)
        rows_grad.append(rows)
        cot_terms.append(tp_terms(parts))
        before = [*cot_terms[-1][1:], both_terms[1]]
    hidden_part = parts[0]

    units = shared_down.shape[0]
    shared_in = (jnp.concatenate([shared_gate.T, shared_up.T], axis=0).astype(F32) * gain).astype(
        BF16
    )
    shared_out = jnp.concatenate([shared_down, jnp.zeros((8, quarter), BF16)], axis=0)
    shared_parts = shared_partials(
        shared_in, shared_out, in_chunks, grad_chunks, [hidden_part]
    )
    own_slot = jnp.stack(
        [lax.dynamic_index_in_dim(slot[half], tp, 0, keepdims=False) for half in halves]
    )
    own_hit = jnp.arange(ROWS, dtype=jnp.int32)[None, :, None] == own_slot
    row_scales = jnp.concatenate(
        [
            jnp.sum(jnp.where(own_hit, value, 0.0), axis=2, keepdims=True)
            for value in (own_weight, own_inv)
        ],
        axis=2,
    )
    both_cots, hiddens, row_cots, row_inners = [], (), [], []
    for n in range(2):
        both_cot, hidden, row_cot, row_inner = act(
            row_scales[n], both_terms[n], cot_terms[n], *hiddens, after=[shared_parts]
        )
        both_cots.append(tp_gather(both_cot))
        hiddens = (hidden,)
        row_cots.append(row_cot)
        row_inners.append(row_inner)
    s_line = jnp.arange(2, dtype=jnp.int32)[None, :]
    j_line = jnp.arange(SIDE, dtype=jnp.int32)
    j_col = j_line[:, None]
    return_expert = jnp.where(
        core == 0,
        (z * SIDE + (y + j_col) % SIDE) * 2 + s_line,
        (((z + j_col) % SIDE) * SIDE + y) * 2 + 1 - s_line,
    ).reshape(-1)
    pick_expert = (
        return_expert[:, None] == jnp.arange(EXPERTS, dtype=jnp.int32)[None, :]
    ).astype(F32)
    line_position = held(own_position, [hidden_part])
    line_position = jnp.stack(
        [line_position]
        + [lax.ppermute(line_position, "ep", first_hop(k)) for k in range(1, SIDE)]
    )
    position_here = jnp.einsum(
        "ket,me->ktm", line_position, pick_expert, precision=HIGHEST
    ).astype(jnp.int32)
    return_slot = jnp.where(
        position_here >= 0, position_here + (CAP * j_line)[:, None, None], -1
    ).reshape(SIDE * tok_rows, GROUPS)

    back, ordered_cots = [], []
    for n, before in ((0, row_cot), (1, return_slot)):
        ordered, rows = back_rows_of(turn, w_gate, w_up, both_cots[n], [before])
        ordered_cots.append(ordered)
        back.extend(rows)

    returned = []
    for j in range(SIDE):
        returned.append(back[j] if j == 0 else lax.ppermute(back[j], "ep", second_hop(-j)))
        returned.append(lax.ppermute(back[SIDE + j], "ep", swap_second_hop(-j)))
    summed = combine(return_slot, returned)
    routed_cot = summed[0].astype(F32)
    for k in range(1, SIDE):
        routed_cot = routed_cot + lax.ppermute(summed[k], "ep", first_hop(-k)).astype(F32)

    inner = shared_parts.shape[2]
    shared_sum = tp_scatter(shared_parts)
    gate_s = shared_sum[:, :units] * own_inv
    up_s = shared_sum[:, units : 2 * units] * own_inv
    hid_cot_s = shared_sum[:, 2 * units : 3 * units]
    gate_cot_s, up_cot_s = gate_grads(hid_cot_s, gate_s, up_s)

    def to_tokens(row_values):
        return jnp.sum(jnp.where(own_hit, jnp.stack(row_values), 0.0), axis=1, keepdims=True)

    shared_inner = jnp.sum(gate_cot_s * gate_s + up_cot_s * up_s, axis=1, keepdims=True)
    cots = jnp.concatenate(
        [
            gate_cot_s * own_inv,
            up_cot_s * own_inv,
            gate_s * jax.nn.sigmoid(gate_s) * up_s,
            to_tokens(row_cots),
            to_tokens(row_inners) + shared_inner,
            jnp.zeros((2, inner - 3 * units - 2, SIDE * tok_rows), F32),
        ],
        axis=1,
    ).astype(BF16)
    cots_all = tp_exchange(jnp.broadcast_to(cots[None], (SIDE,) + cots.shape))
    to_owner = by_owner(block_of, cots_all)
    to_owner = lax.all_to_all(to_owner, "ep", split_axis=0, concat_axis=0, tiled=True)
    shared_whole = lax.all_gather(
        held(shared_in, [hidden_part]), "ep", axis=0, tiled=True
    )
    shared_scaled = lax.dot_general(
        to_owner[:, : 2 * units].reshape(-1, tok_rows),
        shared_whole,
        (((0,), (0,)), ((), ())),
        preferred_element_type=F32,
    ) * rms

    sums = to_owner[:, 3 * units : 3 * units + 2].astype(F32)
    weight_cot = sums[:, 0].T
    chosen_cot = picks * (
        ROUTE_SCALE
        * (
            weight_cot / chosen_total
            - jnp.sum(weight_cot * chosen, axis=1, keepdims=True) / (chosen_total * chosen_total)
        )
    )
    logit_cot = chosen_cot * scores * (1.0 - scores)
    router_part = jnp.dot(logit_cot.T, normed.astype(F32), precision=HIGHEST)
    router_cot = jnp.dot(logit_cot, router_weight.T, precision=HIGHEST)
    inner_sum = jnp.sum(sums[:, 1], axis=0).reshape(tok_rows, 1) * rms + jnp.sum(
        logit_cot * plain_logits, axis=1, keepdims=True
    )

    scaled = (routed_cot * rms + router_cot) * gain + shared_scaled
    input_cot = inv_rms * scaled - wide_in * (inv_rms * inv_rms * inv_rms) * (
        inner_sum / feature_count
    )
    dense_cot = (out_grad.astype(F32) + input_cot).astype(BF16)

    cot_chunks = second_gather(first_gather([dense_cot]), 0, 1, [])
    gate_t, up_t = dense_gate.T, dense_up.T
    hidden2 = (jax.nn.silu(gate_t.astype(F32)) * up_t.astype(F32)).astype(BF16)

    def flat(parts, columns=slice(None)):
        whole = jnp.concatenate([part[:, :, columns] for part in parts], axis=1)
        return whole.reshape(GROUPS * ROWS, -1)

    def rows_dot(left, right):
        return lax.dot_general(
            left, right, (((0,), (0,)), ((), ())), preferred_element_type=F32
        ).astype(BF16)[None]

    grads_in, grads_down = shared_grads(
        cots_all, gain, in_chunks, grad_chunks, 2 * units, [summed[0]]
    )
    units_r = w_gate.shape[1]
    rows_in = flat(rows_in)
    grad_expert_gate = rows_dot(rows_in, flat(ordered_cots, slice(0, units_r)))
    hidden_all = tp_exchange(held(hiddens[0], [to_owner])).reshape(GROUPS * ROWS, -1)

    dense_place = (block_z * SIDE + block_y).reshape(2, -1)
    own_part = dense_hidden(
        dense_place[0], dense_down, cot_chunks[own], [hidden_all]
    )
    own_sum = tp_scatter(own_part)
    turned = (((block_z - tp) % SIDE) * SIDE + block_y).reshape(2, -1)
    hidden2_part = dense_hidden(turned[1], dense_down, cot_chunks[other])
    other_sum = sum(term.astype(F32) for term in tp_terms(list(hidden2_part)))

    def by_core(mine, others):
        both = jnp.where(core == 0, jnp.stack([mine, others]), jnp.stack([others, mine]))
        both = both.reshape(2, mine.shape[0], SIDE, tok_rows).transpose(1, 2, 0, 3)
        return both.reshape(mine.shape[0], -1)

    hidden2_cot = by_core(own_sum, other_sum)
    share = 8 * tok_rows
    gate_mine = lax.dynamic_slice_in_dim(gate_t, tp * share, share, 1).astype(F32)
    up_mine = lax.dynamic_slice_in_dim(up_t, tp * share, share, 1).astype(F32)
    grad_gate2, grad_up2 = gate_grads(hidden2_cot, gate_mine, up_mine)
    grad_dense_down = dense_grad(block_of, hidden2, cot_chunks, [hidden2_part])
    grad_router = ep_sum(
        router_part, (dense_cot, own_part, hidden2_part, grad_dense_down, grad_dense_down)
    ).T
    return (
        grad_gate2.astype(BF16).T,
        grad_up2.astype(BF16).T,
        grad_dense_down,
        grad_expert_gate,
        rows_dot(rows_in, flat(ordered_cots, slice(units_r, None))),
        rows_dot(held(hidden_all, [hidden2_part]), flat(rows_grad)),
        grads_in[:units].T,
        grads_in[units:].T,
        grads_down[:units],
        grad_router,
    )


def solution(mesh):
    in_specs = (
        P("ep", "tp"),
        P("ep", "tp"),
        P("tp"),
        P("tp", None),
        P("ep", None),
        P("ep", "tp", None),
        P("ep", "tp", None),
        P("ep", None, "tp"),
        P("tp", "ep"),
        P("tp", "ep"),
        P("ep", "tp"),
        P(None, "ep"),
        P(None, "ep"),
        P("ep", "tp"),
    )
    out_specs = (
        P("tp", "ep"),
        P("tp", "ep"),
        P("ep", "tp"),
        P("ep", "tp", None),
        P("ep", "tp", None),
        P("ep", None, "tp"),
        P("tp", "ep"),
        P("tp", "ep"),
        P("ep", "tp"),
        P("tp", None),
    )
    return jax.shard_map(local, mesh=mesh, in_specs=in_specs, out_specs=out_specs, check_vma=False)
```

```python
import functools

import jax
import jax.numpy as jnp
from jax import lax
from jax.experimental import pallas as pl
from jax.experimental.pallas import tpu as pltpu
from jax.sharding import PartitionSpec as P

EXPERTS = 32
TOP = 8
CAP = 36
SIDE = 4
GROUPS = 8
ROWS = SIDE * CAP

EPSILON = 1e-05
ROUTE_SCALE = 2.5
F32 = jnp.float32
BF16 = jnp.bfloat16
HIGHEST = lax.Precision.HIGHEST
VMEM_BYTES = 50 * 1024 * 1024


def ep_at(z, y, core):
    return ((z % SIDE) * SIDE + y % SIDE) * 2 + core


def ep_pairs(target):
    return [
        (ep_at(z, y, core), target(z, y, core))
        for z in range(SIDE)
        for y in range(SIDE)
        for core in range(2)
    ]


def first_hop(k):
    return ep_pairs(lambda z, y, core: ep_at(z, y + k, 1) if core else ep_at(z + k, y, 0))


def first_lines():
    core_0 = [[ep_at(z, y, 0) for z in range(SIDE)] for y in range(SIDE)]
    return core_0 + [[ep_at(z, y, 1) for y in range(SIDE)] for z in range(SIDE)]


def second_hop(k):
    return ep_pairs(lambda z, y, core: ep_at(z + k, y, 1) if core else ep_at(z, y + k, 0))


def swap_second_hop(k):
    return ep_pairs(lambda z, y, core: ep_at(z, y + k, 0) if core else ep_at(z + k, y, 1))


def core_swap():
    return ep_pairs(lambda z, y, core: ep_at(z, y, 1 - core))


def tp_hop(k):
    return [(i, (i + k) % SIDE) for i in range(SIDE)]


def join_kernel(first, count, *refs):
    blocks, out = refs[:SIDE], refs[SIDE]
    rows = out.shape[0] // SIDE
    for i in range(SIDE):
        out[i * rows : (i + 1) * rows] = blocks[i][first : first + rows]


def join(blocks, number, count, after):
    rows, width = blocks[0].shape[0] // count, blocks[0].shape[1]
    return local_call(
        functools.partial(join_kernel, number * rows, count),
        jax.ShapeDtypeStruct((SIDE * rows, width), blocks[0].dtype),
        vmem(SIDE),
        0,
        4 * SIDE * rows * width,
        after=after,
    )(*blocks)


def first_gather(blocks):
    stack = jnp.concatenate(blocks, axis=0) if len(blocks) > 1 else blocks[0]
    return [stack] + [lax.ppermute(stack, "ep", first_hop(k)) for k in range(1, SIDE)]


def second_gather(first, number, count, after):
    joined = join(first, number, count, after)
    own = [joined] + [lax.ppermute(joined, "ep", second_hop(k)) for k in range(1, SIDE)]
    return own + [lax.ppermute(chunk, "ep", core_swap()) for chunk in own]


def add_kernel(first, second, out):
    out[...] = first[...] + second[...]


def ep_sum(value, stages):
    pairings = ((0, 0, 1), (0, 1, 0), (1, 0, 0), (0, 2, 0), (2, 0, 0))
    shape = jax.ShapeDtypeStruct(value.shape, value.dtype)
    for (dz, dy, dcore), stage in zip(pairings, stages, strict=True):
        pairs = ep_pairs(lambda z, y, core: ep_at(z ^ dz, y ^ dy, core ^ dcore))
        met = lax.ppermute(value, "ep", pairs)
        value = local_call(add_kernel, shape, vmem(2), 0, 12 * value.size, after=[stage])(
            value, met
        )
    return value


def tp_gather(piece):
    return [piece] + [lax.ppermute(piece, "tp", tp_hop(-k)) for k in (1, 2, 3)]


def tp_terms(parts):
    return [parts[0]] + [lax.ppermute(parts[k], "tp", tp_hop(k)) for k in (1, 3, 2)]


def tp_exchange(parts):
    return lax.all_to_all(parts, "tp", split_axis=0, concat_axis=0, tiled=True)


def tp_scatter(parts):
    return jnp.sum(tp_exchange(parts).astype(F32), axis=0)


def vmem(count):
    return [pl.BlockSpec(memory_space=pltpu.VMEM)] * count


def smem():
    return pl.BlockSpec(memory_space=pltpu.SMEM)


def local_call(body, out_shape, in_specs, flops, moved, scratch=(), after=()):
    many = isinstance(out_shape, (list, tuple))
    count = len(in_specs)

    def ordered(*refs):
        body(*refs[:count], *refs[count + len(after) :])

    call = pl.pallas_call(
        ordered,
        out_shape=out_shape,
        in_specs=list(in_specs) + [pl.BlockSpec(memory_space=pl.ANY)] * len(after),
        out_specs=vmem(len(out_shape)) if many else vmem(1)[0],
        scratch_shapes=list(scratch),
        cost_estimate=pl.CostEstimate(flops=flops, bytes_accessed=moved, transcendentals=0),
        compiler_params=pltpu.CompilerParams(vmem_limit_bytes=VMEM_BYTES),
    )
    return lambda *operands: call(*operands, *after)


def held_kernel(value, out):
    out[...] = value[...]


def held(value, after):
    shape = jax.ShapeDtypeStruct(value.shape, value.dtype)
    moved = 2 * value.size * value.dtype.itemsize
    return local_call(held_kernel, shape, vmem(1), 0, moved, after=after)(value)


def term_sum_kernel(terms, out):
    out[...] = sum(terms[k].astype(F32) for k in range(1, SIDE)) + terms[0].astype(F32)


def term_sum(terms, after):
    shape = jax.ShapeDtypeStruct(terms.shape[1:], F32)
    return local_call(term_sum_kernel, shape, vmem(1), 0, 4 * terms.size, after=after)(terms)


def nt_dot(left, right):
    return lax.dot_general(left, right, (((1,), (1,)), ((), ())), preferred_element_type=F32)


def pick_rows(slot, chunk, gain=None):
    hit = lax.broadcasted_iota(jnp.int32, (ROWS, chunk.shape[0]), 0) == slot
    pick = jnp.where(hit, 1.0, 0.0).astype(BF16)
    rows = jnp.dot(pick, chunk[...], preferred_element_type=F32)
    return (rows if gain is None else rows * gain).astype(BF16)


def store_groups(out, columns, value):
    for k in range(SIDE):
        out[k, :, columns] = value[k * ROWS : (k + 1) * ROWS].astype(BF16)


TILE = 256


def in_kernel(slot, gain, w_gate, w_up, *refs):
    chunks, (rows, both) = refs[:SIDE], refs[SIDE:]
    for k in range(SIDE):
        rows[k] = pick_rows(slot[k], chunks[k], gain[...])
    units = w_gate.shape[1]

    def step(n, unused):
        left = rows[...].reshape(SIDE * ROWS, -1)
        for at, weights in ((0, w_gate), (units, w_up)):
            columns = pl.ds(pl.multiple_of(n * TILE, TILE), TILE)
            target = pl.ds(pl.multiple_of(at + n * TILE, TILE), TILE)
            value = jnp.dot(left, weights[:, columns], preferred_element_type=F32)
            store_groups(both, target, value)
        return unused

    lax.fori_loop(0, units // TILE, step, 0)


def rows_through_in(slot, gain, w_gate, w_up, chunks, after=()):
    tokens, width = chunks[0].shape
    units = w_gate.shape[1]
    return local_call(
        in_kernel,
        [
            jax.ShapeDtypeStruct((SIDE, ROWS, width), BF16),
            jax.ShapeDtypeStruct((SIDE, ROWS, 2 * units), BF16),
        ],
        vmem(4 + SIDE),
        2 * SIDE * ROWS * width * (tokens + 2 * units),
        2 * width * (SIDE * (tokens + ROWS) + 2 * units),
        after=after,
    )(slot, gain, w_gate, w_up, *chunks)


def grad_kernel(place, slot, w_down, *refs):
    chunks, rows, parts = refs[:SIDE], refs[SIDE], refs[SIDE + 1 :]
    for k in range(SIDE):
        rows[k] = pick_rows(slot[k], chunks[k])

    def step(n, unused):
        left = jnp.concatenate([rows[place[k]] for k in range(SIDE)], axis=0)
        columns = pl.ds(pl.multiple_of(n * TILE, TILE), TILE)
        value = nt_dot(left, w_down[columns, :]).astype(BF16)
        for k in range(SIDE):
            parts[k][:, columns] = value[k * ROWS : (k + 1) * ROWS]
        return unused

    lax.fori_loop(0, w_down.shape[0] // TILE, step, 0)


def rows_through_down(place, slot, w_down, chunks, after=()):
    tokens, width = chunks[0].shape
    units = w_down.shape[0]
    rows, *parts = local_call(
        grad_kernel,
        [jax.ShapeDtypeStruct((SIDE, ROWS, width), BF16)]
        + [jax.ShapeDtypeStruct((ROWS, units), BF16)] * SIDE,
        [smem()] + vmem(2 + SIDE),
        2 * SIDE * ROWS * width * (tokens + units),
        2 * width * (SIDE * (tokens + ROWS) + units),
        after=after,
    )(place, slot, w_down, *chunks)
    return rows, parts


def back_kernel(place, w_gate, w_up, *refs):
    pieces, cots, out = refs[:SIDE], refs[SIDE], refs[SIDE + 1 :]
    units = w_gate.shape[1]
    for k in range(SIDE):
        cots[place[k]] = pieces[k][...]

    def step(n, unused):
        columns = pl.ds(pl.multiple_of(n * TILE, TILE), TILE)
        left = cots[...].reshape(SIDE * ROWS, 2 * units)
        rows = nt_dot(left[:, :units], w_gate[columns, :])
        rows = (rows + nt_dot(left[:, units:], w_up[columns, :])).astype(BF16)
        for k in range(SIDE):
            out[k][:, columns] = rows[k * ROWS : (k + 1) * ROWS]
        return unused

    lax.fori_loop(0, w_gate.shape[0] // TILE, step, 0)


def back_rows_of(place, w_gate, w_up, pieces, after):
    width, units = w_gate.shape
    cots, *back = local_call(
        back_kernel,
        [jax.ShapeDtypeStruct((SIDE, ROWS, 2 * units), BF16)]
        + [jax.ShapeDtypeStruct((ROWS, width), BF16)] * SIDE,
        [smem()] + vmem(2 + SIDE),
        4 * SIDE * ROWS * units * width,
        2 * (2 * SIDE * ROWS * units + 2 * units * width + SIDE * ROWS * width),
        after=after,
    )(place, w_gate, w_up, *pieces)
    return cots, back


def act_kernel(scales, gate_ups, *refs):
    cots, hidden_before = refs[:SIDE], refs[SIDE:-4]
    cot_out, hidden_out, row_cot, row_inner = refs[-4:]
    tile = 48
    count, width = cots[0].shape

    def step(n, unused):
        rows = pl.ds(pl.multiple_of(n * tile, tile), tile)

        def total(columns):
            return sum(gate_ups[k, rows, columns].astype(F32) for k in range(SIDE))

        weight, inv = scales[rows, 0:1], scales[rows, 1:2]
        gate = total(slice(0, width)) * inv
        up = total(slice(width, 2 * width)) * inv
        cot = sum(term[rows, :].astype(F32) for term in cots)
        sigma = 1.0 / (1.0 + jnp.exp(-gate))
        silu = gate * sigma
        hidden = silu * up
        row_cot[rows, :] = jnp.sum(cot * hidden, axis=1, keepdims=True)
        cot = cot * weight
        gate_cot = cot * up * (sigma + silu * (1.0 - sigma))
        up_cot = cot * silu
        row_inner[rows, :] = jnp.sum(gate_cot * gate + up_cot * up, axis=1, keepdims=True)
        cot_out[rows, :width] = (gate_cot * inv).astype(BF16)
        cot_out[rows, width:] = (up_cot * inv).astype(BF16)
        hidden = (hidden * weight).astype(BF16)
        if hidden_before:
            later = pl.ds(pl.multiple_of(count + n * tile, 16), tile)
            for k in range(SIDE):
                hidden_out[k, rows, :] = hidden_before[0][rows, :]
                hidden_out[k, later, :] = hidden
        else:
            hidden_out[rows, :] = hidden
        return unused

    lax.fori_loop(0, scales.shape[0] // tile, step, 0)


def act(scales, gate_ups, cots, *hidden_before, after):
    rows, hidden = cots[0].shape
    hidden_shape = (SIDE, 2 * rows, hidden) if hidden_before else (rows, hidden)
    return local_call(
        act_kernel,
        [
            jax.ShapeDtypeStruct((rows, 2 * hidden), BF16),
            jax.ShapeDtypeStruct(hidden_shape, BF16),
        ]
        + [jax.ShapeDtypeStruct((rows, 1), F32)] * 2,
        vmem(2 + SIDE + len(hidden_before)),
        40 * rows * hidden,
        48 * rows * hidden,
        after=after,
    )(scales, gate_ups, *cots, *hidden_before)


def combine_kernel(slots, *refs):
    rows, out, pick = refs[:GROUPS], refs[GROUPS:-1], refs[-1]
    tokens = slots.shape[0]
    block = tokens // SIDE
    for m in range(GROUPS):
        hit = lax.broadcasted_iota(jnp.int32, (tokens, ROWS), 1) == slots[:, m : m + 1]
        pick[m] = jnp.where(hit, 1.0, 0.0).astype(BF16)

    def step(n, unused):
        columns = pl.ds(pl.multiple_of(n * TILE, TILE), TILE)
        total = jnp.dot(pick[0], rows[0][:, columns], preferred_element_type=F32)
        for m in range(1, GROUPS):
            total = total + jnp.dot(pick[m], rows[m][:, columns], preferred_element_type=F32)
        total = total.astype(BF16)
        for k in range(SIDE):
            out[k][:, columns] = total[k * block : (k + 1) * block]
        return unused

    lax.fori_loop(0, rows[0].shape[1] // TILE, step, 0)


def combine(slots, rows):
    tokens, width = slots.shape[0], rows[0].shape[1]
    return local_call(
        combine_kernel,
        [jax.ShapeDtypeStruct((tokens // SIDE, width), BF16)] * SIDE,
        vmem(1 + GROUPS),
        2 * GROUPS * ROWS * tokens * width,
        2 * (GROUPS * ROWS + tokens) * width,
        [pltpu.VMEM((GROUPS, tokens, ROWS), BF16)],
    )(slots, *rows)


def shared_in_kernel(weights, *refs):
    ins, out = refs[:GROUPS], refs[GROUPS]
    for g in range(GROUPS):
        out[g % SIDE, g // SIDE] = nt_dot(weights[...], ins[g][...]).astype(BF16)


def shared_in_partials(weights, ins, after):
    tokens, width = ins[0].shape
    hidden = weights.shape[0]
    return local_call(
        shared_in_kernel,
        jax.ShapeDtypeStruct((SIDE, 2, hidden, tokens), BF16),
        vmem(1 + GROUPS),
        2 * GROUPS * tokens * width * hidden // 8,
        2 * GROUPS * tokens * width // 8,
        after=after,
    )(weights, *ins)


def shared_kernel(weights, first, *refs):
    grads, out = refs[:GROUPS], refs[GROUPS]
    top = first.shape[2]
    out[:, :, :top] = first[...]
    for g in range(GROUPS):
        out[g % SIDE, g // SIDE, top:] = nt_dot(weights[...], grads[g][...]).astype(BF16)


def shared_partials(weights, first, grads, after):
    tokens, width = grads[0].shape
    hidden = first.shape[2] + weights.shape[0]
    return local_call(
        shared_kernel,
        jax.ShapeDtypeStruct((SIDE, 2, hidden, tokens), BF16),
        vmem(2 + GROUPS),
        2 * GROUPS * tokens * width * hidden,
        2 * GROUPS * tokens * width,
        after=after,
    )(weights, first, *grads)


def shared_grad_kernel(cots, gain, *refs):
    ins, grads = refs[:GROUPS], refs[GROUPS : 2 * GROUPS]
    out_in, out_down, sum_in, sum_down = refs[2 * GROUPS :]
    top = out_in.shape[0]
    for g in range(GROUPS):
        cot = cots[g % SIDE, g // SIDE]
        first = jnp.dot(cot[:top], ins[g][...], preferred_element_type=F32)
        second = jnp.dot(cot[top:], grads[g][...], preferred_element_type=F32)
        sum_in[...] = first if g == 0 else sum_in[...] + first
        sum_down[...] = second if g == 0 else sum_down[...] + second
    out_in[...] = (sum_in[...] * gain[...]).astype(BF16)
    out_down[...] = sum_down[...].astype(BF16)


def shared_grads(cots, gain, ins, grads, top, after):
    tokens, width = ins[0].shape
    rest = cots.shape[2] - top
    return local_call(
        shared_grad_kernel,
        [jax.ShapeDtypeStruct((top, width), BF16), jax.ShapeDtypeStruct((rest, width), BF16)],
        vmem(2 + 2 * GROUPS),
        2 * GROUPS * tokens * width * (top + rest) // 8,
        4 * GROUPS * tokens * width // 8,
        [pltpu.VMEM((top, width), F32), pltpu.VMEM((rest, width), F32)],
        after,
    )(cots, gain, *ins, *grads)


def owner_kernel(place, cots, out):
    block = out.shape[2]
    for g in range(GROUPS):
        for i in range(SIDE):
            out[place[g * SIDE + i]] = cots[g % SIDE, g // SIDE, :, i * block : (i + 1) * block]


def by_owner(place, cots):
    rows, tokens = cots.shape[2:]
    return local_call(
        owner_kernel,
        jax.ShapeDtypeStruct((GROUPS * SIDE, rows, tokens // SIDE), BF16),
        [smem()] + vmem(1),
        0,
        4 * GROUPS * rows * tokens,
    )(place, cots)


def dense_hidden_kernel(place, w_down, *refs):
    chunks, out = refs[:SIDE], refs[SIDE]
    block = chunks[0].shape[0] // SIDE
    for g in range(SIDE):
        columns = nt_dot(w_down[...], chunks[g][...]).astype(BF16)
        for i in range(SIDE):
            at = place[g * SIDE + i]
            lane = pl.multiple_of(lax.rem(at, SIDE) * block, block)
            out[lax.div(at, SIDE), :, pl.ds(lane, block)] = columns[
                :, i * block : (i + 1) * block
            ]


def dense_hidden(place, w_down, chunks, after=()):
    tokens, width = chunks[0].shape
    hidden = w_down.shape[0]
    return local_call(
        dense_hidden_kernel,
        jax.ShapeDtypeStruct((SIDE, hidden, tokens), BF16),
        [smem()] + vmem(1 + SIDE),
        2 * SIDE * tokens * width * hidden,
        2 * SIDE * tokens * width,
        after=after,
    )(place, w_down, *chunks)


def dense_grad_kernel(place, hidden, *refs):
    chunks, out, total = refs[:GROUPS], refs[GROUPS], refs[GROUPS + 1]
    block = chunks[0].shape[0] // SIDE
    for g in range(GROUPS):
        left = jnp.concatenate(
            [
                hidden[:, pl.ds(pl.multiple_of(place[g * SIDE + i] * block, block), block)]
                for i in range(SIDE)
            ],
            axis=1,
        )
        term = jnp.dot(left, chunks[g][...], preferred_element_type=F32)
        total[...] = term if g == 0 else total[...] + term
    out[...] = total[...].astype(BF16)


def dense_grad(place, hidden, chunks, after):
    tokens, width = chunks[0].shape
    units = hidden.shape[0]
    return local_call(
        dense_grad_kernel,
        jax.ShapeDtypeStruct((units, width), BF16),
        [smem()] + vmem(1 + GROUPS),
        2 * GROUPS * tokens * width * units,
        2 * GROUPS * tokens * width,
        [pltpu.VMEM((units, width), F32)],
        after,
    )(place, hidden, *chunks)


def gate_grads(hidden_cot, gate_value, up_value):
    sigma = jax.nn.sigmoid(gate_value)
    gate_cot = hidden_cot * up_value * sigma * (1.0 + gate_value * (1.0 - sigma))
    up_cot = hidden_cot * gate_value * sigma
    return (gate_cot, up_cot)


def local(
    hidden_in,
    out_grad,
    norm_gain,
    router_weight,
    route_ids,
    expert_gate,
    expert_up,
    expert_down,
    shared_gate,
    shared_up,
    shared_down,
    dense_gate,
    dense_up,
    dense_down,
):
    tok_rows, quarter = hidden_in.shape
    feature_count = quarter * lax.axis_size("tp")
    ep, tp = lax.axis_index("ep"), lax.axis_index("tp")
    z, y, core = ep // 8, (ep // 2) % SIDE, ep % 2
    w_gate, w_up, w_down = expert_gate[0], expert_up[0], expert_down[0]
    gain = norm_gain[None, :]

    g_at = jnp.arange(GROUPS, dtype=jnp.int32)[:, None]
    i_at = jnp.arange(SIDE, dtype=jnp.int32)[None, :]
    j_at = g_at % SIDE
    block_core = (core + g_at // SIDE) % 2
    block_z = jnp.where(block_core == 0, z - i_at, z - j_at) % SIDE
    block_y = jnp.where(block_core == 0, y - j_at, y - i_at) % SIDE
    block_of = ((block_z * SIDE + block_y) * 2 + block_core).reshape(-1)
    to_path = (block_of[:, None] == jnp.arange(EXPERTS, dtype=jnp.int32)[None, :]).astype(F32)

    picks = jnp.any(
        route_ids[:, :, None] == jnp.arange(EXPERTS, dtype=jnp.int32)[None, None, :], axis=1
    ).astype(F32)
    token_line = jnp.arange(tok_rows, dtype=jnp.int32)
    earlier = (token_line[:, None] < token_line[None, :]).astype(F32)
    own_position = jnp.dot(picks.T, earlier, precision=HIGHEST)
    own_position = jnp.where(picks.T > 0.0, own_position, -1.0)
    wide_in = hidden_in.astype(F32)
    square_part = jnp.sum(wide_in * wide_in, axis=1, keepdims=True)
    logit_part = jnp.dot(wide_in * gain, router_weight, precision=HIGHEST)
    stats = jnp.concatenate([logit_part, square_part], axis=1)
    stats = tp_scatter(jnp.broadcast_to(stats[None], (SIDE,) + stats.shape))
    plain_logits = stats[:, :EXPERTS]
    mean_square = stats[:, EXPERTS:] / feature_count + EPSILON
    inv_rms = lax.rsqrt(mean_square)
    rms = mean_square * inv_rms
    normed = (wide_in * inv_rms * gain).astype(BF16)
    scores = jax.nn.sigmoid(plain_logits * inv_rms)
    chosen = picks * scores
    chosen_total = jnp.sum(chosen, axis=1, keepdims=True)
    route_weight = ROUTE_SCALE * chosen / chosen_total

    told = jnp.concatenate(
        [
            own_position[:, None, :],
            route_weight.T[:, None, :],
            jnp.broadcast_to(inv_rms.reshape(1, 1, tok_rows), (EXPERTS, 1, tok_rows)),
        ],
        axis=1,
    )
    told = lax.all_to_all(told, "ep", split_axis=0, concat_axis=0, tiled=True)
    told_path = jnp.dot(to_path, told.reshape(EXPERTS, 3 * tok_rows), precision=HIGHEST)
    told_path = told_path.reshape(GROUPS, SIDE, 3, tok_rows)
    position = told_path[:, :, 0].astype(jnp.int32)
    offset = (CAP * jnp.arange(SIDE, dtype=jnp.int32))[None, :, None]
    slot = jnp.where(position >= 0, position + offset, -1).reshape(GROUPS, 1, SIDE * tok_rows)
    own_told = told_path.reshape(2, SIDE, SIDE, 3, tok_rows)
    own_told = lax.dynamic_index_in_dim(own_told, tp, 1, keepdims=False)
    own_weight = own_told[:, :, 1].reshape(2, 1, SIDE * tok_rows)
    own_inv = own_told[:, :, 2].reshape(2, 1, SIDE * tok_rows)

    first = first_gather([hidden_in, out_grad])
    in_chunks = second_gather(first, 0, 2, [told])

    own, other = slice(0, SIDE), slice(SIDE, GROUPS)
    halves = (own, other)
    turn = (jnp.arange(SIDE, dtype=jnp.int32) + tp) % SIDE
    rows_in, both_terms, rows_grad, cot_terms = [], [], [], []
    for half in halves:
        rows, part = rows_through_in(
            slot[half], gain, w_gate, w_up, in_chunks[half], both_terms[:1]
        )
        rows_in.append(rows)
        both_terms.append(tp_exchange(part))
        if half is own:
            grad_chunks = second_gather(first, 1, 2, [part, in_chunks[-1]])
    units = shared_down.shape[0]
    shared_in = (jnp.concatenate([shared_gate.T, shared_up.T], axis=0).astype(F32) * gain).astype(
        BF16
    )
    shared_out = jnp.concatenate([shared_down, jnp.zeros((8, quarter), BF16)], axis=0)
    before = [part]
    for half in halves:
        rows, parts = rows_through_down(turn, slot[half], w_down, grad_chunks[half], before)
        rows_grad.append(rows)
        cot_terms.append(tp_terms(parts))
        if half is own:
            shared_first = shared_in_partials(shared_in, in_chunks, [parts[0]])
        before = [shared_first, both_terms[1]]
    hidden_part = parts[0]

    shared_parts = shared_partials(shared_out, shared_first, grad_chunks, [hidden_part])
    own_slot = jnp.stack(
        [lax.dynamic_index_in_dim(slot[half], tp, 0, keepdims=False) for half in halves]
    )
    own_hit = jnp.arange(ROWS, dtype=jnp.int32)[None, :, None] == own_slot
    row_scales = jnp.concatenate(
        [
            jnp.sum(jnp.where(own_hit, value, 0.0), axis=2, keepdims=True)
            for value in (own_weight, own_inv)
        ],
        axis=2,
    )
    both_cots, hiddens, row_cots, row_inners = [], (), [], []
    for n in range(2):
        both_cot, hidden, row_cot, row_inner = act(
            row_scales[n], both_terms[n], cot_terms[n], *hiddens, after=[shared_parts]
        )
        both_cots.append(tp_gather(both_cot))
        hiddens = (hidden,)
        row_cots.append(row_cot)
        row_inners.append(row_inner)
    s_line = jnp.arange(2, dtype=jnp.int32)[None, :]
    j_line = jnp.arange(SIDE, dtype=jnp.int32)
    j_col = j_line[:, None]
    return_expert = jnp.where(
        core == 0,
        (z * SIDE + (y + j_col) % SIDE) * 2 + s_line,
        (((z + j_col) % SIDE) * SIDE + y) * 2 + 1 - s_line,
    ).reshape(-1)
    pick_expert = (
        return_expert[:, None] == jnp.arange(EXPERTS, dtype=jnp.int32)[None, :]
    ).astype(F32)
    line_position = held(own_position, [hidden_part])
    line_position = jnp.stack(
        [line_position]
        + [lax.ppermute(line_position, "ep", first_hop(k)) for k in range(1, SIDE)]
    )
    position_here = jnp.einsum(
        "ket,me->ktm", line_position, pick_expert, precision=HIGHEST
    ).astype(jnp.int32)
    return_slot = jnp.where(
        position_here >= 0, position_here + (CAP * j_line)[:, None, None], -1
    ).reshape(SIDE * tok_rows, GROUPS)

    back, ordered_cots = [], []
    for n, before in ((0, row_cot), (1, return_slot)):
        ordered, rows = back_rows_of(turn, w_gate, w_up, both_cots[n], [before])
        ordered_cots.append(ordered)
        back.extend(rows)

    returned = []
    for j in range(SIDE):
        returned.append(back[j] if j == 0 else lax.ppermute(back[j], "ep", second_hop(-j)))
        returned.append(lax.ppermute(back[SIDE + j], "ep", swap_second_hop(-j)))
    summed = combine(return_slot, returned)
    routed_cot = summed[0].astype(F32)
    for k in range(1, SIDE):
        routed_cot = routed_cot + lax.ppermute(summed[k], "ep", first_hop(-k)).astype(F32)

    inner = shared_parts.shape[2]
    shared_sum = tp_scatter(shared_parts)
    gate_s = shared_sum[:, :units] * own_inv
    up_s = shared_sum[:, units : 2 * units] * own_inv
    hid_cot_s = shared_sum[:, 2 * units : 3 * units]
    gate_cot_s, up_cot_s = gate_grads(hid_cot_s, gate_s, up_s)

    def to_tokens(row_values):
        return jnp.sum(jnp.where(own_hit, jnp.stack(row_values), 0.0), axis=1, keepdims=True)

    shared_inner = jnp.sum(gate_cot_s * gate_s + up_cot_s * up_s, axis=1, keepdims=True)
    cots = jnp.concatenate(
        [
            gate_cot_s * own_inv,
            up_cot_s * own_inv,
            gate_s * jax.nn.sigmoid(gate_s) * up_s,
            to_tokens(row_cots),
            to_tokens(row_inners) + shared_inner,
            jnp.zeros((2, inner - 3 * units - 2, SIDE * tok_rows), F32),
        ],
        axis=1,
    ).astype(BF16)
    cots_all = tp_exchange(jnp.broadcast_to(cots[None], (SIDE,) + cots.shape))
    to_owner = by_owner(block_of, cots_all)
    to_owner = lax.all_to_all(to_owner, "ep", split_axis=0, concat_axis=0, tiled=True)
    shared_whole = lax.all_gather(
        held(shared_in, [hidden_part]), "ep", axis=0, tiled=True
    )
    shared_scaled = lax.dot_general(
        to_owner[:, : 2 * units].reshape(-1, tok_rows),
        shared_whole,
        (((0,), (0,)), ((), ())),
        preferred_element_type=F32,
    ) * rms

    sums = to_owner[:, 3 * units : 3 * units + 2].astype(F32)
    weight_cot = sums[:, 0].T
    chosen_cot = picks * (
        ROUTE_SCALE
        * (
            weight_cot / chosen_total
            - jnp.sum(weight_cot * chosen, axis=1, keepdims=True) / (chosen_total * chosen_total)
        )
    )
    logit_cot = chosen_cot * scores * (1.0 - scores)
    router_part = jnp.dot(logit_cot.T, normed.astype(F32), precision=HIGHEST)
    router_cot = jnp.dot(logit_cot, router_weight.T, precision=HIGHEST)
    inner_sum = jnp.sum(sums[:, 1], axis=0).reshape(tok_rows, 1) * rms + jnp.sum(
        logit_cot * plain_logits, axis=1, keepdims=True
    )

    scaled = (routed_cot * rms + router_cot) * gain + shared_scaled
    input_cot = inv_rms * scaled - wide_in * (inv_rms * inv_rms * inv_rms) * (
        inner_sum / feature_count
    )
    dense_cot = (out_grad.astype(F32) + input_cot).astype(BF16)

    grads_in, grads_down = shared_grads(
        cots_all, gain, in_chunks, grad_chunks, 2 * units, [dense_cot]
    )
    cot_chunks = second_gather(first_gather([dense_cot]), 0, 1, [grads_in])
    gate_t, up_t = dense_gate.T, dense_up.T
    hidden2 = (jax.nn.silu(gate_t.astype(F32)) * up_t.astype(F32)).astype(BF16)

    def flat(parts, columns=slice(None)):
        whole = jnp.concatenate([part[:, :, columns] for part in parts], axis=1)
        return whole.reshape(GROUPS * ROWS, -1)

    def rows_dot(left, right):
        return lax.dot_general(
            left, right, (((0,), (0,)), ((), ())), preferred_element_type=F32
        ).astype(BF16)[None]

    units_r = w_gate.shape[1]
    rows_in = flat(rows_in)
    grad_expert_gate = rows_dot(rows_in, flat(ordered_cots, slice(0, units_r)))
    grad_expert_up = rows_dot(rows_in, flat(ordered_cots, slice(units_r, None)))
    rows_grad = flat(rows_grad)
    hidden_all = tp_exchange(held(hiddens[0], [to_owner])).reshape(GROUPS * ROWS, -1)

    dense_place = (block_z * SIDE + block_y).reshape(2, -1)
    own_part = dense_hidden(
        dense_place[0], dense_down, cot_chunks[own], [hidden_all, grad_expert_gate, grad_expert_up, rows_grad]
    )
    own_terms = tp_exchange(own_part)
    turned = (((block_z - tp) % SIDE) * SIDE + block_y).reshape(2, -1)
    hidden2_part = dense_hidden(turned[1], dense_down, cot_chunks[other])
    own_sum = term_sum(own_terms, [hidden2_part])
    other_sum = sum(term.astype(F32) for term in tp_terms(list(hidden2_part)))

    def by_core(mine, others):
        both = jnp.where(core == 0, jnp.stack([mine, others]), jnp.stack([others, mine]))
        both = both.reshape(2, mine.shape[0], SIDE, tok_rows).transpose(1, 2, 0, 3)
        return both.reshape(mine.shape[0], -1)

    hidden2_cot = by_core(own_sum, other_sum)
    share = 8 * tok_rows
    gate_mine = lax.dynamic_slice_in_dim(gate_t, tp * share, share, 1).astype(F32)
    up_mine = lax.dynamic_slice_in_dim(up_t, tp * share, share, 1).astype(F32)
    grad_gate2, grad_up2 = gate_grads(hidden2_cot, gate_mine, up_mine)
    grad_dense_down = dense_grad(block_of, hidden2, cot_chunks, [hidden2_part])
    grad_router = ep_sum(
        router_part, (dense_cot, hidden2_part, hidden2_part, grad_dense_down, grad_dense_down)
    ).T
    return (
        grad_gate2.astype(BF16).T,
        grad_up2.astype(BF16).T,
        grad_dense_down,
        grad_expert_gate,
        grad_expert_up,
        rows_dot(held(hidden_all, [hidden2_part]), rows_grad),
        grads_in[:units].T,
        grads_in[units:].T,
        grads_down[:units],
        grad_router,
    )


def solution(mesh):
    in_specs = (
        P("ep", "tp"),
        P("ep", "tp"),
        P("tp"),
        P("tp", None),
        P("ep", None),
        P("ep", "tp", None),
        P("ep", "tp", None),
        P("ep", None, "tp"),
        P("tp", "ep"),
        P("tp", "ep"),
        P("ep", "tp"),
        P(None, "ep"),
        P(None, "ep"),
        P("ep", "tp"),
    )
    out_specs = (
        P("tp", "ep"),
        P("tp", "ep"),
        P("ep", "tp"),
        P("ep", "tp", None),
        P("ep", "tp", None),
        P("ep", None, "tp"),
        P("tp", "ep"),
        P("tp", "ep"),
        P("ep", "tp"),
        P("tp", None),
    )
    return jax.shard_map(local, mesh=mesh, in_specs=in_specs, out_specs=out_specs, check_vma=False)
```

```python
import functools

import jax
import jax.numpy as jnp
from jax import lax
from jax.experimental import pallas as pl
from jax.experimental.pallas import tpu as pltpu
from jax.sharding import PartitionSpec as P

EXPERTS = 32
TOP = 8
CAP = 36
SIDE = 4
GROUPS = 8
ROWS = SIDE * CAP

EPSILON = 1e-05
ROUTE_SCALE = 2.5
F32 = jnp.float32
BF16 = jnp.bfloat16
HIGHEST = lax.Precision.HIGHEST
VMEM_BYTES = 50 * 1024 * 1024


def ep_at(z, y, core):
    return ((z % SIDE) * SIDE + y % SIDE) * 2 + core


def ep_pairs(target):
    return [
        (ep_at(z, y, core), target(z, y, core))
        for z in range(SIDE)
        for y in range(SIDE)
        for core in range(2)
    ]


def first_hop(k):
    return ep_pairs(lambda z, y, core: ep_at(z, y + k, 1) if core else ep_at(z + k, y, 0))


def first_lines():
    core_0 = [[ep_at(z, y, 0) for z in range(SIDE)] for y in range(SIDE)]
    return core_0 + [[ep_at(z, y, 1) for y in range(SIDE)] for z in range(SIDE)]


def second_hop(k):
    return ep_pairs(lambda z, y, core: ep_at(z + k, y, 1) if core else ep_at(z, y + k, 0))


def swap_second_hop(k):
    return ep_pairs(lambda z, y, core: ep_at(z, y + k, 0) if core else ep_at(z + k, y, 1))


def core_swap():
    return ep_pairs(lambda z, y, core: ep_at(z, y, 1 - core))


def tp_hop(k):
    return [(i, (i + k) % SIDE) for i in range(SIDE)]


def join_kernel(first, count, *refs):
    blocks, out = refs[:SIDE], refs[SIDE]
    rows = out.shape[0] // SIDE
    for i in range(SIDE):
        out[i * rows : (i + 1) * rows] = blocks[i][first : first + rows]


def join(blocks, number, count, after):
    rows, width = blocks[0].shape[0] // count, blocks[0].shape[1]
    return local_call(
        functools.partial(join_kernel, number * rows, count),
        jax.ShapeDtypeStruct((SIDE * rows, width), blocks[0].dtype),
        vmem(SIDE),
        0,
        4 * SIDE * rows * width,
        after=after,
    )(*blocks)


def first_gather(blocks):
    stack = jnp.concatenate(blocks, axis=0) if len(blocks) > 1 else blocks[0]
    return [stack] + [lax.ppermute(stack, "ep", first_hop(k)) for k in range(1, SIDE)]


def second_gather(first, number, count, after):
    joined = join(first, number, count, after)
    own = [joined] + [lax.ppermute(joined, "ep", second_hop(k)) for k in range(1, SIDE)]
    return own + [lax.ppermute(chunk, "ep", core_swap()) for chunk in own]


def add_kernel(first, second, out):
    out[...] = first[...] + second[...]


def ep_sum(value, stages):
    pairings = ((0, 0, 1), (0, 1, 0), (1, 0, 0), (0, 2, 0), (2, 0, 0))
    shape = jax.ShapeDtypeStruct(value.shape, value.dtype)
    for (dz, dy, dcore), stage in zip(pairings, stages, strict=True):
        pairs = ep_pairs(lambda z, y, core: ep_at(z ^ dz, y ^ dy, core ^ dcore))
        met = lax.ppermute(value, "ep", pairs)
        value = local_call(add_kernel, shape, vmem(2), 0, 12 * value.size, after=[stage])(
            value, met
        )
    return value


def tp_gather(piece):
    return [piece] + [lax.ppermute(piece, "tp", tp_hop(-k)) for k in (1, 2, 3)]


def tp_terms(parts):
    return [parts[0]] + [lax.ppermute(parts[k], "tp", tp_hop(k)) for k in (1, 3, 2)]


def tp_exchange(parts):
    return lax.all_to_all(parts, "tp", split_axis=0, concat_axis=0, tiled=True)


def tp_scatter(parts):
    return jnp.sum(tp_exchange(parts).astype(F32), axis=0)


def vmem(count):
    return [pl.BlockSpec(memory_space=pltpu.VMEM)] * count


def smem():
    return pl.BlockSpec(memory_space=pltpu.SMEM)


def local_call(body, out_shape, in_specs, flops, moved, scratch=(), after=()):
    many = isinstance(out_shape, (list, tuple))
    count = len(in_specs)

    def ordered(*refs):
        body(*refs[:count], *refs[count + len(after) :])

    call = pl.pallas_call(
        ordered,
        out_shape=out_shape,
        in_specs=list(in_specs) + [pl.BlockSpec(memory_space=pl.ANY)] * len(after),
        out_specs=vmem(len(out_shape)) if many else vmem(1)[0],
        scratch_shapes=list(scratch),
        cost_estimate=pl.CostEstimate(flops=flops, bytes_accessed=moved, transcendentals=0),
        compiler_params=pltpu.CompilerParams(vmem_limit_bytes=VMEM_BYTES),
    )
    return lambda *operands: call(*operands, *after)


def held_kernel(value, out):
    out[...] = value[...]


def held(value, after):
    shape = jax.ShapeDtypeStruct(value.shape, value.dtype)
    moved = 2 * value.size * value.dtype.itemsize
    return local_call(held_kernel, shape, vmem(1), 0, moved, after=after)(value)


def nt_dot(left, right):
    return lax.dot_general(left, right, (((1,), (1,)), ((), ())), preferred_element_type=F32)


def pick_rows(slot, chunk, gain=None):
    hit = lax.broadcasted_iota(jnp.int32, (ROWS, chunk.shape[0]), 0) == slot
    pick = jnp.where(hit, 1.0, 0.0).astype(BF16)
    rows = jnp.dot(pick, chunk[...], preferred_element_type=F32)
    return (rows if gain is None else rows * gain).astype(BF16)


def store_groups(out, columns, value):
    for k in range(SIDE):
        out[k, :, columns] = value[k * ROWS : (k + 1) * ROWS].astype(BF16)


TILE = 256


def in_kernel(slot, gain, w_gate, w_up, *refs):
    chunks, (rows, both) = refs[:SIDE], refs[SIDE:]
    for k in range(SIDE):
        rows[k] = pick_rows(slot[k], chunks[k], gain[...])
    units = w_gate.shape[1]

    def step(n, unused):
        left = rows[...].reshape(SIDE * ROWS, -1)
        for at, weights in ((0, w_gate), (units, w_up)):
            columns = pl.ds(pl.multiple_of(n * TILE, TILE), TILE)
            target = pl.ds(pl.multiple_of(at + n * TILE, TILE), TILE)
            value = jnp.dot(left, weights[:, columns], preferred_element_type=F32)
            store_groups(both, target, value)
        return unused

    lax.fori_loop(0, units // TILE, step, 0)


def rows_through_in(slot, gain, w_gate, w_up, chunks, after=()):
    tokens, width = chunks[0].shape
    units = w_gate.shape[1]
    return local_call(
        in_kernel,
        [
            jax.ShapeDtypeStruct((SIDE, ROWS, width), BF16),
            jax.ShapeDtypeStruct((SIDE, ROWS, 2 * units), BF16),
        ],
        vmem(4 + SIDE),
        2 * SIDE * ROWS * width * (tokens + 2 * units),
        2 * width * (SIDE * (tokens + ROWS) + 2 * units),
        after=after,
    )(slot, gain, w_gate, w_up, *chunks)


def grad_kernel(place, slot, w_down, *refs):
    chunks, rows, parts = refs[:SIDE], refs[SIDE], refs[SIDE + 1 :]
    for k in range(SIDE):
        rows[k] = pick_rows(slot[k], chunks[k])

    def step(n, unused):
        left = jnp.concatenate([rows[place[k]] for k in range(SIDE)], axis=0)
        columns = pl.ds(pl.multiple_of(n * TILE, TILE), TILE)
        value = nt_dot(left, w_down[columns, :]).astype(BF16)
        for k in range(SIDE):
            parts[k][:, columns] = value[k * ROWS : (k + 1) * ROWS]
        return unused

    lax.fori_loop(0, w_down.shape[0] // TILE, step, 0)


def rows_through_down(place, slot, w_down, chunks, after=()):
    tokens, width = chunks[0].shape
    units = w_down.shape[0]
    rows, *parts = local_call(
        grad_kernel,
        [jax.ShapeDtypeStruct((SIDE, ROWS, width), BF16)]
        + [jax.ShapeDtypeStruct((ROWS, units), BF16)] * SIDE,
        [smem()] + vmem(2 + SIDE),
        2 * SIDE * ROWS * width * (tokens + units),
        2 * width * (SIDE * (tokens + ROWS) + units),
        after=after,
    )(place, slot, w_down, *chunks)
    return rows, parts


def back_kernel(place, w_gate, w_up, *refs):
    pieces, cots, out = refs[:SIDE], refs[SIDE], refs[SIDE + 1 :]
    units = w_gate.shape[1]
    for k in range(SIDE):
        cots[place[k]] = pieces[k][...]

    def step(n, unused):
        columns = pl.ds(pl.multiple_of(n * TILE, TILE), TILE)
        left = cots[...].reshape(SIDE * ROWS, 2 * units)
        rows = nt_dot(left[:, :units], w_gate[columns, :])
        rows = (rows + nt_dot(left[:, units:], w_up[columns, :])).astype(BF16)
        for k in range(SIDE):
            out[k][:, columns] = rows[k * ROWS : (k + 1) * ROWS]
        return unused

    lax.fori_loop(0, w_gate.shape[0] // TILE, step, 0)


def back_rows_of(place, w_gate, w_up, pieces, after):
    width, units = w_gate.shape
    cots, *back = local_call(
        back_kernel,
        [jax.ShapeDtypeStruct((SIDE, ROWS, 2 * units), BF16)]
        + [jax.ShapeDtypeStruct((ROWS, width), BF16)] * SIDE,
        [smem()] + vmem(2 + SIDE),
        4 * SIDE * ROWS * units * width,
        2 * (2 * SIDE * ROWS * units + 2 * units * width + SIDE * ROWS * width),
        after=after,
    )(place, w_gate, w_up, *pieces)
    return cots, back


def act_kernel(scales, gate_ups, *refs):
    cots, hidden_before = refs[:SIDE], refs[SIDE:-4]
    cot_out, hidden_out, row_cot, row_inner = refs[-4:]
    tile = 48
    count, width = cots[0].shape

    def step(n, unused):
        rows = pl.ds(pl.multiple_of(n * tile, tile), tile)

        def total(columns):
            return sum(gate_ups[k, rows, columns].astype(F32) for k in range(SIDE))

        weight, inv = scales[rows, 0:1], scales[rows, 1:2]
        gate = total(slice(0, width)) * inv
        up = total(slice(width, 2 * width)) * inv
        cot = sum(term[rows, :].astype(F32) for term in cots)
        sigma = 1.0 / (1.0 + jnp.exp(-gate))
        silu = gate * sigma
        hidden = silu * up
        row_cot[rows, :] = jnp.sum(cot * hidden, axis=1, keepdims=True)
        cot = cot * weight
        gate_cot = cot * up * (sigma + silu * (1.0 - sigma))
        up_cot = cot * silu
        row_inner[rows, :] = jnp.sum(gate_cot * gate + up_cot * up, axis=1, keepdims=True)
        cot_out[rows, :width] = (gate_cot * inv).astype(BF16)
        cot_out[rows, width:] = (up_cot * inv).astype(BF16)
        hidden = (hidden * weight).astype(BF16)
        if hidden_before:
            later = pl.ds(pl.multiple_of(count + n * tile, 16), tile)
            for k in range(SIDE):
                hidden_out[k, rows, :] = hidden_before[0][rows, :]
                hidden_out[k, later, :] = hidden
        else:
            hidden_out[rows, :] = hidden
        return unused

    lax.fori_loop(0, scales.shape[0] // tile, step, 0)


def act(scales, gate_ups, cots, *hidden_before, after):
    rows, hidden = cots[0].shape
    hidden_shape = (SIDE, 2 * rows, hidden) if hidden_before else (rows, hidden)
    return local_call(
        act_kernel,
        [
            jax.ShapeDtypeStruct((rows, 2 * hidden), BF16),
            jax.ShapeDtypeStruct(hidden_shape, BF16),
        ]
        + [jax.ShapeDtypeStruct((rows, 1), F32)] * 2,
        vmem(2 + SIDE + len(hidden_before)),
        40 * rows * hidden,
        48 * rows * hidden,
        after=after,
    )(scales, gate_ups, *cots, *hidden_before)


def combine_kernel(slots, *refs):
    rows, out, pick = refs[:GROUPS], refs[GROUPS:-1], refs[-1]
    tokens = slots.shape[0]
    block = tokens // SIDE
    for m in range(GROUPS):
        hit = lax.broadcasted_iota(jnp.int32, (tokens, ROWS), 1) == slots[:, m : m + 1]
        pick[m] = jnp.where(hit, 1.0, 0.0).astype(BF16)

    def step(n, unused):
        columns = pl.ds(pl.multiple_of(n * TILE, TILE), TILE)
        total = jnp.dot(pick[0], rows[0][:, columns], preferred_element_type=F32)
        for m in range(1, GROUPS):
            total = total + jnp.dot(pick[m], rows[m][:, columns], preferred_element_type=F32)
        total = total.astype(BF16)
        for k in range(SIDE):
            out[k][:, columns] = total[k * block : (k + 1) * block]
        return unused

    lax.fori_loop(0, rows[0].shape[1] // TILE, step, 0)


def combine(slots, rows):
    tokens, width = slots.shape[0], rows[0].shape[1]
    return local_call(
        combine_kernel,
        [jax.ShapeDtypeStruct((tokens // SIDE, width), BF16)] * SIDE,
        vmem(1 + GROUPS),
        2 * GROUPS * ROWS * tokens * width,
        2 * (GROUPS * ROWS + tokens) * width,
        [pltpu.VMEM((GROUPS, tokens, ROWS), BF16)],
    )(slots, *rows)


def shared_in_kernel(weights, *refs):
    ins, out = refs[:GROUPS], refs[GROUPS]
    for g in range(GROUPS):
        out[g % SIDE, g // SIDE] = nt_dot(weights[...], ins[g][...]).astype(BF16)


def shared_in_partials(weights, ins, after):
    tokens, width = ins[0].shape
    hidden = weights.shape[0]
    return local_call(
        shared_in_kernel,
        jax.ShapeDtypeStruct((SIDE, 2, hidden, tokens), BF16),
        vmem(1 + GROUPS),
        2 * GROUPS * tokens * width * hidden // 8,
        2 * GROUPS * tokens * width // 8,
        after=after,
    )(weights, *ins)


def shared_kernel(weights, first, *refs):
    grads, out = refs[:GROUPS], refs[GROUPS]
    top = first.shape[2]
    out[:, :, :top] = first[...]
    for g in range(GROUPS):
        out[g % SIDE, g // SIDE, top:] = nt_dot(weights[...], grads[g][...]).astype(BF16)


def shared_partials(weights, first, grads, after):
    tokens, width = grads[0].shape
    hidden = first.shape[2] + weights.shape[0]
    return local_call(
        shared_kernel,
        jax.ShapeDtypeStruct((SIDE, 2, hidden, tokens), BF16),
        vmem(2 + GROUPS),
        2 * GROUPS * tokens * width * hidden,
        2 * GROUPS * tokens * width,
        after=after,
    )(weights, first, *grads)


def shared_grad_kernel(cots, gain, *refs):
    ins, grads = refs[:GROUPS], refs[GROUPS : 2 * GROUPS]
    out_in, out_down, sum_in, sum_down = refs[2 * GROUPS :]
    top = out_in.shape[0]
    for g in range(GROUPS):
        cot = cots[g % SIDE, g // SIDE]
        first = jnp.dot(cot[:top], ins[g][...], preferred_element_type=F32)
        second = jnp.dot(cot[top:], grads[g][...], preferred_element_type=F32)
        sum_in[...] = first if g == 0 else sum_in[...] + first
        sum_down[...] = second if g == 0 else sum_down[...] + second
    out_in[...] = (sum_in[...] * gain[...]).astype(BF16)
    out_down[...] = sum_down[...].astype(BF16)


def shared_grads(cots, gain, ins, grads, top, after):
    tokens, width = ins[0].shape
    rest = cots.shape[2] - top
    return local_call(
        shared_grad_kernel,
        [jax.ShapeDtypeStruct((top, width), BF16), jax.ShapeDtypeStruct((rest, width), BF16)],
        vmem(2 + 2 * GROUPS),
        2 * GROUPS * tokens * width * (top + rest),
        4 * GROUPS * tokens * width,
        [pltpu.VMEM((top, width), F32), pltpu.VMEM((rest, width), F32)],
        after,
    )(cots, gain, *ins, *grads)


def owner_kernel(place, cots, out):
    block = out.shape[2]
    for g in range(GROUPS):
        for i in range(SIDE):
            out[place[g * SIDE + i]] = cots[g % SIDE, g // SIDE, :, i * block : (i + 1) * block]


def by_owner(place, cots):
    rows, tokens = cots.shape[2:]
    return local_call(
        owner_kernel,
        jax.ShapeDtypeStruct((GROUPS * SIDE, rows, tokens // SIDE), BF16),
        [smem()] + vmem(1),
        0,
        4 * GROUPS * rows * tokens,
    )(place, cots)


def dense_hidden_kernel(place, w_down, *refs):
    chunks, out = refs[:SIDE], refs[SIDE]
    block = chunks[0].shape[0] // SIDE
    for g in range(SIDE):
        columns = nt_dot(w_down[...], chunks[g][...]).astype(BF16)
        for i in range(SIDE):
            at = place[g * SIDE + i]
            lane = pl.multiple_of(lax.rem(at, SIDE) * block, block)
            out[lax.div(at, SIDE), :, pl.ds(lane, block)] = columns[
                :, i * block : (i + 1) * block
            ]


def dense_hidden(place, w_down, chunks, after=()):
    tokens, width = chunks[0].shape
    hidden = w_down.shape[0]
    return local_call(
        dense_hidden_kernel,
        jax.ShapeDtypeStruct((SIDE, hidden, tokens), BF16),
        [smem()] + vmem(1 + SIDE),
        2 * SIDE * tokens * width * hidden,
        2 * SIDE * tokens * width,
        after=after,
    )(place, w_down, *chunks)


def dense_grad_kernel(place, hidden, *refs):
    chunks, out, total = refs[:GROUPS], refs[GROUPS], refs[GROUPS + 1]
    block = chunks[0].shape[0] // SIDE
    for g in range(GROUPS):
        left = jnp.concatenate(
            [
                hidden[:, pl.ds(pl.multiple_of(place[g * SIDE + i] * block, block), block)]
                for i in range(SIDE)
            ],
            axis=1,
        )
        term = jnp.dot(left, chunks[g][...], preferred_element_type=F32)
        total[...] = term if g == 0 else total[...] + term
    out[...] = total[...].astype(BF16)


def dense_grad(place, hidden, chunks, after):
    tokens, width = chunks[0].shape
    units = hidden.shape[0]
    return local_call(
        dense_grad_kernel,
        jax.ShapeDtypeStruct((units, width), BF16),
        [smem()] + vmem(1 + GROUPS),
        2 * GROUPS * tokens * width * units,
        2 * GROUPS * tokens * width,
        [pltpu.VMEM((units, width), F32)],
        after,
    )(place, hidden, *chunks)


def gate_grads(hidden_cot, gate_value, up_value):
    sigma = jax.nn.sigmoid(gate_value)
    gate_cot = hidden_cot * up_value * sigma * (1.0 + gate_value * (1.0 - sigma))
    up_cot = hidden_cot * gate_value * sigma
    return (gate_cot, up_cot)


def local(
    hidden_in,
    out_grad,
    norm_gain,
    router_weight,
    route_ids,
    expert_gate,
    expert_up,
    expert_down,
    shared_gate,
    shared_up,
    shared_down,
    dense_gate,
    dense_up,
    dense_down,
):
    tok_rows, quarter = hidden_in.shape
    feature_count = quarter * lax.axis_size("tp")
    ep, tp = lax.axis_index("ep"), lax.axis_index("tp")
    z, y, core = ep // 8, (ep // 2) % SIDE, ep % 2
    w_gate, w_up, w_down = expert_gate[0], expert_up[0], expert_down[0]
    gain = norm_gain[None, :]

    g_at = jnp.arange(GROUPS, dtype=jnp.int32)[:, None]
    i_at = jnp.arange(SIDE, dtype=jnp.int32)[None, :]
    j_at = g_at % SIDE
    block_core = (core + g_at // SIDE) % 2
    block_z = jnp.where(block_core == 0, z - i_at, z - j_at) % SIDE
    block_y = jnp.where(block_core == 0, y - j_at, y - i_at) % SIDE
    block_of = ((block_z * SIDE + block_y) * 2 + block_core).reshape(-1)
    to_path = (block_of[:, None] == jnp.arange(EXPERTS, dtype=jnp.int32)[None, :]).astype(F32)

    picks = jnp.any(
        route_ids[:, :, None] == jnp.arange(EXPERTS, dtype=jnp.int32)[None, None, :], axis=1
    ).astype(F32)
    token_line = jnp.arange(tok_rows, dtype=jnp.int32)
    earlier = (token_line[:, None] < token_line[None, :]).astype(F32)
    own_position = jnp.dot(picks.T, earlier, precision=HIGHEST)
    own_position = jnp.where(picks.T > 0.0, own_position, -1.0)
    wide_in = hidden_in.astype(F32)
    square_part = jnp.sum(wide_in * wide_in, axis=1, keepdims=True)
    logit_part = jnp.dot(wide_in * gain, router_weight, precision=HIGHEST)
    stats = jnp.concatenate([logit_part, square_part], axis=1)
    stats = tp_scatter(jnp.broadcast_to(stats[None], (SIDE,) + stats.shape))
    plain_logits = stats[:, :EXPERTS]
    mean_square = stats[:, EXPERTS:] / feature_count + EPSILON
    inv_rms = lax.rsqrt(mean_square)
    rms = mean_square * inv_rms
    normed = (wide_in * inv_rms * gain).astype(BF16)
    scores = jax.nn.sigmoid(plain_logits * inv_rms)
    chosen = picks * scores
    chosen_total = jnp.sum(chosen, axis=1, keepdims=True)
    route_weight = ROUTE_SCALE * chosen / chosen_total

    told = jnp.concatenate(
        [
            own_position[:, None, :],
            route_weight.T[:, None, :],
            jnp.broadcast_to(inv_rms.reshape(1, 1, tok_rows), (EXPERTS, 1, tok_rows)),
        ],
        axis=1,
    )
    told = lax.all_to_all(told, "ep", split_axis=0, concat_axis=0, tiled=True)
    told_path = jnp.dot(to_path, told.reshape(EXPERTS, 3 * tok_rows), precision=HIGHEST)
    told_path = told_path.reshape(GROUPS, SIDE, 3, tok_rows)
    position = told_path[:, :, 0].astype(jnp.int32)
    offset = (CAP * jnp.arange(SIDE, dtype=jnp.int32))[None, :, None]
    slot = jnp.where(position >= 0, position + offset, -1).reshape(GROUPS, 1, SIDE * tok_rows)
    own_told = told_path.reshape(2, SIDE, SIDE, 3, tok_rows)
    own_told = lax.dynamic_index_in_dim(own_told, tp, 1, keepdims=False)
    own_weight = own_told[:, :, 1].reshape(2, 1, SIDE * tok_rows)
    own_inv = own_told[:, :, 2].reshape(2, 1, SIDE * tok_rows)

    first = first_gather([hidden_in, out_grad])
    in_chunks = second_gather(first, 0, 2, [told])

    own, other = slice(0, SIDE), slice(SIDE, GROUPS)
    halves = (own, other)
    turn = (jnp.arange(SIDE, dtype=jnp.int32) + tp) % SIDE
    rows_in, both_terms, rows_grad, cot_terms = [], [], [], []
    for half in halves:
        rows, part = rows_through_in(
            slot[half], gain, w_gate, w_up, in_chunks[half], both_terms[:1]
        )
        rows_in.append(rows)
        both_terms.append(tp_exchange(part))
        if half is own:
            grad_chunks = second_gather(first, 1, 2, [part, in_chunks[-1]])
    units = shared_down.shape[0]
    shared_in = (jnp.concatenate([shared_gate.T, shared_up.T], axis=0).astype(F32) * gain).astype(
        BF16
    )
    shared_out = jnp.concatenate([shared_down, jnp.zeros((8, quarter), BF16)], axis=0)
    before = [part]
    for half in halves:
        rows, parts = rows_through_down(turn, slot[half], w_down, grad_chunks[half], before)
        rows_grad.append(rows)
        cot_terms.append(tp_terms(parts))
        if half is own:
            shared_first = shared_in_partials(shared_in, in_chunks, [parts[0]])
        before = [shared_first, both_terms[1]]
    hidden_part = parts[0]

    shared_parts = shared_partials(shared_out, shared_first, grad_chunks, [hidden_part])
    own_slot = jnp.stack(
        [lax.dynamic_index_in_dim(slot[half], tp, 0, keepdims=False) for half in halves]
    )
    own_hit = jnp.arange(ROWS, dtype=jnp.int32)[None, :, None] == own_slot
    row_scales = jnp.concatenate(
        [
            jnp.sum(jnp.where(own_hit, value, 0.0), axis=2, keepdims=True)
            for value in (own_weight, own_inv)
        ],
        axis=2,
    )
    both_cots, hiddens, row_cots, row_inners = [], (), [], []
    for n in range(2):
        both_cot, hidden, row_cot, row_inner = act(
            row_scales[n], both_terms[n], cot_terms[n], *hiddens, after=[shared_parts]
        )
        both_cots.append(tp_gather(both_cot))
        hiddens = (hidden,)
        row_cots.append(row_cot)
        row_inners.append(row_inner)
    s_line = jnp.arange(2, dtype=jnp.int32)[None, :]
    j_line = jnp.arange(SIDE, dtype=jnp.int32)
    j_col = j_line[:, None]
    return_expert = jnp.where(
        core == 0,
        (z * SIDE + (y + j_col) % SIDE) * 2 + s_line,
        (((z + j_col) % SIDE) * SIDE + y) * 2 + 1 - s_line,
    ).reshape(-1)
    pick_expert = (
        return_expert[:, None] == jnp.arange(EXPERTS, dtype=jnp.int32)[None, :]
    ).astype(F32)
    line_position = held(own_position, [hidden_part])
    line_position = jnp.stack(
        [line_position]
        + [lax.ppermute(line_position, "ep", first_hop(k)) for k in range(1, SIDE)]
    )
    position_here = jnp.einsum(
        "ket,me->ktm", line_position, pick_expert, precision=HIGHEST
    ).astype(jnp.int32)
    return_slot = jnp.where(
        position_here >= 0, position_here + (CAP * j_line)[:, None, None], -1
    ).reshape(SIDE * tok_rows, GROUPS)

    back, ordered_cots = [], []
    for n, before in ((0, row_cot), (1, return_slot)):
        ordered, rows = back_rows_of(turn, w_gate, w_up, both_cots[n], [before])
        ordered_cots.append(ordered)
        back.extend(rows)

    returned = []
    for j in range(SIDE):
        returned.append(back[j] if j == 0 else lax.ppermute(back[j], "ep", second_hop(-j)))
        returned.append(lax.ppermute(back[SIDE + j], "ep", swap_second_hop(-j)))
    summed = combine(return_slot, returned)
    routed_cot = summed[0].astype(F32)
    for k in range(1, SIDE):
        routed_cot = routed_cot + lax.ppermute(summed[k], "ep", first_hop(-k)).astype(F32)

    inner = shared_parts.shape[2]
    shared_sum = tp_scatter(shared_parts)
    gate_s = shared_sum[:, :units] * own_inv
    up_s = shared_sum[:, units : 2 * units] * own_inv
    hid_cot_s = shared_sum[:, 2 * units : 3 * units]
    gate_cot_s, up_cot_s = gate_grads(hid_cot_s, gate_s, up_s)

    def to_tokens(row_values):
        return jnp.sum(jnp.where(own_hit, jnp.stack(row_values), 0.0), axis=1, keepdims=True)

    shared_inner = jnp.sum(gate_cot_s * gate_s + up_cot_s * up_s, axis=1, keepdims=True)
    cots = jnp.concatenate(
        [
            gate_cot_s * own_inv,
            up_cot_s * own_inv,
            gate_s * jax.nn.sigmoid(gate_s) * up_s,
            to_tokens(row_cots),
            to_tokens(row_inners) + shared_inner,
            jnp.zeros((2, inner - 3 * units - 2, SIDE * tok_rows), F32),
        ],
        axis=1,
    ).astype(BF16)
    cots_all = tp_exchange(jnp.broadcast_to(cots[None], (SIDE,) + cots.shape))
    to_owner = by_owner(block_of, cots_all)
    to_owner = lax.all_to_all(to_owner, "ep", split_axis=0, concat_axis=0, tiled=True)
    shared_whole = lax.all_gather(
        held(shared_in, [hidden_part]), "ep", axis=0, tiled=True
    )
    shared_scaled = lax.dot_general(
        to_owner[:, : 2 * units].reshape(-1, tok_rows),
        shared_whole,
        (((0,), (0,)), ((), ())),
        preferred_element_type=F32,
    ) * rms

    sums = to_owner[:, 3 * units : 3 * units + 2].astype(F32)
    weight_cot = sums[:, 0].T
    chosen_cot = picks * (
        ROUTE_SCALE
        * (
            weight_cot / chosen_total
            - jnp.sum(weight_cot * chosen, axis=1, keepdims=True) / (chosen_total * chosen_total)
        )
    )
    logit_cot = chosen_cot * scores * (1.0 - scores)
    router_part = jnp.dot(logit_cot.T, normed.astype(F32), precision=HIGHEST)
    router_cot = jnp.dot(logit_cot, router_weight.T, precision=HIGHEST)
    inner_sum = jnp.sum(sums[:, 1], axis=0).reshape(tok_rows, 1) * rms + jnp.sum(
        logit_cot * plain_logits, axis=1, keepdims=True
    )

    scaled = (routed_cot * rms + router_cot) * gain + shared_scaled
    input_cot = inv_rms * scaled - wide_in * (inv_rms * inv_rms * inv_rms) * (
        inner_sum / feature_count
    )
    dense_cot = (out_grad.astype(F32) + input_cot).astype(BF16)

    cot_chunks = second_gather(first_gather([dense_cot]), 0, 1, [])
    gate_t, up_t = dense_gate.T, dense_up.T
    hidden2 = (jax.nn.silu(gate_t.astype(F32)) * up_t.astype(F32)).astype(BF16)

    def flat(parts, columns=slice(None)):
        whole = jnp.concatenate([part[:, :, columns] for part in parts], axis=1)
        return whole.reshape(GROUPS * ROWS, -1)

    def rows_dot(left, right):
        return lax.dot_general(
            left, right, (((0,), (0,)), ((), ())), preferred_element_type=F32
        ).astype(BF16)[None]

    grads_in, grads_down = shared_grads(
        cots_all, gain, in_chunks, grad_chunks, 2 * units, [summed[0]]
    )
    units_r = w_gate.shape[1]
    rows_in = flat(rows_in)
    grad_expert_gate = rows_dot(rows_in, flat(ordered_cots, slice(0, units_r)))
    hidden_all = tp_exchange(held(hiddens[0], [to_owner])).reshape(GROUPS * ROWS, -1)

    dense_place = (block_z * SIDE + block_y).reshape(2, -1)
    own_part = dense_hidden(
        dense_place[0], dense_down, cot_chunks[own], [hidden_all]
    )
    own_sum = tp_scatter(own_part)
    turned = (((block_z - tp) % SIDE) * SIDE + block_y).reshape(2, -1)
    hidden2_part = dense_hidden(turned[1], dense_down, cot_chunks[other])
    other_sum = sum(term.astype(F32) for term in tp_terms(list(hidden2_part)))

    def by_core(mine, others):
        both = jnp.where(core == 0, jnp.stack([mine, others]), jnp.stack([others, mine]))
        both = both.reshape(2, mine.shape[0], SIDE, tok_rows).transpose(1, 2, 0, 3)
        return both.reshape(mine.shape[0], -1)

    hidden2_cot = by_core(own_sum, other_sum)
    share = 8 * tok_rows
    gate_mine = lax.dynamic_slice_in_dim(gate_t, tp * share, share, 1).astype(F32)
    up_mine = lax.dynamic_slice_in_dim(up_t, tp * share, share, 1).astype(F32)
    grad_gate2, grad_up2 = gate_grads(hidden2_cot, gate_mine, up_mine)
    grad_dense_down = dense_grad(block_of, hidden2, cot_chunks, [hidden2_part])
    grad_router = ep_sum(
        router_part, (dense_cot, own_part, hidden2_part, hidden2_part, grad_dense_down)
    ).T
    return (
        grad_gate2.astype(BF16).T,
        grad_up2.astype(BF16).T,
        grad_dense_down,
        grad_expert_gate,
        rows_dot(rows_in, flat(ordered_cots, slice(units_r, None))),
        rows_dot(hidden_all, flat(rows_grad)),
        grads_in[:units].T,
        grads_in[units:].T,
        grads_down[:units],
        grad_router,
    )


def solution(mesh):
    in_specs = (
        P("ep", "tp"),
        P("ep", "tp"),
        P("tp"),
        P("tp", None),
        P("ep", None),
        P("ep", "tp", None),
        P("ep", "tp", None),
        P("ep", None, "tp"),
        P("tp", "ep"),
        P("tp", "ep"),
        P("ep", "tp"),
        P(None, "ep"),
        P(None, "ep"),
        P("ep", "tp"),
    )
    out_specs = (
        P("tp", "ep"),
        P("tp", "ep"),
        P("ep", "tp"),
        P("ep", "tp", None),
        P("ep", "tp", None),
        P("ep", None, "tp"),
        P("tp", "ep"),
        P("tp", "ep"),
        P("ep", "tp"),
        P("tp", None),
    )
    return jax.shard_map(local, mesh=mesh, in_specs=in_specs, out_specs=out_specs, check_vma=False)
```
